32 devices in a mesh: gx: 4 (over x, core), gy: 8 (over z, y).
Axes of the slice: x: 2, y: 2, z: 4, core: 2. Of those that a mesh axis runs over, the one named last changes fastest.
Arguments:
- bond_mask: int32 [3, 64, 128, 128], P(None, 'gx', 'gy'), may hold values 0 or 1
- levels: float32 [2, 3], replicated, may hold values from 0.3 to 3
- electrode: int32 [2, 64, 128], P(None, 'gx', 'gy'), may hold values 0 or 1
- leakage: float32 [64, 128, 128], P('gx', 'gy'), may hold values from 0.05 to 0.5
- source: float32 [64, 128, 128], P('gx', 'gy'), may hold values from -72 to 72
- weight: float32 [64, 128, 128], P('gx', 'gy'), may hold values from -72 to 72
Outputs:
- potential: float32 [64, 128, 128], P('gx', 'gy')
- adjoint: float32 [64, 128, 128], P('gx', 'gy')
- sensitivity: float32 [3, 64, 128, 128], P(None, 'gx', 'gy')
The draws below stay inside these ranges and needn't reach their ends.
All inputs are finite; a program needn't handle non-finite values. No bound on the sum of `bond_mask` or of `electrode` on one device may be relied on, other than what follows from the above.
Results may differ from the reference program's by a relative error of at most 0.0003.
Values sent between devices are 32-bit elements; how exact they have to be, the bound alone decides.
A program may use at most 64 MiB of HBM per device.

```python
import math
import jax
import jax.numpy as jnp

NZ = 128
ITERS = 4
NX = 64
NY = 128


def rough_field(key):
    ix = (jnp.arange(NX, dtype=jnp.float32) / max(NX - 1, 1))[:, None, None]
    iy = (jnp.arange(NY, dtype=jnp.float32) / max(NY - 1, 1))[None, :, None]
    base = jnp.clip(jax.random.normal(key, (NX, NY, NZ), jnp.float32), -6.0, 6.0)
    amp = jnp.sqrt(1.0 + 2.0 * ix) * jnp.sqrt(1.0 + 2.0 * iy)
    return 4.0 * amp * base


def draw_source(key, part):
    return rough_field(jax.random.fold_in(key, 3))


def draw_weight(key, part):
    return rough_field(jax.random.fold_in(key, 7))


def touch_ends(array, rng, least, top_value):
    longest = array.shape.index(max(array.shape))
    spots = []
    for shift in (0, 1):
        where = [jax.random.randint(jax.random.fold_in(rng, axis), (), 0, length) for axis, length in enumerate(array.shape)]
        where[longest] = (where[longest] + shift) % array.shape[longest]
        spots.append(tuple(where))
    return array.at[spots[0]].set(least).at[spots[1]].set(top_value)


def block_levels(own_key, shape, shards, least, top_value):
    level = 1.0
    for dim, parts in shards:
        heights = jax.random.uniform(jax.random.fold_in(jax.random.fold_in(own_key, 6), dim), (parts,), jnp.float32, least / len(shards), top_value / len(shards))
        level = level * jnp.repeat(jnp.exp(heights), shape[dim] // parts).reshape((-1,) + (1,) * (len(shape) - 1 - dim))
    return level


def setup_inputs(seed: int = 0) -> dict:
    key_of = jax.random.split(jax.random.key(seed), 7)
    bond_mask = touch_ends((jax.random.randint(key_of[0], (3, NX, NY, NZ), 0, 20) < 7).astype(jnp.int32), jax.random.fold_in(key_of[0], 1), 0, 1)
    levels = jnp.clip(jax.random.uniform(key_of[1], (2, 3), jnp.float32, 0.3, 3.0), 0.3, 3.0)
    electrode = touch_ends((jax.random.randint(key_of[2], (2, NX, NY), 0, 2) < 1).astype(jnp.int32), jax.random.fold_in(key_of[2], 1), 0, 1)
    leakage = jnp.clip(jnp.exp(math.log(0.5) - 2.3025851 * jax.random.uniform(key_of[3], (NX, NY, NZ), jnp.float32) ** block_levels(key_of[3], (NX, NY, NZ), ((0, 4), (1, 8)), -0.2, 0.2)), 0.05, 0.5)
    source = draw_source(jax.random.fold_in(key_of[6], 71), 0)
    weight = draw_weight(jax.random.fold_in(key_of[6], 71), 0)
    return {"bond_mask": bond_mask, "levels": levels, "electrode": electrode, "leakage": leakage, "source": source, "weight": weight}


def shift_up(v):
    padded = jnp.pad(v, ((0, 1), (0, 1), (0, 1)))
    return padded[1:, :-1, :-1], padded[:-1, 1:, :-1], padded[:-1, :-1, 1:]


def shift_down(v):
    padded = jnp.pad(v, ((1, 0), (1, 0), (1, 0)))
    return padded[:-1, 1:, 1:], padded[1:, :-1, 1:], padded[1:, 1:, :-1]


def reference(bond_mask, levels, electrode, leakage, source, weight):
    shape = (NX, NY, NZ)
    ix = jnp.arange(NX)[:, None, None]
    iy = jnp.arange(NY)[None, :, None]
    iz = jnp.arange(NZ)[None, None, :]
    inside = jnp.stack([jnp.broadcast_to(ix < NX - 1, shape), jnp.broadcast_to(iy < NY - 1, shape), jnp.broadcast_to(iz < NZ - 1, shape)]).astype(jnp.float32)
    cond = jnp.where(bond_mask == 1, levels[1][:, None, None, None], levels[0][:, None, None, None]) * inside
    below_x = shift_down(cond[0])[0]
    below_y = shift_down(cond[1])[1]
    below_z = shift_down(cond[2])[2]
    elec = electrode.astype(jnp.float32)
    first = jnp.where(iz == 0, elec[0][:, :, None], 0.0)
    last = jnp.where(iz == NZ - 1, elec[1][:, :, None], 0.0)
    diag = leakage + first + last + cond[0] + cond[1] + cond[2] + below_x + below_y + below_z

    def operate(v):
        up_x, up_y, up_z = shift_up(v)
        dn_x, dn_y, dn_z = shift_down(v)
        beside = cond[0] * up_x + below_x * dn_x + cond[1] * up_y + below_y * dn_y + cond[2] * up_z + below_z * dn_z
        return diag * v - beside

    def solve(rhs):
        x = jnp.zeros(shape, jnp.float32)
        r = rhs
        z = r / diag
        p = z
        rz = jnp.sum(r * z)
        for step in range(ITERS):
            q = operate(p)
            alpha = rz / jnp.sum(p * q)
            x = x + alpha * p
            r = r - alpha * q
            if step + 1 < ITERS:
                z = r / diag
                fresh = jnp.sum(r * z)
                p = z + (fresh / rz) * p
                rz = fresh
        return x

    potential = solve(source + first)
    adjoint = solve(weight + last)
    pu = shift_up(potential)
    au = shift_up(adjoint)
    sens = jnp.stack([-(adjoint - au[d]) * (potential - pu[d]) * inside[d] for d in range(3)])
    return potential, adjoint, sens
```

```python
import functools

import jax
import jax.numpy as jnp
from jax import lax
from jax.experimental import pallas as pl
from jax.experimental.pallas import tpu as pltpu
from jax.sharding import PartitionSpec as P

ITERS = 4
MOMENTS = 2 * ITERS
MESH = pl.DeviceIdType.MESH
UNROLL = 16


def coefficients(mu):
    def norm(c):
        total = None
        for i in range(len(c)):
            for j in range(i, len(c)):
                term = c[i] * c[j] * mu[i + j]
                term = term if i == j else term + term
                total = term if total is None else total + term
        return total

    def curved(c):
        total = None
        for i in range(len(c)):
            for j in range(i, len(c)):
                term = c[i] * c[j] * (mu[i + j] - mu[i + j + 1])
                term = term if i == j else term + term
                total = term if total is None else total + term
        return total

    one = jnp.ones_like(mu[0])
    scaled, direction, answer = [one], [one], []
    norm_now = mu[0]
    for step in range(ITERS):
        alpha = norm_now / curved(direction)
        answer = [a + alpha * d for a, d in zip(answer, direction)] + [alpha * direction[-1]]
        if step + 1 < ITERS:
            image = [direction[0]]
            image += [b - a for a, b in zip(direction[:-1], direction[1:])]
            image += [-direction[-1]]
            scaled = [s - alpha * q for s, q in zip(scaled, image)] + [-alpha * image[-1]]
            fresh = norm(scaled)
            beta = fresh / norm_now
            direction = [s + beta * d for s, d in zip(scaled, direction)] + [scaled[-1]]
            norm_now = fresh
    return answer


def kernel(
    nx, ny,
    levels, mask_in, elec_in, leak_in, src_in, wgt_in,
    pot_out, adj_out, sens_out,
    mask, elec, leak, rhs, in_sem,
    cx, cy, by, cz, bz, inv,
    rim_x, rim_y, rim_y_send, rim_send, rim_recv,
    field, y_lo, y_hi, y_lo_send, y_hi_send, halo_send, halo_recv,
    part, part_x, sum_y, part_y, px_send, px_recv, py_send, py_recv,
    answer, sens, out_sem,
):
    bx, by_rows, nz = leak.shape
    ix, iy = lax.axis_index("gx"), lax.axis_index("gy")
    has_xl, has_xh = ix > 0, ix < nx - 1
    has_yl, has_yh = iy > 0, iy < ny - 1

    loads = [
        pltpu.make_async_copy(mask_in, mask, in_sem.at[0]),
        pltpu.make_async_copy(elec_in, elec, in_sem.at[1]),
        pltpu.make_async_copy(leak_in, leak, in_sem.at[2]),
        pltpu.make_async_copy(src_in, rhs.at[0], in_sem.at[3]),
        pltpu.make_async_copy(wgt_in, rhs.at[1], in_sem.at[4]),
    ]
    for load in loads:
        load.start()

    barrier = pltpu.get_barrier_semaphore()
    for k in range(1, nx):
        pl.semaphore_signal(barrier, inc=1, device_id={"gx": lax.rem(ix + k, nx)}, device_id_type=MESH)
    for k in range(1, ny):
        pl.semaphore_signal(barrier, inc=1, device_id={"gy": lax.rem(iy + k, ny)}, device_id_type=MESH)
    pl.semaphore_wait(barrier, nx + ny - 2)

    loads[0].wait()
    row = lax.broadcasted_iota(jnp.int32, (by_rows, nz), 0)
    lane = lax.broadcasted_iota(jnp.int32, (by_rows, nz), 1)
    rim_y_send[...] = mask[1, :, by_rows - 1 : by_rows, :]
    rim_copy_x = pltpu.make_async_remote_copy(
        mask.at[0, bx - 1], rim_x, rim_send.at[0], rim_recv.at[0],
        device_id={"gx": lax.rem(ix + 1, nx)}, device_id_type=MESH,
    )
    rim_copy_y = pltpu.make_async_remote_copy(
        rim_y_send, rim_y, rim_send.at[1], rim_recv.at[1],
        device_id={"gy": lax.rem(iy + 1, ny)}, device_id_type=MESH,
    )
    pl.when(has_xh)(rim_copy_x.start)
    pl.when(has_yh)(rim_copy_y.start)

    @pl.when(jnp.logical_not(has_xl))
    def _():
        rim_x[...] = jnp.zeros_like(rim_x)
        field[:, :, 0] = jnp.zeros_like(field[:, :, 0])

    @pl.when(jnp.logical_not(has_xh))
    def _():
        field[:, :, bx + 1] = jnp.zeros_like(field[:, :, bx + 1])

    @pl.when(jnp.logical_not(has_yl))
    def _():
        rim_y[...] = jnp.zeros_like(rim_y)
        y_lo[...] = jnp.zeros_like(y_lo)

    @pl.when(jnp.logical_not(has_yh))
    def _():
        y_hi[...] = jnp.zeros_like(y_hi)

    def conductance(bits, d):
        return jnp.where(bits == 1, levels[1, d], levels[0, d])

    x_low = has_xl.astype(jnp.float32)
    x_high = has_xh.astype(jnp.float32)
    y_low = has_yl.astype(jnp.float32)
    y_high = has_yh.astype(jnp.float32)
    not_last_row = jnp.where(row < by_rows - 1, 1.0, y_high)
    for load in loads[1:]:
        load.wait()
    square = (by_rows, by_rows)
    eye = lax.broadcasted_iota(jnp.int32, square, 0) == lax.broadcasted_iota(jnp.int32, square, 1)

    def column(which, x):
        line = elec[which, pl.ds(x, 1), :].astype(jnp.float32)
        return jnp.sum(jnp.where(eye, line, 0.0), axis=1, keepdims=True)

    def set_up(x, carry):
        here = conductance(mask[0, x], 0)
        cx[x + 1] = here * jnp.where(x < bx - 1, 1.0, x_high)
        here_y = conductance(mask[1, x], 1) * not_last_row
        cy[x] = here_y
        here_z = jnp.where(lane < nz - 1, conductance(mask[2, x], 2), 0.0)
        cz[x] = here_z
        back_z = pltpu.roll(here_z, 1, 1)
        bz[x] = back_z
        first = jnp.where(lane == 0, column(0, x), 0.0)
        last = jnp.where(lane == nz - 1, column(1, x), 0.0)
        rhs[0, x] = rhs[0, x] + first
        rhs[1, x] = rhs[1, x] + last
        leak[x] = leak[x] + first + last + cx[x + 1] + here_y + here_z + back_z
        return carry

    lax.fori_loop(0, bx, set_up, 0, unroll=UNROLL)
    pl.when(has_xl)(rim_copy_x.wait_recv)
    pl.when(has_yl)(rim_copy_y.wait_recv)
    cx[0] = conductance(rim_x[...], 0) * x_low

    def halos(k):
        return [
            (has_xl, has_xh, pltpu.make_async_remote_copy(
                field.at[k, :, 1], field.at[k, :, bx + 1], halo_send.at[k, 0], halo_recv.at[k, 0],
                device_id={"gx": lax.rem(ix + nx - 1, nx)}, device_id_type=MESH)),
            (has_xh, has_xl, pltpu.make_async_remote_copy(
                field.at[k, :, bx], field.at[k, :, 0], halo_send.at[k, 1], halo_recv.at[k, 1],
                device_id={"gx": lax.rem(ix + 1, nx)}, device_id_type=MESH)),
            (has_yl, has_yh, pltpu.make_async_remote_copy(
                y_lo_send.at[k], y_hi.at[k], halo_send.at[k, 2], halo_recv.at[k, 2],
                device_id={"gy": lax.rem(iy + ny - 1, ny)}, device_id_type=MESH)),
            (has_yh, has_yl, pltpu.make_async_remote_copy(
                y_hi_send.at[k], y_lo.at[k], halo_send.at[k, 3], halo_recv.at[k, 3],
                device_id={"gy": lax.rem(iy + 1, ny)}, device_id_type=MESH)),
        ]

    def put(k, f, x, value):
        field[k, f, x + 1] = value
        y_lo_send[k, f, x] = value[0:1]
        y_hi_send[k, f, x] = value[by_rows - 1 : by_rows]

    def fold(value):
        total = value[0:8]
        for at in range(8, by_rows, 8):
            total = total + value[at : at + 8]
        return total

    nought = jnp.zeros((8, nz), jnp.float32)

    def begin(x, sums):
        back_y = jnp.where(row == 0, conductance(rim_y[x], 1) * y_low, pltpu.roll(cy[x], 1, 0))
        by[x] = back_y
        scale = 1.0 / (leak[x] + cx[x] + back_y)
        inv[x] = scale
        out = []
        for f in range(2):
            value = rhs[f, x] * scale
            put(0, f, x, value)
            out.append(sums[f] + fold(rhs[f, x] * value))
        return tuple(out)

    moments = [lax.fori_loop(0, bx, begin, (nought, nought), unroll=UNROLL)]

    def beside(k, f, x):
        here = field[k, f, x + 1]
        up_y = jnp.where(row == by_rows - 1, y_hi[k, f, x], pltpu.roll(here, by_rows - 1, 0))
        dn_y = jnp.where(row == 0, y_lo[k, f, x], pltpu.roll(here, 1, 0))
        total = cx[x + 1] * field[k, f, x + 2] + cx[x] * field[k, f, x]
        total = total + (cy[x] * up_y + by[x] * dn_y)
        total = total + (cz[x] * pltpu.roll(here, nz - 1, 1) + bz[x] * pltpu.roll(here, 1, 1))
        return here, total

    for k in range(ITERS):
        copies = halos(k)
        for sends, _, copy in copies:
            pl.when(sends)(copy.start)
        for _, receives, copy in copies:
            pl.when(receives)(copy.wait_recv)

        def advance(x, sums, k=k):
            out = []
            for f in range(2):
                here, total = beside(k, f, x)
                out.append(sums[len(out)] + fold(here * total))
                if k + 1 < ITERS:
                    value = total * inv[x]
                    put(k + 1, f, x, value)
                    out.append(sums[len(out)] + fold(value * total))
            return tuple(out)

        count = 4 if k + 1 < ITERS else 2
        sums = lax.fori_loop(0, bx, advance, (nought,) * count, unroll=UNROLL)
        if k + 1 < ITERS:
            moments += [(sums[0], sums[2]), (sums[1], sums[3])]
        else:
            moments += [(sums[0], sums[1])]

    rows = 2 * MOMENTS
    pick = lax.broadcasted_iota(jnp.int32, (rows, nz), 0) == lax.broadcasted_iota(jnp.int32, (rows, nz), 1)
    lines = [jnp.sum(value, axis=0, keepdims=True) for pair in moments for value in pair]
    each = jnp.sum(jnp.concatenate(lines, axis=0), axis=1, keepdims=True)
    message = jnp.sum(jnp.where(pick, each, 0.0), axis=0, keepdims=True)

    part[...] = message
    part_x[ix] = message
    copies = []
    for k in range(1, nx):
        copies.append(pltpu.make_async_remote_copy(
            part, part_x.at[ix], px_send.at[k], px_recv.at[k],
            device_id={"gx": lax.rem(ix + k, nx)}, device_id_type=MESH))
    for copy in copies:
        copy.start()
    for copy in copies:
        copy.wait_recv()
    message = jnp.sum(part_x[...], axis=0)
    sum_y[...] = message
    part_y[iy] = message
    for k in range(1, ny):
        copy = pltpu.make_async_remote_copy(
            sum_y, part_y.at[iy], py_send.at[k], py_recv.at[k],
            device_id={"gy": lax.rem(iy + k, ny)}, device_id_type=MESH)
        copies.append(copy)
        copy.start()
    for copy in copies[nx - 1 :]:
        copy.wait_recv()
    message = jnp.sum(part_y[...], axis=0)

    square = jnp.sum(jnp.where(pick, message, 0.0), axis=1, keepdims=True)
    square = jnp.broadcast_to(square, (rows, nz))
    weights = coefficients([square[2 * k : 2 * k + 2] for k in range(MOMENTS)])
    weights = [[jnp.broadcast_to(w[f : f + 1], (by_rows, nz)) for w in weights] for f in range(2)]

    def combine(x, carry):
        for f in range(2):
            total = weights[f][0] * field[0, f, x + 1]
            for k in range(1, ITERS):
                total = total + weights[f][k] * field[k, f, x + 1]
            answer[f, x] = total
        return carry

    lax.fori_loop(0, bx + 1, combine, 0, unroll=UNROLL + 1)
    stores = [
        pltpu.make_async_copy(answer.at[0, pl.ds(0, bx)], pot_out, out_sem.at[0]),
        pltpu.make_async_copy(answer.at[1, pl.ds(0, bx)], adj_out, out_sem.at[1]),
    ]
    for store in stores:
        store.start()

    def differences(x, carry):
        gaps = []
        for f in range(2):
            here = answer[f, x]
            rim = weights[f][0][0:1] * y_hi[0, f, x]
            for k in range(1, ITERS):
                rim = rim + weights[f][k][0:1] * y_hi[k, f, x]
            up_y = jnp.where(row == by_rows - 1, rim, pltpu.roll(here, by_rows - 1, 0))
            gaps.append((here - answer[f, x + 1], here - up_y, here - pltpu.roll(here, nz - 1, 1)))
        sens[0, x] = -gaps[1][0] * gaps[0][0] * jnp.where(x < bx - 1, 1.0, x_high)
        sens[1, x] = -gaps[1][1] * gaps[0][1] * not_last_row
        sens[2, x] = jnp.where(lane < nz - 1, -gaps[1][2] * gaps[0][2], 0.0)
        return carry

    lax.fori_loop(0, bx, differences, 0, unroll=UNROLL)
    stores.append(pltpu.make_async_copy(sens, sens_out, out_sem.at[2]))
    stores[-1].start()

    pl.when(has_xh)(rim_copy_x.wait_send)
    pl.when(has_yh)(rim_copy_y.wait_send)
    for k in range(ITERS):
        for sends, _, copy in halos(k):
            pl.when(sends)(copy.wait_send)
    for copy in copies:
        copy.wait_send()
    for store in stores:
        store.wait()


def body(nx, ny, bond_mask, levels, electrode, leakage, source, weight):
    bx, by, nz = leakage.shape
    f32, i32 = jnp.float32, jnp.int32
    vmem, dma = pltpu.VMEM, pltpu.SemaphoreType.DMA
    block = (bx, by, nz)
    anywhere = pl.BlockSpec(memory_space=pl.ANY)
    return pl.pallas_call(
        functools.partial(kernel, nx, ny),
        out_shape=(
            jax.ShapeDtypeStruct(block, f32),
            jax.ShapeDtypeStruct(block, f32),
            jax.ShapeDtypeStruct((3,) + block, f32),
        ),
        in_specs=[pl.BlockSpec(memory_space=pltpu.SMEM)] + [anywhere] * 5,
        out_specs=[anywhere] * 3,
        scratch_shapes=[
            vmem((3,) + block, i32), vmem((2, bx, by), i32), vmem(block, f32), vmem((2,) + block, f32), dma((5,)),
            vmem((bx + 1, by, nz), f32), vmem(block, f32), vmem(block, f32), vmem(block, f32), vmem(block, f32),
            vmem(block, f32),
            vmem((by, nz), i32), vmem((bx, 1, nz), i32), vmem((bx, 1, nz), i32), dma((2,)), dma((2,)),
            vmem((ITERS, 2, bx + 2, by, nz), f32),
            vmem((ITERS, 2, bx, 1, nz), f32), vmem((ITERS, 2, bx, 1, nz), f32),
            vmem((ITERS, 2, bx, 1, nz), f32), vmem((ITERS, 2, bx, 1, nz), f32),
            dma((ITERS, 4)), dma((ITERS, 4)),
            vmem((1, nz), f32), vmem((nx, 1, nz), f32), vmem((1, nz), f32), vmem((ny, 1, nz), f32),
            dma((nx,)), dma((nx,)), dma((ny,)), dma((ny,)),
            vmem((2, bx + 1, by, nz), f32), vmem((3,) + block, f32), dma((3,)),
        ],
        compiler_params=pltpu.CompilerParams(
            collective_id=0, has_side_effects=True, vmem_limit_bytes=32 * 1024 * 1024
        ),
    )(levels, bond_mask, electrode, leakage, source, weight)


def solution(mesh):
    return jax.shard_map(
        functools.partial(body, mesh.shape["gx"], mesh.shape["gy"]),
        mesh=mesh,
        in_specs=(
            P(None, "gx", "gy", None),
            P(),
            P(None, "gx", "gy"),
            P("gx", "gy", None),
            P("gx", "gy", None),
            P("gx", "gy", None),
        ),
        out_specs=(P("gx", "gy", None), P("gx", "gy", None), P(None, "gx", "gy", None)),
        check_vma=False,
    )
```

```python
import functools

import jax
import jax.numpy as jnp
from jax import lax
from jax.experimental import pallas as pl
from jax.experimental.pallas import tpu as pltpu
from jax.sharding import PartitionSpec as P

ITERS = 4
MOMENTS = 2 * ITERS
MESH = pl.DeviceIdType.MESH
UNROLL = 16
VMEM_LIMIT = 62 * 1024 * 1024


def coefficients(mu):
    def norm(c):
        total = None
        for i in range(len(c)):
            for j in range(i, len(c)):
                term = c[i] * c[j] * mu[i + j]
                term = term if i == j else term + term
                total = term if total is None else total + term
        return total

    def curved(c):
        total = None
        for i in range(len(c)):
            for j in range(i, len(c)):
                term = c[i] * c[j] * (mu[i + j] - mu[i + j + 1])
                term = term if i == j else term + term
                total = term if total is None else total + term
        return total

    one = jnp.ones_like(mu[0])
    scaled, direction, answer = [one], [one], []
    norm_now = mu[0]
    for step in range(ITERS):
        alpha = norm_now / curved(direction)
        answer = [a + alpha * d for a, d in zip(answer, direction)] + [alpha * direction[-1]]
        if step + 1 < ITERS:
            image = [direction[0]]
            image += [b - a for a, b in zip(direction[:-1], direction[1:])]
            image += [-direction[-1]]
            scaled = [s - alpha * q for s, q in zip(scaled, image)] + [-alpha * image[-1]]
            fresh = norm(scaled)
            beta = fresh / norm_now
            direction = [s + beta * d for s, d in zip(scaled, direction)] + [scaled[-1]]
            norm_now = fresh
    return answer


def kernel(
    nx, ny,
    levels, mask_in, elec_in, leak_in, src_in, wgt_in,
    answer_out, rims_out,
    mask, elec, leak, rhs, in_sem,
    cx, cy, by, cz, bz, inv,
    rim_x, rim_y, rim_y_send, rim_send, rim_recv,
    field, y_lo, y_hi, y_lo_send, y_hi_send, halo_send, halo_recv,
    part, part_x, sum_y, part_y, px_send, px_recv, py_send, py_recv,
    answer, rims, out_sem,
):
    bx, by_rows, nz = leak.shape
    ix, iy = lax.axis_index("gx"), lax.axis_index("gy")
    has_xl, has_xh = ix > 0, ix < nx - 1
    has_yl, has_yh = iy > 0, iy < ny - 1

    loads = [
        pltpu.make_async_copy(mask_in, mask, in_sem.at[0]),
        pltpu.make_async_copy(elec_in, elec, in_sem.at[1]),
        pltpu.make_async_copy(leak_in, leak, in_sem.at[2]),
        pltpu.make_async_copy(src_in, rhs.at[0], in_sem.at[3]),
        pltpu.make_async_copy(wgt_in, rhs.at[1], in_sem.at[4]),
    ]
    for load in loads:
        load.start()

    barrier = pltpu.get_barrier_semaphore()
    for k in range(1, nx):
        pl.semaphore_signal(barrier, inc=1, device_id={"gx": lax.rem(ix + k, nx)}, device_id_type=MESH)
    for k in range(1, ny):
        pl.semaphore_signal(barrier, inc=1, device_id={"gy": lax.rem(iy + k, ny)}, device_id_type=MESH)
    pl.semaphore_wait(barrier, nx + ny - 2)

    loads[0].wait()
    row = lax.broadcasted_iota(jnp.int32, (by_rows, nz), 0)
    lane = lax.broadcasted_iota(jnp.int32, (by_rows, nz), 1)
    rim_y_send[...] = mask[1, :, by_rows - 1 : by_rows, :]
    rim_copy_x = pltpu.make_async_remote_copy(
        mask.at[0, bx - 1], rim_x, rim_send.at[0], rim_recv.at[0],
        device_id={"gx": lax.rem(ix + 1, nx)}, device_id_type=MESH,
    )
    rim_copy_y = pltpu.make_async_remote_copy(
        rim_y_send, rim_y, rim_send.at[1], rim_recv.at[1],
        device_id={"gy": lax.rem(iy + 1, ny)}, device_id_type=MESH,
    )
    pl.when(has_xh)(rim_copy_x.start)
    pl.when(has_yh)(rim_copy_y.start)

    @pl.when(jnp.logical_not(has_xl))
    def _():
        rim_x[...] = jnp.zeros_like(rim_x)
        field[:, :, 0] = jnp.zeros_like(field[:, :, 0])

    @pl.when(jnp.logical_not(has_xh))
    def _():
        field[:, :, bx + 1] = jnp.zeros_like(field[:, :, bx + 1])

    @pl.when(jnp.logical_not(has_yl))
    def _():
        rim_y[...] = jnp.zeros_like(rim_y)
        y_lo[...] = jnp.zeros_like(y_lo)

    @pl.when(jnp.logical_not(has_yh))
    def _():
        y_hi[...] = jnp.zeros_like(y_hi)

    def conductance(bits, d):
        return jnp.where(bits == 1, levels[1, d], levels[0, d])

    x_low = has_xl.astype(jnp.float32)
    x_high = has_xh.astype(jnp.float32)
    y_low = has_yl.astype(jnp.float32)
    y_high = has_yh.astype(jnp.float32)
    not_last_row = jnp.where(row < by_rows - 1, 1.0, y_high)
    for load in loads[1:]:
        load.wait()
    square = (by_rows, by_rows)
    eye = lax.broadcasted_iota(jnp.int32, square, 0) == lax.broadcasted_iota(jnp.int32, square, 1)

    def column(which, x):
        line = elec[which, pl.ds(x, 1), :].astype(jnp.float32)
        return jnp.sum(jnp.where(eye, line, 0.0), axis=1, keepdims=True)

    def set_up(x, carry):
        here = conductance(mask[0, x], 0)
        cx[x + 1] = here * jnp.where(x < bx - 1, 1.0, x_high)
        here_y = conductance(mask[1, x], 1) * not_last_row
        cy[x] = here_y
        here_z = jnp.where(lane < nz - 1, conductance(mask[2, x], 2), 0.0)
        cz[x] = here_z
        back_z = pltpu.roll(here_z, 1, 1)
        bz[x] = back_z
        first = jnp.where(lane == 0, column(0, x), 0.0)
        last = jnp.where(lane == nz - 1, column(1, x), 0.0)
        rhs[0, x] = rhs[0, x] + first
        rhs[1, x] = rhs[1, x] + last
        leak[x] = leak[x] + first + last + cx[x + 1] + here_y + here_z + back_z
        return carry

    lax.fori_loop(0, bx, set_up, 0, unroll=UNROLL)
    pl.when(has_xl)(rim_copy_x.wait_recv)
    pl.when(has_yl)(rim_copy_y.wait_recv)
    cx[0] = conductance(rim_x[...], 0) * x_low

    def halos(k):
        return [
            (has_xl, has_xh, pltpu.make_async_remote_copy(
                field.at[k, :, 1], field.at[k, :, bx + 1], halo_send.at[k, 0], halo_recv.at[k, 0],
                device_id={"gx": lax.rem(ix + nx - 1, nx)}, device_id_type=MESH)),
            (has_xh, has_xl, pltpu.make_async_remote_copy(
                field.at[k, :, bx], field.at[k, :, 0], halo_send.at[k, 1], halo_recv.at[k, 1],
                device_id={"gx": lax.rem(ix + 1, nx)}, device_id_type=MESH)),
            (has_yl, has_yh, pltpu.make_async_remote_copy(
                y_lo_send.at[k], y_hi.at[k], halo_send.at[k, 2], halo_recv.at[k, 2],
                device_id={"gy": lax.rem(iy + ny - 1, ny)}, device_id_type=MESH)),
            (has_yh, has_yl, pltpu.make_async_remote_copy(
                y_hi_send.at[k], y_lo.at[k], halo_send.at[k, 3], halo_recv.at[k, 3],
                device_id={"gy": lax.rem(iy + 1, ny)}, device_id_type=MESH)),
        ]

    def put(k, f, x, value):
        field[k, f, x + 1] = value
        y_lo_send[k, f, pl.ds(x, 1), :] = value[0:1]
        y_hi_send[k, f, pl.ds(x, 1), :] = value[by_rows - 1 : by_rows]

    def fold(value):
        total = value[0:8]
        for at in range(8, by_rows, 8):
            total = total + value[at : at + 8]
        return total

    nought = jnp.zeros((8, nz), jnp.float32)

    def begin(x, sums):
        back_y = jnp.where(row == 0, conductance(rim_y[x], 1) * y_low, pltpu.roll(cy[x], 1, 0))
        by[x] = back_y
        scale = 1.0 / (leak[x] + cx[x] + back_y)
        inv[x] = scale
        out = []
        for f in range(2):
            value = rhs[f, x] * scale
            put(0, f, x, value)
            out.append(sums[f] + fold(rhs[f, x] * value))
        return tuple(out)

    moments = [lax.fori_loop(0, bx, begin, (nought, nought), unroll=UNROLL)]

    def beside(k, f, x):
        here = field[k, f, x + 1]
        up_y = jnp.where(row == by_rows - 1, y_hi[k, f, pl.ds(x, 1), :], pltpu.roll(here, by_rows - 1, 0))
        dn_y = jnp.where(row == 0, y_lo[k, f, pl.ds(x, 1), :], pltpu.roll(here, 1, 0))
        total = cx[x + 1] * field[k, f, x + 2] + cx[x] * field[k, f, x]
        total = total + (cy[x] * up_y + by[x] * dn_y)
        total = total + (cz[x] * pltpu.roll(here, nz - 1, 1) + bz[x] * pltpu.roll(here, 1, 1))
        return here, total

    for k in range(ITERS):
        copies = halos(k)
        for sends, _, copy in copies:
            pl.when(sends)(copy.start)
        for _, receives, copy in copies:
            pl.when(receives)(copy.wait_recv)

        def advance(x, sums, k=k):
            out = []
            for f in range(2):
                here, total = beside(k, f, x)
                out.append(sums[len(out)] + fold(here * total))
                if k + 1 < ITERS:
                    value = total * inv[x]
                    put(k + 1, f, x, value)
                    out.append(sums[len(out)] + fold(value * total))
            return tuple(out)

        count = 4 if k + 1 < ITERS else 2
        sums = lax.fori_loop(0, bx, advance, (nought,) * count, unroll=UNROLL)
        if k + 1 < ITERS:
            moments += [(sums[0], sums[2]), (sums[1], sums[3])]
        else:
            moments += [(sums[0], sums[1])]

    rows = 2 * MOMENTS
    pick = lax.broadcasted_iota(jnp.int32, (rows, nz), 0) == lax.broadcasted_iota(jnp.int32, (rows, nz), 1)
    lines = [jnp.sum(value, axis=0, keepdims=True) for pair in moments for value in pair]
    each = jnp.sum(jnp.concatenate(lines, axis=0), axis=1, keepdims=True)
    message = jnp.sum(jnp.where(pick, each, 0.0), axis=0, keepdims=True)

    part[...] = message
    part_x[ix] = message
    copies = []
    for k in range(1, nx):
        copies.append(pltpu.make_async_remote_copy(
            part, part_x.at[ix], px_send.at[k], px_recv.at[k],
            device_id={"gx": lax.rem(ix + k, nx)}, device_id_type=MESH))
    for copy in copies:
        copy.start()
    for copy in copies:
        copy.wait_recv()
    message = jnp.sum(part_x[...], axis=0)
    sum_y[...] = message
    part_y[iy] = message
    for k in range(1, ny):
        copy = pltpu.make_async_remote_copy(
            sum_y, part_y.at[iy], py_send.at[k], py_recv.at[k],
            device_id={"gy": lax.rem(iy + k, ny)}, device_id_type=MESH)
        copies.append(copy)
        copy.start()
    for copy in copies[nx - 1 :]:
        copy.wait_recv()
    message = jnp.sum(part_y[...], axis=0)

    square = jnp.sum(jnp.where(pick, message, 0.0), axis=1, keepdims=True)
    square = jnp.broadcast_to(square, (rows, nz))
    weights = coefficients([square[2 * k : 2 * k + 2] for k in range(MOMENTS)])
    weights = [[jnp.broadcast_to(w[f : f + 1], (by_rows, nz)) for w in weights] for f in range(2)]

    def combine(x, carry):
        for f in range(2):
            total = weights[f][0] * field[0, f, x + 1]
            for k in range(1, ITERS):
                total = total + weights[f][k] * field[k, f, x + 1]
            answer[f, x] = total
        return carry

    lax.fori_loop(0, bx + 1, combine, 0, unroll=UNROLL + 1)
    for f in range(2):
        rim = weights[f][0] * y_hi[0, f]
        for k in range(1, ITERS):
            rim = rim + weights[f][k] * y_hi[k, f]
        rims[f] = rim
    stores = [
        pltpu.make_async_copy(answer, answer_out, out_sem.at[0]),
        pltpu.make_async_copy(rims, rims_out, out_sem.at[1]),
    ]
    for store in stores:
        store.start()

    pl.when(has_xh)(rim_copy_x.wait_send)
    pl.when(has_yh)(rim_copy_y.wait_send)
    for k in range(ITERS):
        for sends, _, copy in halos(k):
            pl.when(sends)(copy.wait_send)
    for copy in copies:
        copy.wait_send()
    for store in stores:
        store.wait()


def finish(nx, ny, answer_in, rims_in, pot_out, adj_out, sens_out, answer, rims, sens, in_sem, out_sem):
    bx, by_rows, nz = pot_out.shape
    loads = [
        pltpu.make_async_copy(answer_in, answer, in_sem.at[0]),
        pltpu.make_async_copy(rims_in, rims, in_sem.at[1]),
    ]
    stores = [
        pltpu.make_async_copy(answer_in.at[0, pl.ds(0, bx)], pot_out, out_sem.at[0]),
        pltpu.make_async_copy(answer_in.at[1, pl.ds(0, bx)], adj_out, out_sem.at[1]),
    ]
    for copy in loads + stores:
        copy.start()
    row = lax.broadcasted_iota(jnp.int32, (by_rows, nz), 0)
    lane = lax.broadcasted_iota(jnp.int32, (by_rows, nz), 1)
    x_high = (lax.axis_index("gx") < nx - 1).astype(jnp.float32)
    y_high = (lax.axis_index("gy") < ny - 1).astype(jnp.float32)
    not_last_row = jnp.where(row < by_rows - 1, 1.0, y_high)

    for load in loads:
        load.wait()

    def differences(x, carry):
        gaps = []
        for f in range(2):
            here = answer[f, x]
            up_y = jnp.where(row == by_rows - 1, rims[f, pl.ds(x, 1), :], pltpu.roll(here, by_rows - 1, 0))
            gaps.append((here - answer[f, x + 1], here - up_y, here - pltpu.roll(here, nz - 1, 1)))
        sens[0, x] = -gaps[1][0] * gaps[0][0] * jnp.where(x < bx - 1, 1.0, x_high)
        sens[1, x] = -gaps[1][1] * gaps[0][1] * not_last_row
        sens[2, x] = jnp.where(lane < nz - 1, -gaps[1][2] * gaps[0][2], 0.0)
        return carry

    lax.fori_loop(0, bx, differences, 0, unroll=UNROLL)
    stores.append(pltpu.make_async_copy(sens, sens_out, out_sem.at[2]))
    stores[-1].start()
    for store in stores:
        store.wait()


def body(nx, ny, bond_mask, levels, electrode, leakage, source, weight):
    bx, by, nz = leakage.shape
    f32, i32 = jnp.float32, jnp.int32
    vmem, dma = pltpu.VMEM, pltpu.SemaphoreType.DMA
    block = (bx, by, nz)
    hbm = pl.BlockSpec(memory_space=pltpu.HBM)
    answer, rims = pl.pallas_call(
        functools.partial(kernel, nx, ny),
        out_shape=(
            jax.ShapeDtypeStruct((2, bx + 1, by, nz), f32),
            jax.ShapeDtypeStruct((2, bx, nz), f32),
        ),
        in_specs=[pl.BlockSpec(memory_space=pltpu.SMEM)] + [hbm] * 5,
        out_specs=[hbm] * 2,
        scratch_shapes=[
            vmem((3,) + block, i32), vmem((2, bx, by), i32), vmem(block, f32), vmem((2,) + block, f32), dma((5,)),
            vmem((bx + 1, by, nz), f32), vmem(block, f32), vmem(block, f32), vmem(block, f32), vmem(block, f32),
            vmem(block, f32),
            vmem((by, nz), i32), vmem((bx, 1, nz), i32), vmem((bx, 1, nz), i32), dma((2,)), dma((2,)),
            vmem((ITERS, 2, bx + 2, by, nz), f32),
            vmem((ITERS, 2, bx, nz), f32), vmem((ITERS, 2, bx, nz), f32),
            vmem((ITERS, 2, bx, nz), f32), vmem((ITERS, 2, bx, nz), f32),
            dma((ITERS, 4)), dma((ITERS, 4)),
            vmem((1, nz), f32), vmem((nx, 1, nz), f32), vmem((1, nz), f32), vmem((ny, 1, nz), f32),
            dma((nx,)), dma((nx,)), dma((ny,)), dma((ny,)),
            vmem((2, bx + 1, by, nz), f32), vmem((2, bx, nz), f32), dma((2,)),
        ],
        compiler_params=pltpu.CompilerParams(
            collective_id=0, has_side_effects=True, vmem_limit_bytes=VMEM_LIMIT
        ),
    )(levels, bond_mask, electrode, leakage, source, weight)
    return pl.pallas_call(
        functools.partial(finish, nx, ny),
        out_shape=(
            jax.ShapeDtypeStruct(block, f32),
            jax.ShapeDtypeStruct(block, f32),
            jax.ShapeDtypeStruct((3,) + block, f32),
        ),
        in_specs=[hbm] * 2,
        out_specs=[hbm] * 3,
        scratch_shapes=[
            vmem((2, bx + 1, by, nz), f32), vmem((2, bx, nz), f32), vmem((3,) + block, f32), dma((2,)), dma((3,)),
        ],
        compiler_params=pltpu.CompilerParams(vmem_limit_bytes=VMEM_LIMIT),
    )(answer, rims)


def solution(mesh):
    return jax.shard_map(
        functools.partial(body, mesh.shape["gx"], mesh.shape["gy"]),
        mesh=mesh,
        in_specs=(
            P(None, "gx", "gy", None),
            P(),
            P(None, "gx", "gy"),
            P("gx", "gy", None),
            P("gx", "gy", None),
            P("gx", "gy", None),
        ),
        out_specs=(P("gx", "gy", None), P("gx", "gy", None), P(None, "gx", "gy", None)),
        check_vma=False,
    )
```

```python
import functools

import jax
import jax.numpy as jnp
from jax import lax
from jax.experimental import pallas as pl
from jax.experimental.pallas import tpu as pltpu
from jax.sharding import PartitionSpec as P

ITERS = 4
MOMENTS = 2 * ITERS
MESH = pl.DeviceIdType.MESH
UNROLL = 4
VMEM_LIMIT = 62 * 1024 * 1024


def coefficients(mu):
    def norm(c):
        total = None
        for i in range(len(c)):
            for j in range(i, len(c)):
                term = c[i] * c[j] * mu[i + j]
                term = term if i == j else term + term
                total = term if total is None else total + term
        return total

    def curved(c):
        total = None
        for i in range(len(c)):
            for j in range(i, len(c)):
                term = c[i] * c[j] * (mu[i + j] - mu[i + j + 1])
                term = term if i == j else term + term
                total = term if total is None else total + term
        return total

    one = jnp.ones_like(mu[0])
    scaled, direction, answer = [one], [one], []
    norm_now = mu[0]
    for step in range(ITERS):
        alpha = norm_now / curved(direction)
        answer = [a + alpha * d for a, d in zip(answer, direction)] + [alpha * direction[-1]]
        if step + 1 < ITERS:
            image = [direction[0]]
            image += [b - a for a, b in zip(direction[:-1], direction[1:])]
            image += [-direction[-1]]
            scaled = [s - alpha * q for s, q in zip(scaled, image)] + [-alpha * image[-1]]
            fresh = norm(scaled)
            beta = fresh / norm_now
            direction = [s + beta * d for s, d in zip(scaled, direction)] + [scaled[-1]]
            norm_now = fresh
    return answer


def kernel(
    nx, ny,
    levels, mask_in, elec_in, leak_in, src_in, wgt_in,
    pot_out, adj_out, sens_out,
    mask, elec, leak, rhs, in_sem,
    cx, cy, by, cz, bz, inv,
    rim_x, rim_y, rim_y_send, rim_send, rim_recv,
    field, y_lo, y_hi, y_lo_send, y_hi_send, halo_send, halo_recv,
    part, part_x, sum_y, part_y, px_send, px_recv, py_send, py_recv,
    answer, rims, sens, out_sem,
):
    bx, by_rows, nz = leak.shape
    ix, iy = lax.axis_index("gx"), lax.axis_index("gy")
    has_xl, has_xh = ix > 0, ix < nx - 1
    has_yl, has_yh = iy > 0, iy < ny - 1

    loads = [
        pltpu.make_async_copy(mask_in, mask, in_sem.at[0]),
        pltpu.make_async_copy(elec_in, elec, in_sem.at[1]),
        pltpu.make_async_copy(leak_in, leak, in_sem.at[2]),
        pltpu.make_async_copy(src_in, rhs.at[0], in_sem.at[3]),
        pltpu.make_async_copy(wgt_in, rhs.at[1], in_sem.at[4]),
    ]
    for load in loads:
        load.start()

    barrier = pltpu.get_barrier_semaphore()
    for k in range(1, nx):
        pl.semaphore_signal(barrier, inc=1, device_id={"gx": lax.rem(ix + k, nx)}, device_id_type=MESH)
    for k in range(1, ny):
        pl.semaphore_signal(barrier, inc=1, device_id={"gy": lax.rem(iy + k, ny)}, device_id_type=MESH)
    pl.semaphore_wait(barrier, nx + ny - 2)

    loads[0].wait()
    row = lax.broadcasted_iota(jnp.int32, (by_rows, nz), 0)
    lane = lax.broadcasted_iota(jnp.int32, (by_rows, nz), 1)
    rim_y_send[...] = mask[1, :, by_rows - 1 : by_rows, :]
    rim_copy_x = pltpu.make_async_remote_copy(
        mask.at[0, bx - 1], rim_x, rim_send.at[0], rim_recv.at[0],
        device_id={"gx": lax.rem(ix + 1, nx)}, device_id_type=MESH,
    )
    rim_copy_y = pltpu.make_async_remote_copy(
        rim_y_send, rim_y, rim_send.at[1], rim_recv.at[1],
        device_id={"gy": lax.rem(iy + 1, ny)}, device_id_type=MESH,
    )
    pl.when(has_xh)(rim_copy_x.start)
    pl.when(has_yh)(rim_copy_y.start)

    @pl.when(jnp.logical_not(has_xl))
    def _():
        rim_x[...] = jnp.zeros_like(rim_x)
        field[:, :, 0] = jnp.zeros_like(field[:, :, 0])

    @pl.when(jnp.logical_not(has_xh))
    def _():
        field[:, :, bx + 1] = jnp.zeros_like(field[:, :, bx + 1])

    @pl.when(jnp.logical_not(has_yl))
    def _():
        rim_y[...] = jnp.zeros_like(rim_y)
        y_lo[...] = jnp.zeros_like(y_lo)

    @pl.when(jnp.logical_not(has_yh))
    def _():
        y_hi[...] = jnp.zeros_like(y_hi)

    def conductance(bits, d):
        return jnp.where(bits == 1, levels[1, d], levels[0, d])

    x_low = has_xl.astype(jnp.float32)
    x_high = has_xh.astype(jnp.float32)
    y_low = has_yl.astype(jnp.float32)
    y_high = has_yh.astype(jnp.float32)
    not_last_row = jnp.where(row < by_rows - 1, 1.0, y_high)
    for load in loads[1:]:
        load.wait()
    square = (by_rows, by_rows)
    eye = lax.broadcasted_iota(jnp.int32, square, 0) == lax.broadcasted_iota(jnp.int32, square, 1)

    def column(which, x):
        line = elec[which, pl.ds(x, 1), :].astype(jnp.float32)
        return jnp.sum(jnp.where(eye, line, 0.0), axis=1, keepdims=True)

    def set_up(x, carry):
        here = conductance(mask[0, x], 0)
        cx[x + 1] = here * jnp.where(x < bx - 1, 1.0, x_high)
        here_y = conductance(mask[1, x], 1) * not_last_row
        cy[x] = here_y
        here_z = jnp.where(lane < nz - 1, conductance(mask[2, x], 2), 0.0)
        cz[x] = here_z
        back_z = pltpu.roll(here_z, 1, 1)
        bz[x] = back_z
        first = jnp.where(lane == 0, column(0, x), 0.0)
        last = jnp.where(lane == nz - 1, column(1, x), 0.0)
        rhs[0, x] = rhs[0, x] + first
        rhs[1, x] = rhs[1, x] + last
        leak[x] = leak[x] + first + last + cx[x + 1] + here_y + here_z + back_z
        return carry

    lax.fori_loop(0, bx, set_up, 0, unroll=UNROLL)
    pl.when(has_xl)(rim_copy_x.wait_recv)
    pl.when(has_yl)(rim_copy_y.wait_recv)
    cx[0] = conductance(rim_x[...], 0) * x_low

    def halos(k):
        return [
            (has_xl, has_xh, pltpu.make_async_remote_copy(
                field.at[k, :, 1], field.at[k, :, bx + 1], halo_send.at[k, 0], halo_recv.at[k, 0],
                device_id={"gx": lax.rem(ix + nx - 1, nx)}, device_id_type=MESH)),
            (has_xh, has_xl, pltpu.make_async_remote_copy(
                field.at[k, :, bx], field.at[k, :, 0], halo_send.at[k, 1], halo_recv.at[k, 1],
                device_id={"gx": lax.rem(ix + 1, nx)}, device_id_type=MESH)),
            (has_yl, has_yh, pltpu.make_async_remote_copy(
                y_lo_send.at[k], y_hi.at[k], halo_send.at[k, 2], halo_recv.at[k, 2],
                device_id={"gy": lax.rem(iy + ny - 1, ny)}, device_id_type=MESH)),
            (has_yh, has_yl, pltpu.make_async_remote_copy(
                y_hi_send.at[k], y_lo.at[k], halo_send.at[k, 3], halo_recv.at[k, 3],
                device_id={"gy": lax.rem(iy + 1, ny)}, device_id_type=MESH)),
        ]

    def put(k, f, x, value):
        field[k, f, x + 1] = value
        y_lo_send[k, f, pl.ds(x, 1), :] = value[0:1]
        y_hi_send[k, f, pl.ds(x, 1), :] = value[by_rows - 1 : by_rows]

    def fold(value):
        total = value[0:8]
        for at in range(8, by_rows, 8):
            total = total + value[at : at + 8]
        return total

    nought = jnp.zeros((8, nz), jnp.float32)

    def begin(x, sums):
        back_y = jnp.where(row == 0, conductance(rim_y[x], 1) * y_low, pltpu.roll(cy[x], 1, 0))
        by[x] = back_y
        scale = 1.0 / (leak[x] + cx[x] + back_y)
        inv[x] = scale
        out = []
        for f in range(2):
            value = rhs[f, x] * scale
            put(0, f, x, value)
            out.append(sums[f] + fold(rhs[f, x] * value))
        return tuple(out)

    moments = [lax.fori_loop(0, bx, begin, (nought, nought), unroll=UNROLL)]

    def beside(k, f, x):
        here = field[k, f, x + 1]
        up_y = jnp.where(row == by_rows - 1, y_hi[k, f, pl.ds(x, 1), :], pltpu.roll(here, by_rows - 1, 0))
        dn_y = jnp.where(row == 0, y_lo[k, f, pl.ds(x, 1), :], pltpu.roll(here, 1, 0))
        total = cx[x + 1] * field[k, f, x + 2] + cx[x] * field[k, f, x]
        total = total + (cy[x] * up_y + by[x] * dn_y)
        total = total + (cz[x] * pltpu.roll(here, nz - 1, 1) + bz[x] * pltpu.roll(here, 1, 1))
        return here, total

    for k in range(ITERS):
        copies = halos(k)
        for sends, _, copy in copies:
            pl.when(sends)(copy.start)
        for _, receives, copy in copies:
            pl.when(receives)(copy.wait_recv)

        def advance(x, sums, k=k):
            out = []
            for f in range(2):
                here, total = beside(k, f, x)
                out.append(sums[len(out)] + fold(here * total))
                if k + 1 < ITERS:
                    value = total * inv[x]
                    put(k + 1, f, x, value)
                    out.append(sums[len(out)] + fold(value * total))
            return tuple(out)

        count = 4 if k + 1 < ITERS else 2
        sums = lax.fori_loop(0, bx, advance, (nought,) * count, unroll=UNROLL)
        if k + 1 < ITERS:
            moments += [(sums[0], sums[2]), (sums[1], sums[3])]
        else:
            moments += [(sums[0], sums[1])]

    rows = 2 * MOMENTS
    pick = lax.broadcasted_iota(jnp.int32, (rows, nz), 0) == lax.broadcasted_iota(jnp.int32, (rows, nz), 1)
    lines = [jnp.sum(value, axis=0, keepdims=True) for pair in moments for value in pair]
    each = jnp.sum(jnp.concatenate(lines, axis=0), axis=1, keepdims=True)
    message = jnp.sum(jnp.where(pick, each, 0.0), axis=0, keepdims=True)

    part[...] = message
    part_x[ix] = message
    copies = []
    for k in range(1, nx):
        copies.append(pltpu.make_async_remote_copy(
            part, part_x.at[ix], px_send.at[k], px_recv.at[k],
            device_id={"gx": lax.rem(ix + k, nx)}, device_id_type=MESH))
    for copy in copies:
        copy.start()
    for copy in copies:
        copy.wait_recv()
    message = jnp.sum(part_x[...], axis=0)
    sum_y[...] = message
    part_y[iy] = message
    for k in range(1, ny):
        copy = pltpu.make_async_remote_copy(
            sum_y, part_y.at[iy], py_send.at[k], py_recv.at[k],
            device_id={"gy": lax.rem(iy + k, ny)}, device_id_type=MESH)
        copies.append(copy)
        copy.start()
    for copy in copies[nx - 1 :]:
        copy.wait_recv()
    message = jnp.sum(part_y[...], axis=0)

    square = jnp.sum(jnp.where(pick, message, 0.0), axis=1, keepdims=True)
    square = jnp.broadcast_to(square, (rows, nz))
    weights = coefficients([square[2 * k : 2 * k + 2] for k in range(MOMENTS)])
    weights = [[jnp.broadcast_to(w[f : f + 1], (by_rows, nz)) for w in weights] for f in range(2)]

    def combine(x, carry):
        for f in range(2):
            total = weights[f][0] * field[0, f, x + 1]
            for k in range(1, ITERS):
                total = total + weights[f][k] * field[k, f, x + 1]
            answer[f, x] = total
        return carry

    lax.fori_loop(0, bx + 1, combine, 0, unroll=UNROLL)
    for f in range(2):
        rim = weights[f][0] * y_hi[0, f]
        for k in range(1, ITERS):
            rim = rim + weights[f][k] * y_hi[k, f]
        rims[f] = rim
    stores = [
        pltpu.make_async_copy(answer.at[0, pl.ds(0, bx)], pot_out, out_sem.at[0]),
        pltpu.make_async_copy(answer.at[1, pl.ds(0, bx)], adj_out, out_sem.at[1]),
        pltpu.make_async_copy(sens, sens_out, out_sem.at[2]),
    ]
    stores[0].start()
    stores[1].start()

    def differences(x, carry):
        gaps = []
        for f in range(2):
            here = answer[f, x]
            up_y = jnp.where(row == by_rows - 1, rims[f, pl.ds(x, 1), :], pltpu.roll(here, by_rows - 1, 0))
            gaps.append((here - answer[f, x + 1], here - up_y, here - pltpu.roll(here, nz - 1, 1)))
        sens[0, x] = -gaps[1][0] * gaps[0][0] * jnp.where(x < bx - 1, 1.0, x_high)
        sens[1, x] = -gaps[1][1] * gaps[0][1] * not_last_row
        sens[2, x] = jnp.where(lane < nz - 1, -gaps[1][2] * gaps[0][2], 0.0)
        return carry

    lax.fori_loop(0, bx, differences, 0, unroll=UNROLL)
    stores[2].start()

    pl.when(has_xh)(rim_copy_x.wait_send)
    pl.when(has_yh)(rim_copy_y.wait_send)
    for k in range(ITERS):
        for sends, _, copy in halos(k):
            pl.when(sends)(copy.wait_send)
    for copy in copies:
        copy.wait_send()
    for store in stores:
        store.wait()


def body(nx, ny, bond_mask, levels, electrode, leakage, source, weight):
    bx, by, nz = leakage.shape
    f32, i32 = jnp.float32, jnp.int32
    vmem, dma = pltpu.VMEM, pltpu.SemaphoreType.DMA
    block = (bx, by, nz)
    hbm = pl.BlockSpec(memory_space=pltpu.HBM)
    return pl.pallas_call(
        functools.partial(kernel, nx, ny),
        out_shape=(
            jax.ShapeDtypeStruct(block, f32),
            jax.ShapeDtypeStruct(block, f32),
            jax.ShapeDtypeStruct((3,) + block, f32),
        ),
        in_specs=[pl.BlockSpec(memory_space=pltpu.SMEM)] + [hbm] * 5,
        out_specs=[hbm] * 3,
        scratch_shapes=[
            vmem((3,) + block, i32), vmem((2, bx, by), i32), vmem(block, f32), vmem((2,) + block, f32), dma((5,)),
            vmem((bx + 1, by, nz), f32), vmem(block, f32), vmem(block, f32), vmem(block, f32), vmem(block, f32),
            vmem(block, f32),
            vmem((by, nz), i32), vmem((bx, 1, nz), i32), vmem((bx, 1, nz), i32), dma((2,)), dma((2,)),
            vmem((ITERS, 2, bx + 2, by, nz), f32),
            vmem((ITERS, 2, bx, nz), f32), vmem((ITERS, 2, bx, nz), f32),
            vmem((ITERS, 2, bx, nz), f32), vmem((ITERS, 2, bx, nz), f32),
            dma((ITERS, 4)), dma((ITERS, 4)),
            vmem((1, nz), f32), vmem((nx, 1, nz), f32), vmem((1, nz), f32), vmem((ny, 1, nz), f32),
            dma((nx,)), dma((nx,)), dma((ny,)), dma((ny,)),
            vmem((2, bx + 1, by, nz), f32), vmem((2, bx, nz), f32), vmem((3,) + block, f32), dma((3,)),
        ],
        compiler_params=pltpu.CompilerParams(
            collective_id=0, has_side_effects=True, vmem_limit_bytes=VMEM_LIMIT
        ),
    )(levels, bond_mask, electrode, leakage, source, weight)


def solution(mesh):
    return jax.shard_map(
        functools.partial(body, mesh.shape["gx"], mesh.shape["gy"]),
        mesh=mesh,
        in_specs=(
            P(None, "gx", "gy", None),
            P(),
            P(None, "gx", "gy"),
            P("gx", "gy", None),
            P("gx", "gy", None),
            P("gx", "gy", None),
        ),
        out_specs=(P("gx", "gy", None), P("gx", "gy", None), P(None, "gx", "gy", None)),
        check_vma=False,
    )
```

```python
import functools

import jax
import jax.numpy as jnp
from jax import lax
from jax.experimental import pallas as pl
from jax.experimental.pallas import tpu as pltpu
from jax.sharding import PartitionSpec as P

ITERS = 4
MOMENTS = 2 * ITERS
MESH = pl.DeviceIdType.MESH
UNROLL = 4
VMEM_LIMIT = 62 * 1024 * 1024


def coefficients(mu):
    def norm(c):
        total = None
        for i in range(len(c)):
            for j in range(i, len(c)):
                term = c[i] * c[j] * mu[i + j]
                term = term if i == j else term + term
                total = term if total is None else total + term
        return total

    def curved(c):
        total = None
        for i in range(len(c)):
            for j in range(i, len(c)):
                term = c[i] * c[j] * (mu[i + j] - mu[i + j + 1])
                term = term if i == j else term + term
                total = term if total is None else total + term
        return total

    one = jnp.ones_like(mu[0])
    scaled, direction, answer = [one], [one], []
    norm_now = mu[0]
    for step in range(ITERS):
        alpha = norm_now / curved(direction)
        answer = [a + alpha * d for a, d in zip(answer, direction)] + [alpha * direction[-1]]
        if step + 1 < ITERS:
            image = [direction[0]]
            image += [b - a for a, b in zip(direction[:-1], direction[1:])]
            image += [-direction[-1]]
            scaled = [s - alpha * q for s, q in zip(scaled, image)] + [-alpha * image[-1]]
            fresh = norm(scaled)
            beta = fresh / norm_now
            direction = [s + beta * d for s, d in zip(scaled, direction)] + [scaled[-1]]
            norm_now = fresh
    return answer


def kernel(
    nx, ny,
    levels, mask_in, elec_in, leak_in, src_in, wgt_in,
    pot_out, adj_out, sens_out,
    mask, elec, leak, rhs, in_sem,
    cx, coef, coef_y_send, coef_y, coef_send, coef_recv,
    rim_x, rim_y, rim_y_send, rim_send, rim_recv,
    field, y_send, y_halo, corner_send, corner, halo_send, halo_recv,
    part, gathered, part_send, part_recv,
    answer, rims, sens, out_sem,
):
    bx, by_rows, nz = leak.shape
    ix, iy = lax.axis_index("gx"), lax.axis_index("gy")
    devices = nx * ny
    rank = ix * ny + iy
    has_x = (ix > 0, ix < nx - 1)
    has_y = (iy > 0, iy < ny - 1)
    to_x = (lax.rem(ix + nx - 1, nx), lax.rem(ix + 1, nx))
    to_y = (lax.rem(iy + ny - 1, ny), lax.rem(iy + 1, ny))
    edge_x, edge_y = (0, bx - 1), (0, by_rows - 1)

    loads = [
        pltpu.make_async_copy(mask_in, mask, in_sem.at[0]),
        pltpu.make_async_copy(elec_in, elec, in_sem.at[1]),
        pltpu.make_async_copy(leak_in, leak, in_sem.at[2]),
        pltpu.make_async_copy(src_in, rhs.at[0], in_sem.at[3]),
        pltpu.make_async_copy(wgt_in, rhs.at[1], in_sem.at[4]),
    ]
    for load in loads:
        load.start()

    def other(k):
        at = lax.rem(rank + k, devices)
        return {"gx": lax.div(at, ny), "gy": lax.rem(at, ny)}

    def each_other(act):
        def step(k, carry):
            act(k)
            return carry

        lax.fori_loop(1, devices, step, 0)

    barrier = pltpu.get_barrier_semaphore()
    each_other(lambda k: pl.semaphore_signal(barrier, inc=1, device_id=other(k), device_id_type=MESH))
    pl.semaphore_wait(barrier, devices - 1)

    loads[0].wait()
    row = lax.broadcasted_iota(jnp.int32, (by_rows, nz), 0)
    lane = lax.broadcasted_iota(jnp.int32, (by_rows, nz), 1)
    row_x = lax.broadcasted_iota(jnp.int32, (bx, nz), 0)
    rim_y_send[...] = mask[1, :, by_rows - 1 : by_rows, :]
    rim_copy_x = pltpu.make_async_remote_copy(
        mask.at[0, bx - 1], rim_x, rim_send.at[0], rim_recv.at[0],
        device_id={"gx": to_x[1]}, device_id_type=MESH,
    )
    rim_copy_y = pltpu.make_async_remote_copy(
        rim_y_send, rim_y, rim_send.at[1], rim_recv.at[1],
        device_id={"gy": to_y[1]}, device_id_type=MESH,
    )
    pl.when(has_x[1])(rim_copy_x.start)
    pl.when(has_y[1])(rim_copy_y.start)

    @pl.when(jnp.logical_not(has_x[0]))
    def _():
        rim_x[...] = jnp.zeros_like(rim_x)

    @pl.when(jnp.logical_not(has_y[0]))
    def _():
        rim_y[...] = jnp.zeros_like(rim_y)

    for side in range(2):

        @pl.when(jnp.logical_not(has_x[side]))
        def _(side=side):
            for at in (0, 1) if side == 0 else (bx + 2, bx + 3):
                for k in range(ITERS):
                    for f in range(2):
                        field[k, f, at] = jnp.zeros((by_rows, nz), jnp.float32)
            for c in range(7):
                coef[c, 0 if side == 0 else bx + 1] = jnp.zeros((by_rows, nz), jnp.float32)

        @pl.when(jnp.logical_not(has_y[side]))
        def _(side=side):
            coef_y[side] = jnp.zeros_like(coef_y[side])
            for k in range(ITERS):
                y_halo[k, side] = jnp.zeros_like(y_halo[k, side])

    for c in range(4):

        @pl.when(jnp.logical_not(jnp.logical_and(has_x[c // 2], has_y[c % 2])))
        def _(c=c):
            for e in range(ITERS // 2):
                corner[e, c] = jnp.zeros_like(corner[e, c])

    def conductance(bits, d):
        return jnp.where(bits == 1, levels[1, d], levels[0, d])

    x_low = has_x[0].astype(jnp.float32)
    x_high = has_x[1].astype(jnp.float32)
    y_low = has_y[0].astype(jnp.float32)
    y_high = has_y[1].astype(jnp.float32)
    not_last_row = jnp.where(row < by_rows - 1, 1.0, y_high)
    for load in loads[1:]:
        load.wait()
    square = (by_rows, by_rows)
    eye = lax.broadcasted_iota(jnp.int32, square, 0) == lax.broadcasted_iota(jnp.int32, square, 1)

    def column(which, x):
        line = elec[which, pl.ds(x, 1), :].astype(jnp.float32)
        return jnp.sum(jnp.where(eye, line, 0.0), axis=1, keepdims=True)

    def set_up(x, carry):
        here = conductance(mask[0, x], 0) * jnp.where(x < bx - 1, 1.0, x_high)
        cx[x + 1] = here
        here_y = conductance(mask[1, x], 1) * not_last_row
        coef[2, x + 1] = here_y
        here_z = jnp.where(lane < nz - 1, conductance(mask[2, x], 2), 0.0)
        coef[4, x + 1] = here_z
        back_z = pltpu.roll(here_z, 1, 1)
        coef[5, x + 1] = back_z
        first = jnp.where(lane == 0, column(0, x), 0.0)
        last = jnp.where(lane == nz - 1, column(1, x), 0.0)
        rhs[0, x] = rhs[0, x] + first
        rhs[1, x] = rhs[1, x] + last
        leak[x] = leak[x] + first + last + here + here_y + here_z + back_z
        return carry

    lax.fori_loop(0, bx, set_up, 0, unroll=UNROLL)
    pl.when(has_x[0])(rim_copy_x.wait_recv)
    pl.when(has_y[0])(rim_copy_y.wait_recv)
    cx[0] = conductance(rim_x[...], 0) * x_low

    def halos(k):
        e = k // 2
        copies = []
        for side in range(2):
            mine, theirs = ((2, bx + 2), (bx, 0))[side]
            copies.append((has_x[side], has_x[1 - side], pltpu.make_async_remote_copy(
                field.at[k, :, pl.ds(mine, 2)], field.at[k, :, pl.ds(theirs, 2)],
                halo_send.at[e, side], halo_recv.at[e, side],
                device_id={"gx": to_x[side]}, device_id_type=MESH)))
            copies.append((has_y[side], has_y[1 - side], pltpu.make_async_remote_copy(
                y_send.at[e, side], y_halo.at[k, 1 - side],
                halo_send.at[e, 2 + side], halo_recv.at[e, 2 + side],
                device_id={"gy": to_y[side]}, device_id_type=MESH)))
        for c in range(4):
            a, b = c // 2, c % 2
            copies.append((
                jnp.logical_and(has_x[a], has_y[b]), jnp.logical_and(has_x[1 - a], has_y[1 - b]),
                pltpu.make_async_remote_copy(
                    corner_send.at[e, c], corner.at[e, 3 - c], halo_send.at[e, 4 + c], halo_recv.at[e, 4 + c],
                    device_id={"gx": to_x[a], "gy": to_y[b]}, device_id_type=MESH)))
        return copies

    def coef_copies():
        copies = []
        for side in range(2):
            mine, theirs = ((1, bx + 1), (bx, 0))[side]
            copies.append((has_x[side], has_x[1 - side], pltpu.make_async_remote_copy(
                coef.at[:, mine], coef.at[:, theirs], coef_send.at[side], coef_recv.at[side],
                device_id={"gx": to_x[side]}, device_id_type=MESH)))
            copies.append((has_y[side], has_y[1 - side], pltpu.make_async_remote_copy(
                coef_y_send.at[side], coef_y.at[1 - side], coef_send.at[2 + side], coef_recv.at[2 + side],
                device_id={"gy": to_y[side]}, device_id_type=MESH)))
        return copies

    def start(copies):
        for sends, _, copy in copies:
            pl.when(sends)(copy.start)

    def arrive(copies):
        for _, receives, copy in copies:
            pl.when(receives)(copy.wait_recv)

    def put(k, f, x, value):
        field[k, f, x + 2] = value
        if k % 2 == 0:
            for side in range(2):
                for deep in range(2):
                    at = deep if side == 0 else by_rows - 1 - deep
                    y_send[k // 2, side, f, deep, pl.ds(x, 1), :] = value[at : at + 1]

    def send(k):
        for c in range(4):
            at = edge_x[c // 2]
            for f in range(2):
                corner_send[k // 2, c, f] = y_send[k // 2, c % 2, f, 0, at : at + 1, :]
        start(halos(k))

    def fold(value):
        total = value[0:8]
        for at in range(8, by_rows, 8):
            total = total + value[at : at + 8]
        return total

    nought = jnp.zeros((8, nz), jnp.float32)

    def begin(x, sums):
        here_x, back_x, here_y = cx[x + 1], cx[x], coef[2, x + 1]
        back_y = jnp.where(row == 0, conductance(rim_y[x], 1) * y_low, pltpu.roll(here_y, 1, 0))
        scale = 1.0 / (leak[x] + back_x + back_y)
        coef[0, x + 1] = here_x
        coef[1, x + 1] = back_x
        coef[3, x + 1] = back_y
        coef[6, x + 1] = scale
        for c, value in enumerate((here_x, back_x, here_y, back_y, coef[4, x + 1], coef[5, x + 1], scale)):
            for side in range(2):
                at = edge_y[side]
                coef_y_send[side, c, pl.ds(x, 1), :] = value[at : at + 1]
        out = []
        for f in range(2):
            value = rhs[f, x] * scale
            put(0, f, x, value)
            out.append(sums[f] + fold(rhs[f, x] * value))
        return tuple(out)

    moments = [lax.fori_loop(0, bx, begin, (nought, nought), unroll=UNROLL)]

    def stencil(here, dn_x, up_x, dn_y, up_y, c):
        total = c[0] * up_x + c[1] * dn_x
        total = total + (c[2] * up_y + c[3] * dn_y)
        return total + (c[4] * pltpu.roll(here, nz - 1, 1) + c[5] * pltpu.roll(here, 1, 1))

    def beside(k, f, x, low, high):
        here = field[k, f, x + 2]
        up_y = jnp.where(row == by_rows - 1, high, pltpu.roll(here, by_rows - 1, 0))
        dn_y = jnp.where(row == 0, low, pltpu.roll(here, 1, 0))
        c = [coef[i, x + 1] for i in range(6)]
        return here, stencil(here, field[k, f, x + 1], field[k, f, x + 3], dn_y, up_y, c)

    def ghosts(k):
        e = k // 2
        for f in range(2):
            for side in range(2):
                x = (-1, bx)[side]
                _, total = beside(k, f, x, corner[e, 2 * side, f], corner[e, 2 * side + 1, f])
                field[k + 1, f, x + 2] = total * coef[6, x + 1]
                here, outer, own = y_halo[k, side, f, 0], y_halo[k, side, f, 1], y_send[e, side, f, 0]
                dn_x = jnp.where(row_x == 0, corner[e, side, f], pltpu.roll(here, 1, 0))
                up_x = jnp.where(row_x == bx - 1, corner[e, 2 + side, f], pltpu.roll(here, bx - 1, 0))
                dn_y, up_y = (outer, own) if side == 0 else (own, outer)
                total = stencil(here, dn_x, up_x, dn_y, up_y, [coef_y[side, i] for i in range(6)])
                y_halo[k + 1, side, f, 0] = total * coef_y[side, 6]

    for k in range(ITERS):
        if k % 2 == 0:
            send(k)
            if k == 0:
                start(coef_copies())
            arrive(halos(k))

        def advance(x, sums, k=k):
            out = []
            for f in range(2):
                low, high = [y_halo[k, side, f, 0, pl.ds(x, 1), :] for side in range(2)]
                here, total = beside(k, f, x, low, high)
                out.append(sums[len(out)] + fold(here * total))
                if k + 1 < ITERS:
                    value = total * coef[6, x + 1]
                    put(k + 1, f, x, value)
                    out.append(sums[len(out)] + fold(value * total))
            return tuple(out)

        count = 4 if k + 1 < ITERS else 2
        sums = lax.fori_loop(0, bx, advance, (nought,) * count, unroll=UNROLL)
        if k + 1 < ITERS:
            moments += [(sums[0], sums[2]), (sums[1], sums[3])]
        else:
            moments += [(sums[0], sums[1])]
        if k % 2 == 0:
            if k == 0:
                arrive(coef_copies())
            ghosts(k)

    rows = 2 * MOMENTS
    pick = lax.broadcasted_iota(jnp.int32, (rows, nz), 0) == lax.broadcasted_iota(jnp.int32, (rows, nz), 1)
    lines = [jnp.sum(value, axis=0, keepdims=True) for pair in moments for value in pair]
    each = jnp.sum(jnp.concatenate(lines, axis=0), axis=1, keepdims=True)
    message = jnp.sum(jnp.where(pick, each, 0.0), axis=0, keepdims=True)

    part[...] = message
    gathered[rank] = message
    each_other(lambda k: pltpu.make_async_remote_copy(
        part, gathered.at[rank], part_send, part_recv, device_id=other(k), device_id_type=MESH,
    ).start())
    others = gathered.at[pl.ds(0, devices - 1)]
    pltpu.make_async_copy(others, others, part_recv).wait()
    message = jnp.sum(gathered[...], axis=0)

    square = jnp.sum(jnp.where(pick, message, 0.0), axis=1, keepdims=True)
    square = jnp.broadcast_to(square, (rows, nz))
    weights = coefficients([square[2 * k : 2 * k + 2] for k in range(MOMENTS)])
    weights = [[jnp.broadcast_to(w[f : f + 1], (by_rows, nz)) for w in weights] for f in range(2)]

    def combine(x, carry):
        for f in range(2):
            total = weights[f][0] * field[0, f, x + 2]
            for k in range(1, ITERS):
                total = total + weights[f][k] * field[k, f, x + 2]
            answer[f, x] = total
        return carry

    lax.fori_loop(0, bx + 1, combine, 0, unroll=UNROLL)
    for f in range(2):
        rim = weights[f][0] * y_halo[0, 1, f, 0]
        for k in range(1, ITERS):
            rim = rim + weights[f][k] * y_halo[k, 1, f, 0]
        rims[f] = rim
    stores = [
        pltpu.make_async_copy(answer.at[0, pl.ds(0, bx)], pot_out, out_sem.at[0]),
        pltpu.make_async_copy(answer.at[1, pl.ds(0, bx)], adj_out, out_sem.at[1]),
        pltpu.make_async_copy(sens, sens_out, out_sem.at[2]),
    ]
    stores[0].start()
    stores[1].start()

    def differences(x, carry):
        gaps = []
        for f in range(2):
            here = answer[f, x]
            up_y = jnp.where(row == by_rows - 1, rims[f, pl.ds(x, 1), :], pltpu.roll(here, by_rows - 1, 0))
            gaps.append((here - answer[f, x + 1], here - up_y, here - pltpu.roll(here, nz - 1, 1)))
        sens[0, x] = -gaps[1][0] * gaps[0][0] * jnp.where(x < bx - 1, 1.0, x_high)
        sens[1, x] = -gaps[1][1] * gaps[0][1] * not_last_row
        sens[2, x] = jnp.where(lane < nz - 1, -gaps[1][2] * gaps[0][2], 0.0)
        return carry

    lax.fori_loop(0, bx, differences, 0, unroll=UNROLL)
    stores[2].start()

    pl.when(has_x[1])(rim_copy_x.wait_send)
    pl.when(has_y[1])(rim_copy_y.wait_send)
    for sends, _, copy in coef_copies() + halos(0) + halos(2):
        pl.when(sends)(copy.wait_send)
    pltpu.make_async_copy(others, others, part_send).wait()
    for store in stores:
        store.wait()


def body(nx, ny, bond_mask, levels, electrode, leakage, source, weight):
    bx, by, nz = leakage.shape
    f32, i32 = jnp.float32, jnp.int32
    vmem, dma = pltpu.VMEM, pltpu.SemaphoreType.DMA
    block = (bx, by, nz)
    hbm = pl.BlockSpec(memory_space=pltpu.HBM)
    return pl.pallas_call(
        functools.partial(kernel, nx, ny),
        out_shape=(
            jax.ShapeDtypeStruct(block, f32),
            jax.ShapeDtypeStruct(block, f32),
            jax.ShapeDtypeStruct((3,) + block, f32),
        ),
        in_specs=[pl.BlockSpec(memory_space=pltpu.SMEM)] + [hbm] * 5,
        out_specs=[hbm] * 3,
        scratch_shapes=[
            vmem((3,) + block, i32), vmem((2, bx, by), i32), vmem(block, f32), vmem((2,) + block, f32), dma((5,)),
            vmem((bx + 1, by, nz), f32), vmem((7, bx + 2, by, nz), f32),
            vmem((2, 7, bx, nz), f32), vmem((2, 7, bx, nz), f32), dma((4,)), dma((4,)),
            vmem((by, nz), i32), vmem((bx, 1, nz), i32), vmem((bx, 1, nz), i32), dma((2,)), dma((2,)),
            vmem((ITERS, 2, bx + 4, by, nz), f32),
            vmem((ITERS // 2, 2, 2, 2, bx, nz), f32), vmem((ITERS, 2, 2, 2, bx, nz), f32),
            vmem((ITERS // 2, 4, 2, 1, nz), f32), vmem((ITERS // 2, 4, 2, 1, nz), f32),
            dma((ITERS // 2, 8)), dma((ITERS // 2, 8)),
            vmem((1, nz), f32), vmem((nx * ny, 1, nz), f32), dma, dma,
            vmem((2, bx + 1, by, nz), f32), vmem((2, bx, nz), f32), vmem((3,) + block, f32), dma((3,)),
        ],
        compiler_params=pltpu.CompilerParams(
            collective_id=0, has_side_effects=True, vmem_limit_bytes=VMEM_LIMIT
        ),
    )(levels, bond_mask, electrode, leakage, source, weight)


def solution(mesh):
    return jax.shard_map(
        functools.partial(body, mesh.shape["gx"], mesh.shape["gy"]),
        mesh=mesh,
        in_specs=(
            P(None, "gx", "gy", None),
            P(),
            P(None, "gx", "gy"),
            P("gx", "gy", None),
            P("gx", "gy", None),
            P("gx", "gy", None),
        ),
        out_specs=(P("gx", "gy", None), P("gx", "gy", None), P(None, "gx", "gy", None)),
        check_vma=False,
    )
```

```python
import functools

import jax
import jax.numpy as jnp
from jax import lax
from jax.experimental import pallas as pl
from jax.experimental.pallas import tpu as pltpu
from jax.sharding import PartitionSpec as P

ITERS = 4
MOMENTS = 2 * ITERS
MESH = pl.DeviceIdType.MESH
UNROLL = 4
VMEM_LIMIT = 62 * 1024 * 1024


def coefficients(mu):
    def tree(terms):
        while len(terms) > 1:
            terms = [sum(terms[i : i + 2][1:], terms[i]) for i in range(0, len(terms), 2)]
        return terms[0]

    def quadratic(c, m):
        return tree([
            tree([c[i] * c[k - i] for i in range(max(0, k - len(c) + 1), min(k + 1, len(c)))]) * m[k]
            for k in range(2 * len(c) - 1)
        ])

    slope = [a - b for a, b in zip(mu[:-1], mu[1:])]
    one = jnp.ones_like(mu[0])
    scaled, direction, answer = [one], [one], []
    norm_now = mu[0]
    for step in range(ITERS):
        alpha = norm_now / quadratic(direction, slope)
        answer = [a + alpha * d for a, d in zip(answer, direction)] + [alpha * direction[-1]]
        if step + 1 < ITERS:
            image = [direction[0]]
            image += [b - a for a, b in zip(direction[:-1], direction[1:])]
            image += [-direction[-1]]
            scaled = [s - alpha * q for s, q in zip(scaled, image)] + [-alpha * image[-1]]
            fresh = quadratic(scaled, mu)
            beta = fresh / norm_now
            direction = [s + beta * d for s, d in zip(scaled, direction)] + [scaled[-1]]
            norm_now = fresh
    return answer


def kernel(
    nx, ny,
    levels, mask_in, elec_in, leak_in, src_in, wgt_in,
    answer_out, rims_out,
    mask, elec, leak, rhs, in_sem,
    cx, coef, coef_y_send, coef_y, coef_send, coef_recv,
    rim_x, rim_y, rim_y_send, rim_send, rim_recv,
    field, y_send, y_halo, corner_send, corner, halo_send, halo_recv,
    part, gathered, part_send, part_recv,
    answer, rims, out_sem,
):
    bx, by_rows, nz = leak.shape
    ix, iy = lax.axis_index("gx"), lax.axis_index("gy")
    devices = nx * ny
    rank = ix * ny + iy
    has_x = (ix > 0, ix < nx - 1)
    has_y = (iy > 0, iy < ny - 1)
    to_x = (lax.rem(ix + nx - 1, nx), lax.rem(ix + 1, nx))
    to_y = (lax.rem(iy + ny - 1, ny), lax.rem(iy + 1, ny))
    edge_x, edge_y = (0, bx - 1), (0, by_rows - 1)

    loads = [
        pltpu.make_async_copy(mask_in, mask, in_sem.at[0]),
        pltpu.make_async_copy(elec_in, elec, in_sem.at[1]),
        pltpu.make_async_copy(leak_in, leak, in_sem.at[2]),
        pltpu.make_async_copy(src_in, rhs.at[0], in_sem.at[3]),
        pltpu.make_async_copy(wgt_in, rhs.at[1], in_sem.at[4]),
    ]
    for load in loads:
        load.start()

    def other(k):
        at = lax.rem(rank + k, devices)
        return {"gx": lax.div(at, ny), "gy": lax.rem(at, ny)}

    def each_other(act):
        def step(k, carry):
            act(k)
            return carry

        lax.fori_loop(1, devices, step, 0)

    barrier = pltpu.get_barrier_semaphore()
    each_other(lambda k: pl.semaphore_signal(barrier, inc=1, device_id=other(k), device_id_type=MESH))
    pl.semaphore_wait(barrier, devices - 1)

    loads[0].wait()
    row = lax.broadcasted_iota(jnp.int32, (by_rows, nz), 0)
    lane = lax.broadcasted_iota(jnp.int32, (by_rows, nz), 1)
    row_x = lax.broadcasted_iota(jnp.int32, (bx, nz), 0)
    rim_y_send[...] = mask[1, :, by_rows - 1 : by_rows, :]
    rim_copy_x = pltpu.make_async_remote_copy(
        mask.at[0, bx - 1], rim_x, rim_send.at[0], rim_recv.at[0],
        device_id={"gx": to_x[1]}, device_id_type=MESH,
    )
    rim_copy_y = pltpu.make_async_remote_copy(
        rim_y_send, rim_y, rim_send.at[1], rim_recv.at[1],
        device_id={"gy": to_y[1]}, device_id_type=MESH,
    )
    pl.when(has_x[1])(rim_copy_x.start)
    pl.when(has_y[1])(rim_copy_y.start)

    @pl.when(jnp.logical_not(has_x[0]))
    def _():
        rim_x[...] = jnp.zeros_like(rim_x)

    @pl.when(jnp.logical_not(has_y[0]))
    def _():
        rim_y[...] = jnp.zeros_like(rim_y)

    for side in range(2):

        @pl.when(jnp.logical_not(has_x[side]))
        def _(side=side):
            for at in (0, 1) if side == 0 else (bx + 2, bx + 3):
                for k in range(ITERS):
                    for f in range(2):
                        field[k, f, at] = jnp.zeros((by_rows, nz), jnp.float32)
            for c in range(7):
                coef[c, 0 if side == 0 else bx + 1] = jnp.zeros((by_rows, nz), jnp.float32)

        @pl.when(jnp.logical_not(has_y[side]))
        def _(side=side):
            coef_y[side] = jnp.zeros_like(coef_y[side])
            for k in range(ITERS):
                y_halo[k, side] = jnp.zeros_like(y_halo[k, side])

    for c in range(4):

        @pl.when(jnp.logical_not(jnp.logical_and(has_x[c // 2], has_y[c % 2])))
        def _(c=c):
            for e in range(ITERS // 2):
                corner[e, c] = jnp.zeros_like(corner[e, c])

    def conductance(bits, d):
        return jnp.where(bits == 1, levels[1, d], levels[0, d])

    x_low = has_x[0].astype(jnp.float32)
    x_high = has_x[1].astype(jnp.float32)
    y_low = has_y[0].astype(jnp.float32)
    y_high = has_y[1].astype(jnp.float32)
    not_last_row = jnp.where(row < by_rows - 1, 1.0, y_high)
    for load in loads[1:]:
        load.wait()
    square = (by_rows, by_rows)
    eye = lax.broadcasted_iota(jnp.int32, square, 0) == lax.broadcasted_iota(jnp.int32, square, 1)

    def column(which, x):
        line = elec[which, pl.ds(x, 1), :].astype(jnp.float32)
        return jnp.sum(jnp.where(eye, line, 0.0), axis=1, keepdims=True)

    def set_up(x, carry):
        here = conductance(mask[0, x], 0) * jnp.where(x < bx - 1, 1.0, x_high)
        cx[x + 1] = here
        here_y = conductance(mask[1, x], 1) * not_last_row
        coef[2, x + 1] = here_y
        here_z = jnp.where(lane < nz - 1, conductance(mask[2, x], 2), 0.0)
        coef[4, x + 1] = here_z
        back_z = pltpu.roll(here_z, 1, 1)
        coef[5, x + 1] = back_z
        first = jnp.where(lane == 0, column(0, x), 0.0)
        last = jnp.where(lane == nz - 1, column(1, x), 0.0)
        rhs[0, x] = rhs[0, x] + first
        rhs[1, x] = rhs[1, x] + last
        leak[x] = leak[x] + first + last + here + here_y + here_z + back_z
        return carry

    lax.fori_loop(0, bx, set_up, 0, unroll=UNROLL)
    pl.when(has_x[0])(rim_copy_x.wait_recv)
    pl.when(has_y[0])(rim_copy_y.wait_recv)
    cx[0] = conductance(rim_x[...], 0) * x_low

    def halos(k):
        e = k // 2
        copies = []
        for side in range(2):
            mine, theirs = ((2, bx + 2), (bx, 0))[side]
            copies.append((has_x[side], has_x[1 - side], pltpu.make_async_remote_copy(
                field.at[k, :, pl.ds(mine, 2)], field.at[k, :, pl.ds(theirs, 2)],
                halo_send.at[e, side], halo_recv.at[e, side],
                device_id={"gx": to_x[side]}, device_id_type=MESH)))
            copies.append((has_y[side], has_y[1 - side], pltpu.make_async_remote_copy(
                y_send.at[e, side], y_halo.at[k, 1 - side],
                halo_send.at[e, 2 + side], halo_recv.at[e, 2 + side],
                device_id={"gy": to_y[side]}, device_id_type=MESH)))
        for c in range(4):
            a, b = c // 2, c % 2
            copies.append((
                jnp.logical_and(has_x[a], has_y[b]), jnp.logical_and(has_x[1 - a], has_y[1 - b]),
                pltpu.make_async_remote_copy(
                    corner_send.at[e, c], corner.at[e, 3 - c], halo_send.at[e, 4 + c], halo_recv.at[e, 4 + c],
                    device_id={"gx": to_x[a], "gy": to_y[b]}, device_id_type=MESH)))
        return copies

    def coef_copies():
        copies = []
        for side in range(2):
            mine, theirs = ((1, bx + 1), (bx, 0))[side]
            copies.append((has_x[side], has_x[1 - side], pltpu.make_async_remote_copy(
                coef.at[:, mine], coef.at[:, theirs], coef_send.at[side], coef_recv.at[side],
                device_id={"gx": to_x[side]}, device_id_type=MESH)))
            copies.append((has_y[side], has_y[1 - side], pltpu.make_async_remote_copy(
                coef_y_send.at[side], coef_y.at[1 - side], coef_send.at[2 + side], coef_recv.at[2 + side],
                device_id={"gy": to_y[side]}, device_id_type=MESH)))
        return copies

    def start(copies):
        for sends, _, copy in copies:
            pl.when(sends)(copy.start)

    def arrive(copies):
        for _, receives, copy in copies:
            pl.when(receives)(copy.wait_recv)

    def put(k, f, x, value):
        field[k, f, x + 2] = value
        if k % 2 == 0:
            for side in range(2):
                for deep in range(2):
                    at = deep if side == 0 else by_rows - 1 - deep
                    y_send[k // 2, side, f, deep, pl.ds(x, 1), :] = value[at : at + 1]

    def send(k):
        for c in range(4):
            at = edge_x[c // 2]
            for f in range(2):
                corner_send[k // 2, c, f] = y_send[k // 2, c % 2, f, 0, at : at + 1, :]
        start(halos(k))

    def fold(value):
        total = value[0:8]
        for at in range(8, by_rows, 8):
            total = total + value[at : at + 8]
        return total

    nought = jnp.zeros((8, nz), jnp.float32)

    def begin(x, sums):
        here_x, back_x, here_y = cx[x + 1], cx[x], coef[2, x + 1]
        back_y = jnp.where(row == 0, conductance(rim_y[x], 1) * y_low, pltpu.roll(here_y, 1, 0))
        scale = 1.0 / (leak[x] + back_x + back_y)
        coef[0, x + 1] = here_x
        coef[1, x + 1] = back_x
        coef[3, x + 1] = back_y
        coef[6, x + 1] = scale
        out = []
        for f in range(2):
            value = rhs[f, x] * scale
            put(0, f, x, value)
            out.append(sums[f] + fold(rhs[f, x] * value))
        return tuple(out)

    moments = [lax.fori_loop(0, bx, begin, (nought, nought), unroll=UNROLL)]

    def stage(x, carry):
        for c in range(7):
            for side in range(2):
                at = edge_y[side]
                coef_y_send[side, c, pl.ds(x, 1), :] = coef[c, x + 1, at : at + 1, :]
        return carry

    def stencil(here, dn_x, up_x, dn_y, up_y, c):
        total = c[0] * up_x + c[1] * dn_x
        total = total + (c[2] * up_y + c[3] * dn_y)
        return total + (c[4] * pltpu.roll(here, nz - 1, 1) + c[5] * pltpu.roll(here, 1, 1))

    def beside(k, f, x, low, high):
        here = field[k, f, x + 2]
        up_y = jnp.where(row == by_rows - 1, high, pltpu.roll(here, by_rows - 1, 0))
        dn_y = jnp.where(row == 0, low, pltpu.roll(here, 1, 0))
        c = [coef[i, x + 1] for i in range(6)]
        return here, stencil(here, field[k, f, x + 1], field[k, f, x + 3], dn_y, up_y, c)

    def ghosts(k):
        e = k // 2
        for f in range(2):
            for side in range(2):
                x = (-1, bx)[side]
                _, total = beside(k, f, x, corner[e, 2 * side, f], corner[e, 2 * side + 1, f])
                field[k + 1, f, x + 2] = total * coef[6, x + 1]
                here, outer, own = y_halo[k, side, f, 0], y_halo[k, side, f, 1], y_send[e, side, f, 0]
                dn_x = jnp.where(row_x == 0, corner[e, side, f], pltpu.roll(here, 1, 0))
                up_x = jnp.where(row_x == bx - 1, corner[e, 2 + side, f], pltpu.roll(here, bx - 1, 0))
                dn_y, up_y = (outer, own) if side == 0 else (own, outer)
                total = stencil(here, dn_x, up_x, dn_y, up_y, [coef_y[side, i] for i in range(6)])
                y_halo[k + 1, side, f, 0] = total * coef_y[side, 6]

    for k in range(ITERS):
        if k % 2 == 0:
            send(k)
            if k == 0:
                lax.fori_loop(0, bx, stage, 0, unroll=UNROLL)
                start(coef_copies())
            arrive(halos(k))

        def advance(x, sums, k=k):
            out = []
            for f in range(2):
                low, high = [y_halo[k, side, f, 0, pl.ds(x, 1), :] for side in range(2)]
                here, total = beside(k, f, x, low, high)
                out.append(sums[len(out)] + fold(here * total))
                if k + 1 < ITERS:
                    value = total * coef[6, x + 1]
                    put(k + 1, f, x, value)
                    out.append(sums[len(out)] + fold(value * total))
            return tuple(out)

        count = 4 if k + 1 < ITERS else 2
        sums = lax.fori_loop(0, bx, advance, (nought,) * count, unroll=UNROLL)
        if k + 1 < ITERS:
            moments += [(sums[0], sums[2]), (sums[1], sums[3])]
        else:
            moments += [(sums[0], sums[1])]
        if k % 2 == 0:
            if k == 0:
                arrive(coef_copies())
            ghosts(k)

    rows = 2 * MOMENTS
    pick = lax.broadcasted_iota(jnp.int32, (rows, nz), 0) == lax.broadcasted_iota(jnp.int32, (rows, nz), 1)
    lines = [jnp.sum(value, axis=0, keepdims=True) for pair in moments for value in pair]
    each = jnp.sum(jnp.concatenate(lines, axis=0), axis=1, keepdims=True)
    message = jnp.sum(jnp.where(pick, each, 0.0), axis=0, keepdims=True)

    part[...] = message
    gathered[rank] = message
    each_other(lambda k: pltpu.make_async_remote_copy(
        part, gathered.at[rank], part_send, part_recv, device_id=other(k), device_id_type=MESH,
    ).start())
    others = gathered.at[pl.ds(0, devices - 1)]
    pltpu.make_async_copy(others, others, part_recv).wait()
    message = jnp.sum(gathered[...], axis=0)

    square = jnp.sum(jnp.where(pick, message, 0.0), axis=1, keepdims=True)
    square = jnp.broadcast_to(square, (rows, nz))
    weights = coefficients([square[2 * k : 2 * k + 2] for k in range(MOMENTS)])
    weights = [[jnp.broadcast_to(w[f : f + 1], (by_rows, nz)) for w in weights] for f in range(2)]

    def combine(x, carry):
        for f in range(2):
            total = weights[f][0] * field[0, f, x + 2]
            for k in range(1, ITERS):
                total = total + weights[f][k] * field[k, f, x + 2]
            answer[f, x] = total
        return carry

    lax.fori_loop(0, bx + 1, combine, 0, unroll=UNROLL)
    for f in range(2):
        rim = weights[f][0] * y_halo[0, 1, f, 0]
        for k in range(1, ITERS):
            rim = rim + weights[f][k] * y_halo[k, 1, f, 0]
        rims[f] = rim
    stores = [
        pltpu.make_async_copy(answer, answer_out, out_sem.at[0]),
        pltpu.make_async_copy(rims, rims_out, out_sem.at[1]),
    ]
    for store in stores:
        store.start()
    pl.when(has_x[1])(rim_copy_x.wait_send)
    pl.when(has_y[1])(rim_copy_y.wait_send)
    for sends, _, copy in coef_copies() + halos(0) + halos(2):
        pl.when(sends)(copy.wait_send)
    pltpu.make_async_copy(others, others, part_send).wait()
    for store in stores:
        store.wait()


def finish(nx, ny, answer_in, rims_in, pot_out, adj_out, sens_out, answer, rims, sens, in_sem, out_sem):
    bx, by_rows, nz = pot_out.shape
    loads = [
        pltpu.make_async_copy(answer_in, answer, in_sem.at[0]),
        pltpu.make_async_copy(rims_in, rims, in_sem.at[1]),
    ]
    for load in loads:
        load.start()
    stores = [
        pltpu.make_async_copy(answer.at[0, pl.ds(0, bx)], pot_out, out_sem.at[0]),
        pltpu.make_async_copy(answer.at[1, pl.ds(0, bx)], adj_out, out_sem.at[1]),
        pltpu.make_async_copy(sens, sens_out, out_sem.at[2]),
    ]
    loads[0].wait()
    stores[0].start()
    stores[1].start()
    loads[1].wait()
    row = lax.broadcasted_iota(jnp.int32, (by_rows, nz), 0)
    lane = lax.broadcasted_iota(jnp.int32, (by_rows, nz), 1)
    x_high = (lax.axis_index("gx") < nx - 1).astype(jnp.float32)
    y_high = (lax.axis_index("gy") < ny - 1).astype(jnp.float32)
    not_last_row = jnp.where(row < by_rows - 1, 1.0, y_high)

    def differences(x, carry):
        gaps = []
        for f in range(2):
            here = answer[f, x]
            up_y = jnp.where(row == by_rows - 1, rims[f, pl.ds(x, 1), :], pltpu.roll(here, by_rows - 1, 0))
            gaps.append((here - answer[f, x + 1], here - up_y, here - pltpu.roll(here, nz - 1, 1)))
        sens[0, x] = -gaps[1][0] * gaps[0][0] * jnp.where(x < bx - 1, 1.0, x_high)
        sens[1, x] = -gaps[1][1] * gaps[0][1] * not_last_row
        sens[2, x] = jnp.where(lane < nz - 1, -gaps[1][2] * gaps[0][2], 0.0)
        return carry

    lax.fori_loop(0, bx, differences, 0, unroll=UNROLL)
    stores[2].start()
    for store in stores:
        store.wait()


def body(nx, ny, bond_mask, levels, electrode, leakage, source, weight):
    bx, by, nz = leakage.shape
    f32, i32 = jnp.float32, jnp.int32
    vmem, dma = pltpu.VMEM, pltpu.SemaphoreType.DMA
    block = (bx, by, nz)
    hbm = pl.BlockSpec(memory_space=pltpu.HBM)
    answer, rims = pl.pallas_call(
        functools.partial(kernel, nx, ny),
        out_shape=(
            jax.ShapeDtypeStruct((2, bx + 1, by, nz), f32),
            jax.ShapeDtypeStruct((2, bx, nz), f32),
        ),
        in_specs=[pl.BlockSpec(memory_space=pltpu.SMEM)] + [hbm] * 5,
        out_specs=[hbm] * 2,
        scratch_shapes=[
            vmem((3,) + block, i32), vmem((2, bx, by), i32), vmem(block, f32), vmem((2,) + block, f32), dma((5,)),
            vmem((bx + 1, by, nz), f32), vmem((7, bx + 2, by, nz), f32),
            vmem((2, 7, bx, nz), f32), vmem((2, 7, bx, nz), f32), dma((4,)), dma((4,)),
            vmem((by, nz), i32), vmem((bx, 1, nz), i32), vmem((bx, 1, nz), i32), dma((2,)), dma((2,)),
            vmem((ITERS, 2, bx + 4, by, nz), f32),
            vmem((ITERS // 2, 2, 2, 2, bx, nz), f32), vmem((ITERS, 2, 2, 2, bx, nz), f32),
            vmem((ITERS // 2, 4, 2, 1, nz), f32), vmem((ITERS // 2, 4, 2, 1, nz), f32),
            dma((ITERS // 2, 8)), dma((ITERS // 2, 8)),
            vmem((1, nz), f32), vmem((nx * ny, 1, nz), f32), dma, dma,
            vmem((2, bx + 1, by, nz), f32), vmem((2, bx, nz), f32), dma((2,)),
        ],
        compiler_params=pltpu.CompilerParams(
            collective_id=0, has_side_effects=True, vmem_limit_bytes=VMEM_LIMIT
        ),
    )(levels, bond_mask, electrode, leakage, source, weight)
    return pl.pallas_call(
        functools.partial(finish, nx, ny),
        out_shape=(
            jax.ShapeDtypeStruct(block, f32),
            jax.ShapeDtypeStruct(block, f32),
            jax.ShapeDtypeStruct((3,) + block, f32),
        ),
        in_specs=[hbm] * 2,
        out_specs=[hbm] * 3,
        scratch_shapes=[
            vmem((2, bx + 1, by, nz), f32), vmem((2, bx, nz), f32), vmem((3,) + block, f32), dma((2,)), dma((3,)),
        ],
        compiler_params=pltpu.CompilerParams(vmem_limit_bytes=VMEM_LIMIT),
    )(answer, rims)


def solution(mesh):
    return jax.shard_map(
        functools.partial(body, mesh.shape["gx"], mesh.shape["gy"]),
        mesh=mesh,
        in_specs=(
            P(None, "gx", "gy", None),
            P(),
            P(None, "gx", "gy"),
            P("gx", "gy", None),
            P("gx", "gy", None),
            P("gx", "gy", None),
        ),
        out_specs=(P("gx", "gy", None), P("gx", "gy", None), P(None, "gx", "gy", None)),
        check_vma=False,
    )
```

```python
import functools

import jax
import jax.numpy as jnp
from jax import lax
from jax.experimental import pallas as pl
from jax.experimental.pallas import tpu as pltpu
from jax.sharding import PartitionSpec as P

ITERS = 4
MOMENTS = 2 * ITERS
MESH = pl.DeviceIdType.MESH
UNROLL = 4
VMEM_LIMIT = 62 * 1024 * 1024


def coefficients(mu):
    def tree(terms):
        while len(terms) > 1:
            terms = [sum(terms[i : i + 2][1:], terms[i]) for i in range(0, len(terms), 2)]
        return terms[0]

    def quadratic(c, m):
        return tree([
            tree([c[i] * c[k - i] for i in range(max(0, k - len(c) + 1), min(k + 1, len(c)))]) * m[k]
            for k in range(2 * len(c) - 1)
        ])

    slope = [a - b for a, b in zip(mu[:-1], mu[1:])]
    one = jnp.ones_like(mu[0])
    scaled, direction, answer = [one], [one], []
    norm_now = mu[0]
    for step in range(ITERS):
        alpha = norm_now / quadratic(direction, slope)
        answer = [a + alpha * d for a, d in zip(answer, direction)] + [alpha * direction[-1]]
        if step + 1 < ITERS:
            image = [direction[0]]
            image += [b - a for a, b in zip(direction[:-1], direction[1:])]
            image += [-direction[-1]]
            scaled = [s - alpha * q for s, q in zip(scaled, image)] + [-alpha * image[-1]]
            fresh = quadratic(scaled, mu)
            beta = fresh / norm_now
            direction = [s + beta * d for s, d in zip(scaled, direction)] + [scaled[-1]]
            norm_now = fresh
    return answer


def kernel(
    nx, ny,
    levels, mask_in, elec_in, leak_in, src_in, wgt_in,
    answer_out, rims_out,
    mask, elec, leak, rhs, in_sem,
    cx, coef, coef_y_send, coef_y, coef_send, coef_recv,
    rim_x, rim_y, rim_y_send, rim_send, rim_recv,
    field, y_send, y_halo, corner_send, corner, halo_send, halo_recv,
    part, gathered, part_send, part_recv,
    answer, rims, out_sem,
):
    bx, by_rows, nz = leak.shape
    ix, iy = lax.axis_index("gx"), lax.axis_index("gy")
    devices = nx * ny
    rank = ix * ny + iy
    has_x = (ix > 0, ix < nx - 1)
    has_y = (iy > 0, iy < ny - 1)
    to_x = (jnp.maximum(ix - 1, 0), jnp.minimum(ix + 1, nx - 1))
    to_y = (jnp.maximum(iy - 1, 0), jnp.minimum(iy + 1, ny - 1))
    edge_x, edge_y = (0, bx - 1), (0, by_rows - 1)

    loads = [
        pltpu.make_async_copy(mask_in, mask, in_sem.at[0]),
        pltpu.make_async_copy(elec_in, elec, in_sem.at[1]),
        pltpu.make_async_copy(leak_in, leak, in_sem.at[2]),
        pltpu.make_async_copy(src_in, rhs.at[0], in_sem.at[3]),
        pltpu.make_async_copy(wgt_in, rhs.at[1], in_sem.at[4]),
    ]
    for load in loads:
        load.start()

    def ahead(at, count, size):
        places = [at]
        for _ in range(1, count):
            later = places[-1] + 1
            places.append(jnp.where(later == size, 0, later))
        return places

    all_x, all_y = ahead(ix, nx, nx), ahead(iy, ny, ny)

    def each_other(act):
        for dx in range(nx):
            for dy in range(ny):
                if dx or dy:
                    act({"gx": all_x[dx], "gy": all_y[dy]})

    barrier = pltpu.get_barrier_semaphore()
    each_other(lambda to: pl.semaphore_signal(barrier, inc=1, device_id=to, device_id_type=MESH))
    pl.semaphore_wait(barrier, devices - 1)

    loads[0].wait()
    row = lax.broadcasted_iota(jnp.int32, (by_rows, nz), 0)
    lane = lax.broadcasted_iota(jnp.int32, (by_rows, nz), 1)
    row_x = lax.broadcasted_iota(jnp.int32, (bx, nz), 0)
    rim_y_send[...] = mask[1, :, by_rows - 1 : by_rows, :]
    rim_copy_x = pltpu.make_async_remote_copy(
        mask.at[0, bx - 1], rim_x, rim_send.at[0], rim_recv.at[0],
        device_id={"gx": to_x[1]}, device_id_type=MESH,
    )
    rim_copy_y = pltpu.make_async_remote_copy(
        rim_y_send, rim_y, rim_send.at[1], rim_recv.at[1],
        device_id={"gy": to_y[1]}, device_id_type=MESH,
    )
    pl.when(has_x[1])(rim_copy_x.start)
    pl.when(has_y[1])(rim_copy_y.start)

    @pl.when(jnp.logical_not(has_x[0]))
    def _():
        rim_x[...] = jnp.zeros_like(rim_x)

    @pl.when(jnp.logical_not(has_y[0]))
    def _():
        rim_y[...] = jnp.zeros_like(rim_y)

    for side in range(2):

        @pl.when(jnp.logical_not(has_x[side]))
        def _(side=side):
            for at in (0, 1) if side == 0 else (bx + 2, bx + 3):
                for k in range(ITERS):
                    for f in range(2):
                        field[k, f, at] = jnp.zeros((by_rows, nz), jnp.float32)
            for c in range(7):
                coef[c, 0 if side == 0 else bx + 1] = jnp.zeros((by_rows, nz), jnp.float32)

        @pl.when(jnp.logical_not(has_y[side]))
        def _(side=side):
            coef_y[side] = jnp.zeros_like(coef_y[side])
            for k in range(ITERS):
                y_halo[k, side] = jnp.zeros_like(y_halo[k, side])

    for c in range(4):

        @pl.when(jnp.logical_not(jnp.logical_and(has_x[c // 2], has_y[c % 2])))
        def _(c=c):
            for e in range(ITERS // 2):
                corner[e, c] = jnp.zeros_like(corner[e, c])

    def conductance(bits, d):
        return jnp.where(bits == 1, levels[1, d], levels[0, d])

    x_low = has_x[0].astype(jnp.float32)
    x_high = has_x[1].astype(jnp.float32)
    y_low = has_y[0].astype(jnp.float32)
    y_high = has_y[1].astype(jnp.float32)
    not_last_row = jnp.where(row < by_rows - 1, 1.0, y_high)
    for load in loads[1:]:
        load.wait()
    square = (by_rows, by_rows)
    eye = lax.broadcasted_iota(jnp.int32, square, 0) == lax.broadcasted_iota(jnp.int32, square, 1)

    def column(which, x):
        line = elec[which, pl.ds(x, 1), :].astype(jnp.float32)
        return jnp.sum(jnp.where(eye, line, 0.0), axis=1, keepdims=True)

    def set_up(x, carry):
        here = conductance(mask[0, x], 0) * jnp.where(x < bx - 1, 1.0, x_high)
        cx[x + 1] = here
        here_y = conductance(mask[1, x], 1) * not_last_row
        coef[2, x + 1] = here_y
        here_z = jnp.where(lane < nz - 1, conductance(mask[2, x], 2), 0.0)
        coef[4, x + 1] = here_z
        back_z = pltpu.roll(here_z, 1, 1)
        coef[5, x + 1] = back_z
        first = jnp.where(lane == 0, column(0, x), 0.0)
        last = jnp.where(lane == nz - 1, column(1, x), 0.0)
        rhs[0, x] = rhs[0, x] + first
        rhs[1, x] = rhs[1, x] + last
        leak[x] = leak[x] + first + last + here + here_y + here_z + back_z
        return carry

    lax.fori_loop(0, bx, set_up, 0, unroll=UNROLL)
    pl.when(has_x[0])(rim_copy_x.wait_recv)
    pl.when(has_y[0])(rim_copy_y.wait_recv)
    cx[0] = conductance(rim_x[...], 0) * x_low

    def halos(k):
        e = k // 2
        copies = []
        for side in range(2):
            mine, theirs = ((2, bx + 2), (bx, 0))[side]
            copies.append((has_x[side], has_x[1 - side], pltpu.make_async_remote_copy(
                field.at[k, :, pl.ds(mine, 2)], field.at[k, :, pl.ds(theirs, 2)],
                halo_send.at[e, side], halo_recv.at[e, side],
                device_id={"gx": to_x[side]}, device_id_type=MESH)))
            copies.append((has_y[side], has_y[1 - side], pltpu.make_async_remote_copy(
                y_send.at[e, side], y_halo.at[k, 1 - side],
                halo_send.at[e, 2 + side], halo_recv.at[e, 2 + side],
                device_id={"gy": to_y[side]}, device_id_type=MESH)))
        for c in range(4):
            a, b = c // 2, c % 2
            copies.append((
                jnp.logical_and(has_x[a], has_y[b]), jnp.logical_and(has_x[1 - a], has_y[1 - b]),
                pltpu.make_async_remote_copy(
                    corner_send.at[e, c], corner.at[e, 3 - c], halo_send.at[e, 4 + c], halo_recv.at[e, 4 + c],
                    device_id={"gx": to_x[a], "gy": to_y[b]}, device_id_type=MESH)))
        return copies

    def coef_copies():
        copies = []
        for side in range(2):
            mine, theirs = ((1, bx + 1), (bx, 0))[side]
            copies.append((has_x[side], has_x[1 - side], pltpu.make_async_remote_copy(
                coef.at[:, mine], coef.at[:, theirs], coef_send.at[side], coef_recv.at[side],
                device_id={"gx": to_x[side]}, device_id_type=MESH)))
            copies.append((has_y[side], has_y[1 - side], pltpu.make_async_remote_copy(
                coef_y_send.at[side], coef_y.at[1 - side], coef_send.at[2 + side], coef_recv.at[2 + side],
                device_id={"gy": to_y[side]}, device_id_type=MESH)))
        return copies

    def start(copies):
        for sends, _, copy in copies:
            pl.when(sends)(copy.start)

    def arrive(copies):
        for _, receives, copy in copies:
            pl.when(receives)(copy.wait_recv)

    def put(k, f, x, value):
        field[k, f, x + 2] = value
        if k % 2 == 0:
            for side in range(2):
                for deep in range(2):
                    at = deep if side == 0 else by_rows - 1 - deep
                    y_send[k // 2, side, f, deep, pl.ds(x, 1), :] = value[at : at + 1]

    def send(k):
        for c in range(4):
            at = edge_x[c // 2]
            for f in range(2):
                corner_send[k // 2, c, f] = y_send[k // 2, c % 2, f, 0, at : at + 1, :]
        start(halos(k))

    def fold(value):
        total = value[0:8]
        for at in range(8, by_rows, 8):
            total = total + value[at : at + 8]
        return total

    nought = jnp.zeros((8, nz), jnp.float32)

    def begin(x, sums):
        here_x, back_x, here_y = cx[x + 1], cx[x], coef[2, x + 1]
        back_y = jnp.where(row == 0, conductance(rim_y[x], 1) * y_low, pltpu.roll(here_y, 1, 0))
        scale = 1.0 / (leak[x] + back_x + back_y)
        coef[0, x + 1] = here_x
        coef[1, x + 1] = back_x
        coef[3, x + 1] = back_y
        coef[6, x + 1] = scale
        out = []
        for f in range(2):
            value = rhs[f, x] * scale
            put(0, f, x, value)
            out.append(sums[f] + fold(rhs[f, x] * value))
        return tuple(out)

    moments = [lax.fori_loop(0, bx, begin, (nought, nought), unroll=UNROLL)]

    def stage(x, carry):
        for c in range(7):
            for side in range(2):
                at = edge_y[side]
                coef_y_send[side, c, pl.ds(x, 1), :] = coef[c, x + 1, at : at + 1, :]
        return carry

    def stencil(here, dn_x, up_x, dn_y, up_y, c):
        total = c[0] * up_x + c[1] * dn_x
        total = total + (c[2] * up_y + c[3] * dn_y)
        return total + (c[4] * pltpu.roll(here, nz - 1, 1) + c[5] * pltpu.roll(here, 1, 1))

    def beside(k, f, x, low, high):
        here = field[k, f, x + 2]
        up_y = jnp.where(row == by_rows - 1, high, pltpu.roll(here, by_rows - 1, 0))
        dn_y = jnp.where(row == 0, low, pltpu.roll(here, 1, 0))
        c = [coef[i, x + 1] for i in range(6)]
        return here, stencil(here, field[k, f, x + 1], field[k, f, x + 3], dn_y, up_y, c)

    def ghosts(k):
        e = k // 2
        for f in range(2):
            for side in range(2):
                x = (-1, bx)[side]
                _, total = beside(k, f, x, corner[e, 2 * side, f], corner[e, 2 * side + 1, f])
                field[k + 1, f, x + 2] = total * coef[6, x + 1]
                here, outer, own = y_halo[k, side, f, 0], y_halo[k, side, f, 1], y_send[e, side, f, 0]
                dn_x = jnp.where(row_x == 0, corner[e, side, f], pltpu.roll(here, 1, 0))
                up_x = jnp.where(row_x == bx - 1, corner[e, 2 + side, f], pltpu.roll(here, bx - 1, 0))
                dn_y, up_y = (outer, own) if side == 0 else (own, outer)
                total = stencil(here, dn_x, up_x, dn_y, up_y, [coef_y[side, i] for i in range(6)])
                y_halo[k + 1, side, f, 0] = total * coef_y[side, 6]

    for k in range(ITERS):
        if k % 2 == 0:
            send(k)
            if k == 0:
                lax.fori_loop(0, bx, stage, 0, unroll=UNROLL)
                start(coef_copies())
            arrive(halos(k))

        def advance(x, sums, k=k):
            out = []
            for f in range(2):
                low, high = [y_halo[k, side, f, 0, pl.ds(x, 1), :] for side in range(2)]
                here, total = beside(k, f, x, low, high)
                out.append(sums[len(out)] + fold(here * total))
                if k + 1 < ITERS:
                    value = total * coef[6, x + 1]
                    put(k + 1, f, x, value)
                    out.append(sums[len(out)] + fold(value * total))
            return tuple(out)

        count = 4 if k + 1 < ITERS else 2
        sums = lax.fori_loop(0, bx, advance, (nought,) * count, unroll=bx)
        if k + 1 < ITERS:
            moments += [(sums[0], sums[2]), (sums[1], sums[3])]
        else:
            moments += [(sums[0], sums[1])]
        if k % 2 == 0:
            if k == 0:
                arrive(coef_copies())
            ghosts(k)

    rows = 2 * MOMENTS
    pick = lax.broadcasted_iota(jnp.int32, (rows, nz), 0) == lax.broadcasted_iota(jnp.int32, (rows, nz), 1)
    lines = [jnp.sum(value, axis=0, keepdims=True) for pair in moments for value in pair]
    each = jnp.sum(jnp.concatenate(lines, axis=0), axis=1, keepdims=True)
    message = jnp.sum(jnp.where(pick, each, 0.0), axis=0, keepdims=True)

    part[...] = message
    gathered[rank] = message
    each_other(lambda to: pltpu.make_async_remote_copy(
        part, gathered.at[rank], part_send, part_recv, device_id=to, device_id_type=MESH,
    ).start())
    others = gathered.at[pl.ds(0, devices - 1)]
    pltpu.make_async_copy(others, others, part_recv).wait()
    message = jnp.sum(gathered[...], axis=0)

    square = jnp.sum(jnp.where(pick, message, 0.0), axis=1, keepdims=True)
    square = jnp.broadcast_to(square, (rows, nz))
    weights = coefficients([square[2 * k : 2 * k + 2] for k in range(MOMENTS)])
    weights = [[jnp.broadcast_to(w[f : f + 1], (by_rows, nz)) for w in weights] for f in range(2)]

    def combine(x, carry):
        for f in range(2):
            total = weights[f][0] * field[0, f, x + 2]
            for k in range(1, ITERS):
                total = total + weights[f][k] * field[k, f, x + 2]
            answer[f, x] = total
        return carry

    lax.fori_loop(0, bx + 1, combine, 0, unroll=UNROLL)
    for f in range(2):
        rim = weights[f][0] * y_halo[0, 1, f, 0]
        for k in range(1, ITERS):
            rim = rim + weights[f][k] * y_halo[k, 1, f, 0]
        rims[f] = rim
    stores = [
        pltpu.make_async_copy(answer, answer_out, out_sem.at[0]),
        pltpu.make_async_copy(rims, rims_out, out_sem.at[1]),
    ]
    for store in stores:
        store.start()
    pl.when(has_x[1])(rim_copy_x.wait_send)
    pl.when(has_y[1])(rim_copy_y.wait_send)
    for sends, _, copy in coef_copies() + halos(0) + halos(2):
        pl.when(sends)(copy.wait_send)
    pltpu.make_async_copy(others, others, part_send).wait()
    for store in stores:
        store.wait()


def finish(nx, ny, answer_in, rims_in, pot_out, adj_out, sens_out, answer, rims, sens, in_sem, out_sem):
    bx, by_rows, nz = pot_out.shape
    loads = [
        pltpu.make_async_copy(answer_in, answer, in_sem.at[0]),
        pltpu.make_async_copy(rims_in, rims, in_sem.at[1]),
    ]
    for load in loads:
        load.start()
    stores = [
        pltpu.make_async_copy(answer.at[0, pl.ds(0, bx)], pot_out, out_sem.at[0]),
        pltpu.make_async_copy(answer.at[1, pl.ds(0, bx)], adj_out, out_sem.at[1]),
        pltpu.make_async_copy(sens, sens_out, out_sem.at[2]),
    ]
    loads[0].wait()
    stores[0].start()
    stores[1].start()
    loads[1].wait()
    row = lax.broadcasted_iota(jnp.int32, (by_rows, nz), 0)
    lane = lax.broadcasted_iota(jnp.int32, (by_rows, nz), 1)
    x_high = (lax.axis_index("gx") < nx - 1).astype(jnp.float32)
    y_high = (lax.axis_index("gy") < ny - 1).astype(jnp.float32)
    not_last_row = jnp.where(row < by_rows - 1, 1.0, y_high)

    def differences(x, carry):
        gaps = []
        for f in range(2):
            here = answer[f, x]
            up_y = jnp.where(row == by_rows - 1, rims[f, pl.ds(x, 1), :], pltpu.roll(here, by_rows - 1, 0))
            gaps.append((here - answer[f, x + 1], here - up_y, here - pltpu.roll(here, nz - 1, 1)))
        sens[0, x] = -gaps[1][0] * gaps[0][0] * jnp.where(x < bx - 1, 1.0, x_high)
        sens[1, x] = -gaps[1][1] * gaps[0][1] * not_last_row
        sens[2, x] = jnp.where(lane < nz - 1, -gaps[1][2] * gaps[0][2], 0.0)
        return carry

    lax.fori_loop(0, bx, differences, 0, unroll=UNROLL)
    stores[2].start()
    for store in stores:
        store.wait()


def body(nx, ny, bond_mask, levels, electrode, leakage, source, weight):
    bx, by, nz = leakage.shape
    f32, i32 = jnp.float32, jnp.int32
    vmem, dma = pltpu.VMEM, pltpu.SemaphoreType.DMA
    block = (bx, by, nz)
    hbm = pl.BlockSpec(memory_space=pltpu.HBM)
    answer, rims = pl.pallas_call(
        functools.partial(kernel, nx, ny),
        out_shape=(
            jax.ShapeDtypeStruct((2, bx + 1, by, nz), f32),
            jax.ShapeDtypeStruct((2, bx, nz), f32),
        ),
        in_specs=[pl.BlockSpec(memory_space=pltpu.SMEM)] + [hbm] * 5,
        out_specs=[hbm] * 2,
        scratch_shapes=[
            vmem((3,) + block, i32), vmem((2, bx, by), i32), vmem(block, f32), vmem((2,) + block, f32), dma((5,)),
            vmem((bx + 1, by, nz), f32), vmem((7, bx + 2, by, nz), f32),
            vmem((2, 7, bx, nz), f32), vmem((2, 7, bx, nz), f32), dma((4,)), dma((4,)),
            vmem((by, nz), i32), vmem((bx, 1, nz), i32), vmem((bx, 1, nz), i32), dma((2,)), dma((2,)),
            vmem((ITERS, 2, bx + 4, by, nz), f32),
            vmem((ITERS // 2, 2, 2, 2, bx, nz), f32), vmem((ITERS, 2, 2, 2, bx, nz), f32),
            vmem((ITERS // 2, 4, 2, 1, nz), f32), vmem((ITERS // 2, 4, 2, 1, nz), f32),
            dma((ITERS // 2, 8)), dma((ITERS // 2, 8)),
            vmem((1, nz), f32), vmem((nx * ny, 1, nz), f32), dma, dma,
            vmem((2, bx + 1, by, nz), f32), vmem((2, bx, nz), f32), dma((2,)),
        ],
        compiler_params=pltpu.CompilerParams(
            collective_id=0, has_side_effects=True, vmem_limit_bytes=VMEM_LIMIT
        ),
    )(levels, bond_mask, electrode, leakage, source, weight)
    return pl.pallas_call(
        functools.partial(finish, nx, ny),
        out_shape=(
            jax.ShapeDtypeStruct(block, f32),
            jax.ShapeDtypeStruct(block, f32),
            jax.ShapeDtypeStruct((3,) + block, f32),
        ),
        in_specs=[hbm] * 2,
        out_specs=[hbm] * 3,
        scratch_shapes=[
            vmem((2, bx + 1, by, nz), f32), vmem((2, bx, nz), f32), vmem((3,) + block, f32), dma((2,)), dma((3,)),
        ],
        compiler_params=pltpu.CompilerParams(vmem_limit_bytes=VMEM_LIMIT),
    )(answer, rims)


def solution(mesh):
    return jax.shard_map(
        functools.partial(body, mesh.shape["gx"], mesh.shape["gy"]),
        mesh=mesh,
        in_specs=(
            P(None, "gx", "gy", None),
            P(),
            P(None, "gx", "gy"),
            P("gx", "gy", None),
            P("gx", "gy", None),
            P("gx", "gy", None),
        ),
        out_specs=(P("gx", "gy", None), P("gx", "gy", None), P(None, "gx", "gy", None)),
        check_vma=False,
    )
```

```python
import functools

import jax
import jax.numpy as jnp
from jax import lax
from jax.experimental import pallas as pl
from jax.experimental.pallas import tpu as pltpu
from jax.sharding import PartitionSpec as P

ITERS = 4
MOMENTS = 2 * ITERS
MESH = pl.DeviceIdType.MESH
UNROLL = 4
VMEM_LIMIT = 62 * 1024 * 1024


def coefficients(mu):
    def tree(terms):
        while len(terms) > 1:
            terms = [sum(terms[i : i + 2][1:], terms[i]) for i in range(0, len(terms), 2)]
        return terms[0]

    def quadratic(c, m):
        return tree([
            tree([c[i] * c[k - i] for i in range(max(0, k - len(c) + 1), min(k + 1, len(c)))]) * m[k]
            for k in range(2 * len(c) - 1)
        ])

    slope = [a - b for a, b in zip(mu[:-1], mu[1:])]
    one = jnp.ones_like(mu[0])
    scaled, direction, answer = [one], [one], []
    norm_now = mu[0]
    for step in range(ITERS):
        alpha = norm_now / quadratic(direction, slope)
        answer = [a + alpha * d for a, d in zip(answer, direction)] + [alpha * direction[-1]]
        if step + 1 < ITERS:
            image = [direction[0]]
            image += [b - a for a, b in zip(direction[:-1], direction[1:])]
            image += [-direction[-1]]
            scaled = [s - alpha * q for s, q in zip(scaled, image)] + [-alpha * image[-1]]
            fresh = quadratic(scaled, mu)
            beta = fresh / norm_now
            direction = [s + beta * d for s, d in zip(scaled, direction)] + [scaled[-1]]
            norm_now = fresh
    return answer


def kernel(
    nx, ny,
    levels, mask_in, elec_in, leak_in, src_in, wgt_in,
    answer_out, rims_out,
    mask, elec, leak, rhs, in_sem,
    cx, coef, coef_y_send, coef_y, coef_send, coef_recv,
    rim_x, rim_y, rim_y_send, rim_send, rim_recv,
    field, y_send, y_halo, corner_send, corner, halo_send, halo_recv,
    inner, part, gathered, part_send, part_recv,
    answer, rims, out_sem,
):
    bx, by_rows, nz = leak.shape
    ix, iy = lax.axis_index("gx"), lax.axis_index("gy")
    devices = nx * ny
    rank = ix * ny + iy
    has_x = (ix > 0, ix < nx - 1)
    has_y = (iy > 0, iy < ny - 1)
    to_x = (jnp.maximum(ix - 1, 0), jnp.minimum(ix + 1, nx - 1))
    to_y = (jnp.maximum(iy - 1, 0), jnp.minimum(iy + 1, ny - 1))
    edge_x, edge_y = (0, bx - 1), (0, by_rows - 1)

    loads = [
        pltpu.make_async_copy(mask_in, mask, in_sem.at[0]),
        pltpu.make_async_copy(elec_in, elec, in_sem.at[1]),
        pltpu.make_async_copy(leak_in, leak, in_sem.at[2]),
        pltpu.make_async_copy(src_in, rhs.at[0], in_sem.at[3]),
        pltpu.make_async_copy(wgt_in, rhs.at[1], in_sem.at[4]),
    ]
    for load in loads:
        load.start()

    def ahead(at, count, size):
        places = [at]
        for _ in range(1, count):
            later = places[-1] + 1
            places.append(jnp.where(later == size, 0, later))
        return places

    all_x, all_y = ahead(ix, nx, nx), ahead(iy, ny, ny)

    def each_other(act):
        for dx in range(nx):
            for dy in range(ny):
                if dx or dy:
                    act({"gx": all_x[dx], "gy": all_y[dy]})

    barrier = pltpu.get_barrier_semaphore()
    each_other(lambda to: pl.semaphore_signal(barrier, inc=1, device_id=to, device_id_type=MESH))
    pl.semaphore_wait(barrier, devices - 1)

    loads[0].wait()
    row = lax.broadcasted_iota(jnp.int32, (by_rows, nz), 0)
    lane = lax.broadcasted_iota(jnp.int32, (by_rows, nz), 1)
    row_x = lax.broadcasted_iota(jnp.int32, (bx, nz), 0)
    rim_y_send[...] = mask[1, :, by_rows - 1 : by_rows, :]
    rim_copy_x = pltpu.make_async_remote_copy(
        mask.at[0, bx - 1], rim_x, rim_send.at[0], rim_recv.at[0],
        device_id={"gx": to_x[1]}, device_id_type=MESH,
    )
    rim_copy_y = pltpu.make_async_remote_copy(
        rim_y_send, rim_y, rim_send.at[1], rim_recv.at[1],
        device_id={"gy": to_y[1]}, device_id_type=MESH,
    )
    pl.when(has_x[1])(rim_copy_x.start)
    pl.when(has_y[1])(rim_copy_y.start)

    @pl.when(jnp.logical_not(has_x[0]))
    def _():
        rim_x[...] = jnp.zeros_like(rim_x)

    @pl.when(jnp.logical_not(has_y[0]))
    def _():
        rim_y[...] = jnp.zeros_like(rim_y)

    for side in range(2):

        @pl.when(jnp.logical_not(has_x[side]))
        def _(side=side):
            for at in (0, 1) if side == 0 else (bx + 2, bx + 3):
                for k in range(ITERS):
                    for f in range(2):
                        field[k, f, at] = jnp.zeros((by_rows, nz), jnp.float32)
            for c in range(7):
                coef[c, 0 if side == 0 else bx + 1] = jnp.zeros((by_rows, nz), jnp.float32)

        @pl.when(jnp.logical_not(has_y[side]))
        def _(side=side):
            coef_y[side] = jnp.zeros_like(coef_y[side])
            for k in range(ITERS):
                y_halo[k, side] = jnp.zeros_like(y_halo[k, side])

    for c in range(4):

        @pl.when(jnp.logical_not(jnp.logical_and(has_x[c // 2], has_y[c % 2])))
        def _(c=c):
            for e in range(ITERS // 2):
                corner[e, c] = jnp.zeros_like(corner[e, c])

    def conductance(bits, d):
        return jnp.where(bits == 1, levels[1, d], levels[0, d])

    x_low = has_x[0].astype(jnp.float32)
    x_high = has_x[1].astype(jnp.float32)
    y_low = has_y[0].astype(jnp.float32)
    y_high = has_y[1].astype(jnp.float32)
    not_last_row = jnp.where(row < by_rows - 1, 1.0, y_high)
    for load in loads[1:]:
        load.wait()
    square = (by_rows, by_rows)
    eye = lax.broadcasted_iota(jnp.int32, square, 0) == lax.broadcasted_iota(jnp.int32, square, 1)

    def column(which, x):
        line = elec[which, pl.ds(x, 1), :].astype(jnp.float32)
        return jnp.sum(jnp.where(eye, line, 0.0), axis=1, keepdims=True)

    def set_up(x, carry):
        here = conductance(mask[0, x], 0) * jnp.where(x < bx - 1, 1.0, x_high)
        cx[x + 1] = here
        here_y = conductance(mask[1, x], 1) * not_last_row
        coef[2, x + 1] = here_y
        here_z = jnp.where(lane < nz - 1, conductance(mask[2, x], 2), 0.0)
        coef[4, x + 1] = here_z
        back_z = pltpu.roll(here_z, 1, 1)
        coef[5, x + 1] = back_z
        first = jnp.where(lane == 0, column(0, x), 0.0)
        last = jnp.where(lane == nz - 1, column(1, x), 0.0)
        rhs[0, x] = rhs[0, x] + first
        rhs[1, x] = rhs[1, x] + last
        leak[x] = leak[x] + first + last + here + here_y + here_z + back_z
        return carry

    lax.fori_loop(0, bx, set_up, 0, unroll=UNROLL)
    pl.when(has_x[0])(rim_copy_x.wait_recv)
    pl.when(has_y[0])(rim_copy_y.wait_recv)
    cx[0] = conductance(rim_x[...], 0) * x_low

    def halos(k):
        e = k // 2
        copies = []
        for side in range(2):
            mine, theirs = ((2, bx + 2), (bx, 0))[side]
            copies.append((has_x[side], has_x[1 - side], pltpu.make_async_remote_copy(
                field.at[k, :, pl.ds(mine, 2)], field.at[k, :, pl.ds(theirs, 2)],
                halo_send.at[e, side], halo_recv.at[e, side],
                device_id={"gx": to_x[side]}, device_id_type=MESH)))
            copies.append((has_y[side], has_y[1 - side], pltpu.make_async_remote_copy(
                y_send.at[e, side], y_halo.at[k, 1 - side],
                halo_send.at[e, 2 + side], halo_recv.at[e, 2 + side],
                device_id={"gy": to_y[side]}, device_id_type=MESH)))
        for c in range(4):
            a, b = c // 2, c % 2
            copies.append((
                jnp.logical_and(has_x[a], has_y[b]), jnp.logical_and(has_x[1 - a], has_y[1 - b]),
                pltpu.make_async_remote_copy(
                    corner_send.at[e, c], corner.at[e, 3 - c], halo_send.at[e, 4 + c], halo_recv.at[e, 4 + c],
                    device_id={"gx": to_x[a], "gy": to_y[b]}, device_id_type=MESH)))
        return copies

    def coef_copies():
        copies = []
        for side in range(2):
            mine, theirs = ((1, bx + 1), (bx, 0))[side]
            copies.append((has_x[side], has_x[1 - side], pltpu.make_async_remote_copy(
                coef.at[:, mine], coef.at[:, theirs], coef_send.at[side], coef_recv.at[side],
                device_id={"gx": to_x[side]}, device_id_type=MESH)))
            copies.append((has_y[side], has_y[1 - side], pltpu.make_async_remote_copy(
                coef_y_send.at[side], coef_y.at[1 - side], coef_send.at[2 + side], coef_recv.at[2 + side],
                device_id={"gy": to_y[side]}, device_id_type=MESH)))
        return copies

    def start(copies):
        for sends, _, copy in copies:
            pl.when(sends)(copy.start)

    def arrive(copies):
        for _, receives, copy in copies:
            pl.when(receives)(copy.wait_recv)

    def put(k, f, x, value):
        field[k, f, x + 2] = value
        if k % 2 == 0:
            for side in range(2):
                for deep in range(2):
                    at = deep if side == 0 else by_rows - 1 - deep
                    y_send[k // 2, side, f, deep, pl.ds(x, 1), :] = value[at : at + 1]

    def send(k):
        for c in range(4):
            at = edge_x[c // 2]
            for f in range(2):
                corner_send[k // 2, c, f] = y_send[k // 2, c % 2, f, 0, at : at + 1, :]
        start(halos(k))

    def fold(value):
        total = value[0:8]
        for at in range(8, by_rows, 8):
            total = total + value[at : at + 8]
        return total

    nought = jnp.zeros((8, nz), jnp.float32)

    def begin(x, sums):
        here_x, back_x, here_y = cx[x + 1], cx[x], coef[2, x + 1]
        back_y = jnp.where(row == 0, conductance(rim_y[x], 1) * y_low, pltpu.roll(here_y, 1, 0))
        scale = 1.0 / (leak[x] + back_x + back_y)
        coef[0, x + 1] = here_x
        coef[1, x + 1] = back_x
        coef[3, x + 1] = back_y
        coef[6, x + 1] = scale
        out = []
        for f in range(2):
            value = rhs[f, x] * scale
            put(0, f, x, value)
            out.append(sums[f] + fold(rhs[f, x] * value))
        return tuple(out)

    moments = [lax.fori_loop(0, bx, begin, (nought, nought), unroll=bx)]

    def stage(x, carry):
        for c in range(7):
            for side in range(2):
                at = edge_y[side]
                coef_y_send[side, c, pl.ds(x, 1), :] = coef[c, x + 1, at : at + 1, :]
        return carry

    def stencil(here, dn_x, up_x, dn_y, up_y, c):
        total = c[0] * up_x + c[1] * dn_x
        total = total + (c[2] * up_y + c[3] * dn_y)
        return total + (c[4] * pltpu.roll(here, nz - 1, 1) + c[5] * pltpu.roll(here, 1, 1))

    def beside(k, f, x, low, high):
        here = field[k, f, x + 2]
        up_y = jnp.where(row == by_rows - 1, high, pltpu.roll(here, by_rows - 1, 0))
        dn_y = jnp.where(row == 0, low, pltpu.roll(here, 1, 0))
        c = [coef[i, x + 1] for i in range(6)]
        return here, stencil(here, field[k, f, x + 1], field[k, f, x + 3], dn_y, up_y, c)

    def ghosts(k):
        e = k // 2
        for f in range(2):
            for side in range(2):
                x = (-1, bx)[side]
                _, total = beside(k, f, x, corner[e, 2 * side, f], corner[e, 2 * side + 1, f])
                field[k + 1, f, x + 2] = total * coef[6, x + 1]
                here, outer, own = y_halo[k, side, f, 0], y_halo[k, side, f, 1], y_send[e, side, f, 0]
                dn_x = jnp.where(row_x == 0, corner[e, side, f], pltpu.roll(here, 1, 0))
                up_x = jnp.where(row_x == bx - 1, corner[e, 2 + side, f], pltpu.roll(here, bx - 1, 0))
                dn_y, up_y = (outer, own) if side == 0 else (own, outer)
                total = stencil(here, dn_x, up_x, dn_y, up_y, [coef_y[side, i] for i in range(6)])
                y_halo[k + 1, side, f, 0] = total * coef_y[side, 6]

    def within(k):
        for x in range(bx):
            c = [coef[i, x + 1] for i in range(6)]
            for f in range(2):
                here = field[k, f, x + 2]
                up_y = jnp.where(row == by_rows - 1, 0.0, pltpu.roll(here, by_rows - 1, 0))
                dn_y = jnp.where(row == 0, 0.0, pltpu.roll(here, 1, 0))
                total = c[2] * up_y + c[3] * dn_y
                total = total + (c[4] * pltpu.roll(here, nz - 1, 1) + c[5] * pltpu.roll(here, 1, 1))
                if x > 0:
                    total = total + c[1] * field[k, f, x + 1]
                if x < bx - 1:
                    total = total + c[0] * field[k, f, x + 3]
                inner[f, x] = total

    def completed(k, f, x):
        total = inner[f, x]
        if x == 0:
            total = total + coef[1, 1] * field[k, f, 1]
        if x == bx - 1:
            total = total + coef[0, bx] * field[k, f, bx + 2]
        low, high = [y_halo[k, side, f, 0, x : x + 1, :] for side in range(2)]
        total = total + jnp.where(row == 0, coef[3, x + 1] * low, 0.0)
        total = total + jnp.where(row == by_rows - 1, coef[2, x + 1] * high, 0.0)
        return field[k, f, x + 2], total

    for k in range(ITERS):
        if k % 2 == 0:
            send(k)
            if k == 0:
                start(coef_copies()[0::2])
                lax.fori_loop(0, bx, stage, 0, unroll=UNROLL)
                start(coef_copies()[1::2])
            within(k)
            arrive(halos(k))
        sums = [nought] * (4 if k + 1 < ITERS else 2)
        for x in range(bx):
            at = 0
            for f in range(2):
                if k % 2 == 0:
                    here, total = completed(k, f, x)
                else:
                    low, high = [y_halo[k, side, f, 0, x : x + 1, :] for side in range(2)]
                    here, total = beside(k, f, x, low, high)
                sums[at] = sums[at] + fold(here * total)
                at += 1
                if k + 1 < ITERS:
                    value = total * coef[6, x + 1]
                    put(k + 1, f, x, value)
                    sums[at] = sums[at] + fold(value * total)
                    at += 1
        if k + 1 < ITERS:
            moments += [(sums[0], sums[2]), (sums[1], sums[3])]
        else:
            moments += [(sums[0], sums[1])]
        if k % 2 == 0:
            if k == 0:
                arrive(coef_copies())
            ghosts(k)

    rows = 2 * MOMENTS
    pick = lax.broadcasted_iota(jnp.int32, (rows, nz), 0) == lax.broadcasted_iota(jnp.int32, (rows, nz), 1)
    lines = [jnp.sum(value, axis=0, keepdims=True) for pair in moments for value in pair]
    each = jnp.sum(jnp.concatenate(lines, axis=0), axis=1, keepdims=True)
    message = jnp.sum(jnp.where(pick, each, 0.0), axis=0, keepdims=True)

    part[...] = message
    gathered[rank] = message
    each_other(lambda to: pltpu.make_async_remote_copy(
        part, gathered.at[rank], part_send, part_recv, device_id=to, device_id_type=MESH,
    ).start())
    others = gathered.at[pl.ds(0, devices - 1)]
    pltpu.make_async_copy(others, others, part_recv).wait()
    message = jnp.sum(gathered[...], axis=0)

    square = jnp.sum(jnp.where(pick, message, 0.0), axis=1, keepdims=True)
    square = jnp.broadcast_to(square, (rows, nz))
    weights = coefficients([square[2 * k : 2 * k + 2] for k in range(MOMENTS)])
    weights = [[jnp.broadcast_to(w[f : f + 1], (by_rows, nz)) for w in weights] for f in range(2)]

    def combine(x, carry):
        for f in range(2):
            total = weights[f][0] * field[0, f, x + 2]
            for k in range(1, ITERS):
                total = total + weights[f][k] * field[k, f, x + 2]
            answer[f, x] = total
        return carry

    lax.fori_loop(0, bx + 1, combine, 0, unroll=bx + 1)
    for f in range(2):
        rim = weights[f][0] * y_halo[0, 1, f, 0]
        for k in range(1, ITERS):
            rim = rim + weights[f][k] * y_halo[k, 1, f, 0]
        rims[f] = rim
    stores = [
        pltpu.make_async_copy(answer, answer_out, out_sem.at[0]),
        pltpu.make_async_copy(rims, rims_out, out_sem.at[1]),
    ]
    for store in stores:
        store.start()
    pl.when(has_x[1])(rim_copy_x.wait_send)
    pl.when(has_y[1])(rim_copy_y.wait_send)
    for sends, _, copy in coef_copies() + halos(0) + halos(2):
        pl.when(sends)(copy.wait_send)
    pltpu.make_async_copy(others, others, part_send).wait()
    for store in stores:
        store.wait()


def finish(nx, ny, answer_in, rims_in, pot_out, adj_out, sens_out, answer, rims, sens, in_sem, out_sem):
    bx, by_rows, nz = pot_out.shape
    loads = [
        pltpu.make_async_copy(answer_in, answer, in_sem.at[0]),
        pltpu.make_async_copy(rims_in, rims, in_sem.at[1]),
    ]
    for load in loads:
        load.start()
    stores = [
        pltpu.make_async_copy(answer.at[0, pl.ds(0, bx)], pot_out, out_sem.at[0]),
        pltpu.make_async_copy(answer.at[1, pl.ds(0, bx)], adj_out, out_sem.at[1]),
        pltpu.make_async_copy(sens, sens_out, out_sem.at[2]),
    ]
    loads[0].wait()
    stores[0].start()
    stores[1].start()
    loads[1].wait()
    row = lax.broadcasted_iota(jnp.int32, (by_rows, nz), 0)
    lane = lax.broadcasted_iota(jnp.int32, (by_rows, nz), 1)
    x_high = (lax.axis_index("gx") < nx - 1).astype(jnp.float32)
    y_high = (lax.axis_index("gy") < ny - 1).astype(jnp.float32)
    not_last_row = jnp.where(row < by_rows - 1, 1.0, y_high)

    def differences(x, carry):
        gaps = []
        for f in range(2):
            here = answer[f, x]
            up_y = jnp.where(row == by_rows - 1, rims[f, pl.ds(x, 1), :], pltpu.roll(here, by_rows - 1, 0))
            gaps.append((here - answer[f, x + 1], here - up_y, here - pltpu.roll(here, nz - 1, 1)))
        sens[0, x] = -gaps[1][0] * gaps[0][0] * jnp.where(x < bx - 1, 1.0, x_high)
        sens[1, x] = -gaps[1][1] * gaps[0][1] * not_last_row
        sens[2, x] = jnp.where(lane < nz - 1, -gaps[1][2] * gaps[0][2], 0.0)
        return carry

    lax.fori_loop(0, bx, differences, 0, unroll=bx)
    stores[2].start()
    for store in stores:
        store.wait()


def body(nx, ny, bond_mask, levels, electrode, leakage, source, weight):
    bx, by, nz = leakage.shape
    f32, i32 = jnp.float32, jnp.int32
    vmem, dma = pltpu.VMEM, pltpu.SemaphoreType.DMA
    block = (bx, by, nz)
    hbm = pl.BlockSpec(memory_space=pltpu.HBM)
    answer, rims = pl.pallas_call(
        functools.partial(kernel, nx, ny),
        out_shape=(
            jax.ShapeDtypeStruct((2, bx + 1, by, nz), f32),
            jax.ShapeDtypeStruct((2, bx, nz), f32),
        ),
        in_specs=[pl.BlockSpec(memory_space=pltpu.SMEM)] + [hbm] * 5,
        out_specs=[hbm] * 2,
        scratch_shapes=[
            vmem((3,) + block, i32), vmem((2, bx, by), i32), vmem(block, f32), vmem((2,) + block, f32), dma((5,)),
            vmem((bx + 1, by, nz), f32), vmem((7, bx + 2, by, nz), f32),
            vmem((2, 7, bx, nz), f32), vmem((2, 7, bx, nz), f32), dma((4,)), dma((4,)),
            vmem((by, nz), i32), vmem((bx, 1, nz), i32), vmem((bx, 1, nz), i32), dma((2,)), dma((2,)),
            vmem((ITERS, 2, bx + 4, by, nz), f32),
            vmem((ITERS // 2, 2, 2, 2, bx, nz), f32), vmem((ITERS, 2, 2, 2, bx, nz), f32),
            vmem((ITERS // 2, 4, 2, 1, nz), f32), vmem((ITERS // 2, 4, 2, 1, nz), f32),
            dma((ITERS // 2, 8)), dma((ITERS // 2, 8)),
            vmem((2,) + block, f32), vmem((1, nz), f32), vmem((nx * ny, 1, nz), f32), dma, dma,
            vmem((2, bx + 1, by, nz), f32), vmem((2, bx, nz), f32), dma((2,)),
        ],
        compiler_params=pltpu.CompilerParams(
            collective_id=0, has_side_effects=True, vmem_limit_bytes=VMEM_LIMIT
        ),
    )(levels, bond_mask, electrode, leakage, source, weight)
    return pl.pallas_call(
        functools.partial(finish, nx, ny),
        out_shape=(
            jax.ShapeDtypeStruct(block, f32),
            jax.ShapeDtypeStruct(block, f32),
            jax.ShapeDtypeStruct((3,) + block, f32),
        ),
        in_specs=[hbm] * 2,
        out_specs=[hbm] * 3,
        scratch_shapes=[
            vmem((2, bx + 1, by, nz), f32), vmem((2, bx, nz), f32), vmem((3,) + block, f32), dma((2,)), dma((3,)),
        ],
        compiler_params=pltpu.CompilerParams(vmem_limit_bytes=VMEM_LIMIT),
    )(answer, rims)


def solution(mesh):
    return jax.shard_map(
        functools.partial(body, mesh.shape["gx"], mesh.shape["gy"]),
        mesh=mesh,
        in_specs=(
            P(None, "gx", "gy", None),
            P(),
            P(None, "gx", "gy"),
            P("gx", "gy", None),
            P("gx", "gy", None),
            P("gx", "gy", None),
        ),
        out_specs=(P("gx", "gy", None), P("gx", "gy", None), P(None, "gx", "gy", None)),
        check_vma=False,
    )
```

```python
import functools

import jax
import jax.numpy as jnp
from jax import lax
from jax.experimental import pallas as pl
from jax.experimental.pallas import tpu as pltpu
from jax.sharding import PartitionSpec as P

ITERS = 4
MOMENTS = 2 * ITERS
MESH = pl.DeviceIdType.MESH
UNROLL = 4
VMEM_LIMIT = 62 * 1024 * 1024


def coefficients(mu):
    def tree(terms):
        while len(terms) > 1:
            terms = [sum(terms[i : i + 2][1:], terms[i]) for i in range(0, len(terms), 2)]
        return terms[0]

    def quadratic(c, m):
        return tree([
            tree([c[i] * c[k - i] for i in range(max(0, k - len(c) + 1), min(k + 1, len(c)))]) * m[k]
            for k in range(2 * len(c) - 1)
        ])

    slope = [a - b for a, b in zip(mu[:-1], mu[1:])]
    one = jnp.ones_like(mu[0])
    scaled, direction, answer = [one], [one], []
    norm_now = mu[0]
    for step in range(ITERS):
        alpha = norm_now / quadratic(direction, slope)
        answer = [a + alpha * d for a, d in zip(answer, direction)] + [alpha * direction[-1]]
        if step + 1 < ITERS:
            image = [direction[0]]
            image += [b - a for a, b in zip(direction[:-1], direction[1:])]
            image += [-direction[-1]]
            scaled = [s - alpha * q for s, q in zip(scaled, image)] + [-alpha * image[-1]]
            fresh = quadratic(scaled, mu)
            beta = fresh / norm_now
            direction = [s + beta * d for s, d in zip(scaled, direction)] + [scaled[-1]]
            norm_now = fresh
    return answer


def kernel(
    nx, ny,
    levels, mask_in, elec_in, leak_in, src_in, wgt_in,
    answer_out, rims_out,
    mask, elec, leak, rhs, in_sem,
    cx, coef, factor_x_send, factor_x, factor_y_send, factor_y, factor_send, factor_recv,
    own_x_send, own_x, own_y_send, own_y, own_send, own_recv,
    rim_x, rim_y, rim_y_send, rim_send, rim_recv,
    field, y_send, y_halo, corner_send, corner, halo_send, halo_recv,
    inner, part, gathered, part_send, part_recv,
    answer, rims, out_sem,
):
    bx, by_rows, nz = leak.shape
    ix, iy = lax.axis_index("gx"), lax.axis_index("gy")
    devices = nx * ny
    rank = ix * ny + iy
    has_x = (ix > 0, ix < nx - 1)
    has_y = (iy > 0, iy < ny - 1)
    to_x = (jnp.maximum(ix - 1, 0), jnp.minimum(ix + 1, nx - 1))
    to_y = (jnp.maximum(iy - 1, 0), jnp.minimum(iy + 1, ny - 1))
    edge_x, edge_y = (0, bx - 1), (0, by_rows - 1)

    loads = [
        pltpu.make_async_copy(mask_in, mask, in_sem.at[0]),
        pltpu.make_async_copy(elec_in, elec, in_sem.at[1]),
        pltpu.make_async_copy(leak_in, leak, in_sem.at[2]),
        pltpu.make_async_copy(src_in, rhs.at[0], in_sem.at[3]),
        pltpu.make_async_copy(wgt_in, rhs.at[1], in_sem.at[4]),
    ]
    for load in loads:
        load.start()

    def ahead(at, count, size):
        places = [at]
        for _ in range(1, count):
            later = places[-1] + 1
            places.append(jnp.where(later == size, 0, later))
        return places

    all_x, all_y = ahead(ix, nx, nx), ahead(iy, ny, ny)

    def each_other(act):
        for dx in range(nx):
            for dy in range(ny):
                if dx or dy:
                    act({"gx": all_x[dx], "gy": all_y[dy]})

    barrier = pltpu.get_barrier_semaphore()
    each_other(lambda to: pl.semaphore_signal(barrier, inc=1, device_id=to, device_id_type=MESH))
    pl.semaphore_wait(barrier, devices - 1)

    loads[0].wait()
    row = lax.broadcasted_iota(jnp.int32, (by_rows, nz), 0)
    lane = lax.broadcasted_iota(jnp.int32, (by_rows, nz), 1)
    row_x = lax.broadcasted_iota(jnp.int32, (bx, nz), 0)
    rim_y_send[...] = mask[1, :, by_rows - 1 : by_rows, :]
    rim_copy_x = pltpu.make_async_remote_copy(
        mask.at[0, bx - 1], rim_x, rim_send.at[0], rim_recv.at[0],
        device_id={"gx": to_x[1]}, device_id_type=MESH,
    )
    rim_copy_y = pltpu.make_async_remote_copy(
        rim_y_send, rim_y, rim_send.at[1], rim_recv.at[1],
        device_id={"gy": to_y[1]}, device_id_type=MESH,
    )
    pl.when(has_x[1])(rim_copy_x.start)
    pl.when(has_y[1])(rim_copy_y.start)

    @pl.when(jnp.logical_not(has_x[0]))
    def _():
        rim_x[...] = jnp.zeros_like(rim_x)

    @pl.when(jnp.logical_not(has_y[0]))
    def _():
        rim_y[...] = jnp.zeros_like(rim_y)

    for side in range(2):

        @pl.when(jnp.logical_not(has_x[side]))
        def _(side=side):
            for k in range(ITERS):
                for f in range(2):
                    field[k, f, 1 if side == 0 else bx + 2] = jnp.zeros((by_rows, nz), jnp.float32)
            factor_x[side] = jnp.zeros_like(factor_x[side])
            for e in range(ITERS // 2):
                own_x[e, side] = jnp.zeros_like(own_x[e, side])

        @pl.when(jnp.logical_not(has_y[side]))
        def _(side=side):
            factor_y[side] = jnp.zeros_like(factor_y[side])
            for e in range(ITERS // 2):
                own_y[e, side] = jnp.zeros_like(own_y[e, side])
            for k in range(ITERS):
                y_halo[k, side] = jnp.zeros_like(y_halo[k, side])

    for c in range(4):

        @pl.when(jnp.logical_not(jnp.logical_and(has_x[c // 2], has_y[c % 2])))
        def _(c=c):
            for e in range(ITERS // 2):
                corner[e, c] = jnp.zeros_like(corner[e, c])

    def conductance(bits, d):
        return jnp.where(bits == 1, levels[1, d], levels[0, d])

    x_low = has_x[0].astype(jnp.float32)
    x_high = has_x[1].astype(jnp.float32)
    y_low = has_y[0].astype(jnp.float32)
    y_high = has_y[1].astype(jnp.float32)
    not_last_row = jnp.where(row < by_rows - 1, 1.0, y_high)
    for load in loads[1:]:
        load.wait()
    square = (by_rows, by_rows)
    eye = lax.broadcasted_iota(jnp.int32, square, 0) == lax.broadcasted_iota(jnp.int32, square, 1)

    def column(which, x):
        line = elec[which, pl.ds(x, 1), :].astype(jnp.float32)
        return jnp.sum(jnp.where(eye, line, 0.0), axis=1, keepdims=True)

    def set_up(x, carry):
        here = conductance(mask[0, x], 0) * jnp.where(x < bx - 1, 1.0, x_high)
        cx[x + 1] = here
        here_y = conductance(mask[1, x], 1) * not_last_row
        coef[2, x + 1] = here_y
        here_z = jnp.where(lane < nz - 1, conductance(mask[2, x], 2), 0.0)
        coef[4, x + 1] = here_z
        back_z = pltpu.roll(here_z, 1, 1)
        coef[5, x + 1] = back_z
        first = jnp.where(lane == 0, column(0, x), 0.0)
        last = jnp.where(lane == nz - 1, column(1, x), 0.0)
        rhs[0, x] = rhs[0, x] + first
        rhs[1, x] = rhs[1, x] + last
        leak[x] = leak[x] + first + last + here + here_y + here_z + back_z
        return carry

    lax.fori_loop(0, bx, set_up, 0, unroll=UNROLL)
    pl.when(has_x[0])(rim_copy_x.wait_recv)
    pl.when(has_y[0])(rim_copy_y.wait_recv)
    cx[0] = conductance(rim_x[...], 0) * x_low

    def halos(k):
        e = k // 2
        copies = []
        for side in range(2):
            mine, theirs = ((2, bx + 2), (bx + 1, 1))[side]
            copies.append((has_x[side], has_x[1 - side], pltpu.make_async_remote_copy(
                field.at[k, :, mine], field.at[k, :, theirs],
                halo_send.at[e, side], halo_recv.at[e, side],
                device_id={"gx": to_x[side]}, device_id_type=MESH)))
            copies.append((has_y[side], has_y[1 - side], pltpu.make_async_remote_copy(
                y_send.at[e, side], y_halo.at[k, 1 - side],
                halo_send.at[e, 2 + side], halo_recv.at[e, 2 + side],
                device_id={"gy": to_y[side]}, device_id_type=MESH)))
        for c in range(4):
            a, b = c // 2, c % 2
            copies.append((
                jnp.logical_and(has_x[a], has_y[b]), jnp.logical_and(has_x[1 - a], has_y[1 - b]),
                pltpu.make_async_remote_copy(
                    corner_send.at[e, c], corner.at[e, 3 - c], halo_send.at[e, 4 + c], halo_recv.at[e, 4 + c],
                    device_id={"gx": to_x[a], "gy": to_y[b]}, device_id_type=MESH)))
        return copies

    def sided(x_from, x_to, y_from, y_to, sends, receives):
        copies = []
        for side in range(2):
            copies.append((has_x[side], has_x[1 - side], pltpu.make_async_remote_copy(
                x_from.at[side], x_to.at[1 - side], sends.at[side], receives.at[side],
                device_id={"gx": to_x[side]}, device_id_type=MESH)))
            copies.append((has_y[side], has_y[1 - side], pltpu.make_async_remote_copy(
                y_from.at[side], y_to.at[1 - side], sends.at[2 + side], receives.at[2 + side],
                device_id={"gy": to_y[side]}, device_id_type=MESH)))
        return copies

    def factor_copies():
        return sided(factor_x_send, factor_x, factor_y_send, factor_y, factor_send, factor_recv)

    def own_copies(k):
        e = k // 2
        return sided(
            own_x_send.at[e], own_x.at[e], own_y_send.at[e], own_y.at[e], own_send.at[e], own_recv.at[e]
        )

    def start(copies):
        for sends, _, copy in copies:
            pl.when(sends)(copy.start)

    def arrive(copies):
        for _, receives, copy in copies:
            pl.when(receives)(copy.wait_recv)

    def put(k, f, x, value):
        field[k, f, x + 2] = value
        if k % 2 == 0:
            for side in range(2):
                at = edge_y[side]
                y_send[k // 2, side, f, x : x + 1, :] = value[at : at + 1]

    def send(k):
        for c in range(4):
            at = edge_x[c // 2]
            for f in range(2):
                corner_send[k // 2, c, f] = y_send[k // 2, c % 2, f, at : at + 1, :]
        start(halos(k))

    def fold(value):
        total = value[0:8]
        for at in range(8, by_rows, 8):
            total = total + value[at : at + 8]
        return total

    nought = jnp.zeros((8, nz), jnp.float32)

    sums = [nought, nought]
    for x in range(bx):
        here_x, back_x, here_y = cx[x + 1], cx[x], coef[2, x + 1]
        back_y = jnp.where(row == 0, conductance(rim_y[x], 1) * y_low, pltpu.roll(here_y, 1, 0))
        scale = 1.0 / (leak[x] + back_x + back_y)
        coef[0, x + 1] = here_x
        coef[1, x + 1] = back_x
        coef[3, x + 1] = back_y
        coef[6, x + 1] = scale
        for f in range(2):
            value = rhs[f, x] * scale
            put(0, f, x, value)
            sums[f] = sums[f] + fold(rhs[f, x] * value)
    moments = [tuple(sums)]

    def factors():
        for side in range(2):
            factor_x_send[side, by_rows:, :] = jnp.zeros((8, nz), jnp.float32)
            factor_y_send[side, bx:, :] = jnp.zeros((8, nz), jnp.float32)
        for x in range(bx):
            scale = coef[6, x + 1]
            for side in range(2):
                at = edge_y[side]
                factor_y_send[side, x : x + 1, :] = (coef[(3, 2)[side], x + 1] * scale)[at : at + 1]
        for side in range(2):
            at = edge_x[side] + 1
            factor_x_send[side, 0:by_rows, :] = coef[(1, 0)[side], at] * coef[6, at]
        for side in range(2):
            for end in range(2):
                at = edge_x[side]
                factor_x_send[side, by_rows + end : by_rows + end + 1, :] = factor_y_send[end, at : at + 1, :]
                at = edge_y[side]
                factor_y_send[side, bx + end : bx + end + 1, :] = factor_x_send[end, at : at + 1, :]

    def stencil(here, dn_x, up_x, dn_y, up_y, c):
        total = c[0] * up_x + c[1] * dn_x
        total = total + (c[2] * up_y + c[3] * dn_y)
        return total + (c[4] * pltpu.roll(here, nz - 1, 1) + c[5] * pltpu.roll(here, 1, 1))

    def beside(k, f, x, low, high):
        here = field[k, f, x + 2]
        up_y = jnp.where(row == by_rows - 1, high, pltpu.roll(here, by_rows - 1, 0))
        dn_y = jnp.where(row == 0, low, pltpu.roll(here, 1, 0))
        c = [coef[i, x + 1] for i in range(6)]
        return here, stencil(here, field[k, f, x + 1], field[k, f, x + 3], dn_y, up_y, c)

    def ghosts(k):
        e = k // 2
        for side in range(2):
            fx, fy = factor_x[side], factor_y[side]
            for f in range(2):
                total = own_x[e, side, f] + fx[0:by_rows] * field[k, f, edge_x[side] + 2]
                total = total + jnp.where(row == 0, fx[by_rows : by_rows + 1] * corner[e, 2 * side, f], 0.0)
                total = total + jnp.where(
                    row == by_rows - 1, fx[by_rows + 1 : by_rows + 2] * corner[e, 2 * side + 1, f], 0.0
                )
                field[k + 1, f, (1, bx + 2)[side]] = total
                total = own_y[e, side, f] + fy[0:bx] * y_send[e, side, f]
                total = total + jnp.where(row_x == 0, fy[bx : bx + 1] * corner[e, side, f], 0.0)
                total = total + jnp.where(row_x == bx - 1, fy[bx + 1 : bx + 2] * corner[e, 2 + side, f], 0.0)
                y_halo[k + 1, side, f] = total

    def within(k):
        for x in range(bx):
            c = [coef[i, x + 1] for i in range(6)]
            for f in range(2):
                here = field[k, f, x + 2]
                up_y = jnp.where(row == by_rows - 1, 0.0, pltpu.roll(here, by_rows - 1, 0))
                dn_y = jnp.where(row == 0, 0.0, pltpu.roll(here, 1, 0))
                total = c[2] * up_y + c[3] * dn_y
                total = total + (c[4] * pltpu.roll(here, nz - 1, 1) + c[5] * pltpu.roll(here, 1, 1))
                if x > 0:
                    total = total + c[1] * field[k, f, x + 1]
                if x < bx - 1:
                    total = total + c[0] * field[k, f, x + 3]
                inner[f, x] = total
                part_here = total * coef[6, x + 1]
                for side in range(2):
                    if x == edge_x[side]:
                        own_x_send[k // 2, side, f] = part_here
                    at = edge_y[side]
                    own_y_send[k // 2, side, f, x : x + 1, :] = part_here[at : at + 1]

    def completed(k, f, x):
        total = inner[f, x]
        if x == 0:
            total = total + coef[1, 1] * field[k, f, 1]
        if x == bx - 1:
            total = total + coef[0, bx] * field[k, f, bx + 2]
        low, high = [y_halo[k, side, f, x : x + 1, :] for side in range(2)]
        total = total + jnp.where(row == 0, coef[3, x + 1] * low, 0.0)
        total = total + jnp.where(row == by_rows - 1, coef[2, x + 1] * high, 0.0)
        return field[k, f, x + 2], total

    for k in range(ITERS):
        if k % 2 == 0:
            send(k)
            if k == 0:
                factors()
                start(factor_copies())
            within(k)
            start(own_copies(k))
            arrive(halos(k))
        sums = [nought] * (4 if k + 1 < ITERS else 2)
        for x in range(bx):
            at = 0
            for f in range(2):
                if k % 2 == 0:
                    here, total = completed(k, f, x)
                else:
                    low, high = [y_halo[k, side, f, x : x + 1, :] for side in range(2)]
                    here, total = beside(k, f, x, low, high)
                sums[at] = sums[at] + fold(here * total)
                at += 1
                if k + 1 < ITERS:
                    value = total * coef[6, x + 1]
                    put(k + 1, f, x, value)
                    sums[at] = sums[at] + fold(value * total)
                    at += 1
        if k + 1 < ITERS:
            moments += [(sums[0], sums[2]), (sums[1], sums[3])]
        else:
            moments += [(sums[0], sums[1])]
        if k % 2 == 0:
            if k == 0:
                arrive(factor_copies())
            arrive(own_copies(k))
            ghosts(k)

    rows = 2 * MOMENTS
    pick = lax.broadcasted_iota(jnp.int32, (rows, nz), 0) == lax.broadcasted_iota(jnp.int32, (rows, nz), 1)
    lines = [jnp.sum(value, axis=0, keepdims=True) for pair in moments for value in pair]
    each = jnp.sum(jnp.concatenate(lines, axis=0), axis=1, keepdims=True)
    message = jnp.sum(jnp.where(pick, each, 0.0), axis=0, keepdims=True)

    part[...] = message
    gathered[rank] = message
    each_other(lambda to: pltpu.make_async_remote_copy(
        part, gathered.at[rank], part_send, part_recv, device_id=to, device_id_type=MESH,
    ).start())
    others = gathered.at[pl.ds(0, devices - 1)]
    pltpu.make_async_copy(others, others, part_recv).wait()
    message = jnp.sum(gathered[...], axis=0)

    square = jnp.sum(jnp.where(pick, message, 0.0), axis=1, keepdims=True)
    square = jnp.broadcast_to(square, (rows, nz))
    weights = coefficients([square[2 * k : 2 * k + 2] for k in range(MOMENTS)])
    weights = [[jnp.broadcast_to(w[f : f + 1], (by_rows, nz)) for w in weights] for f in range(2)]

    def combine(x, carry):
        for f in range(2):
            total = weights[f][0] * field[0, f, x + 2]
            for k in range(1, ITERS):
                total = total + weights[f][k] * field[k, f, x + 2]
            answer[f, x] = total
        return carry

    lax.fori_loop(0, bx + 1, combine, 0, unroll=bx + 1)
    for f in range(2):
        rim = weights[f][0] * y_halo[0, 1, f]
        for k in range(1, ITERS):
            rim = rim + weights[f][k] * y_halo[k, 1, f]
        rims[f] = rim
    stores = [
        pltpu.make_async_copy(answer, answer_out, out_sem.at[0]),
        pltpu.make_async_copy(rims, rims_out, out_sem.at[1]),
    ]
    for store in stores:
        store.start()
    pl.when(has_x[1])(rim_copy_x.wait_send)
    pl.when(has_y[1])(rim_copy_y.wait_send)
    for sends, _, copy in factor_copies() + own_copies(0) + own_copies(2) + halos(0) + halos(2):
        pl.when(sends)(copy.wait_send)
    pltpu.make_async_copy(others, others, part_send).wait()
    for store in stores:
        store.wait()


def finish(nx, ny, answer_in, rims_in, pot_out, adj_out, sens_out, answer, rims, sens, in_sem, out_sem):
    bx, by_rows, nz = pot_out.shape
    loads = [
        pltpu.make_async_copy(answer_in, answer, in_sem.at[0]),
        pltpu.make_async_copy(rims_in, rims, in_sem.at[1]),
    ]
    for load in loads:
        load.start()
    stores = [
        pltpu.make_async_copy(answer.at[0, pl.ds(0, bx)], pot_out, out_sem.at[0]),
        pltpu.make_async_copy(answer.at[1, pl.ds(0, bx)], adj_out, out_sem.at[1]),
        pltpu.make_async_copy(sens, sens_out, out_sem.at[2]),
    ]
    loads[0].wait()
    stores[0].start()
    stores[1].start()
    loads[1].wait()
    row = lax.broadcasted_iota(jnp.int32, (by_rows, nz), 0)
    lane = lax.broadcasted_iota(jnp.int32, (by_rows, nz), 1)
    x_high = (lax.axis_index("gx") < nx - 1).astype(jnp.float32)
    y_high = (lax.axis_index("gy") < ny - 1).astype(jnp.float32)
    not_last_row = jnp.where(row < by_rows - 1, 1.0, y_high)

    def differences(x, carry):
        gaps = []
        for f in range(2):
            here = answer[f, x]
            up_y = jnp.where(row == by_rows - 1, rims[f, pl.ds(x, 1), :], pltpu.roll(here, by_rows - 1, 0))
            gaps.append((here - answer[f, x + 1], here - up_y, here - pltpu.roll(here, nz - 1, 1)))
        sens[0, x] = -gaps[1][0] * gaps[0][0] * jnp.where(x < bx - 1, 1.0, x_high)
        sens[1, x] = -gaps[1][1] * gaps[0][1] * not_last_row
        sens[2, x] = jnp.where(lane < nz - 1, -gaps[1][2] * gaps[0][2], 0.0)
        return carry

    lax.fori_loop(0, bx, differences, 0, unroll=bx)
    stores[2].start()
    for store in stores:
        store.wait()


def body(nx, ny, bond_mask, levels, electrode, leakage, source, weight):
    bx, by, nz = leakage.shape
    f32, i32 = jnp.float32, jnp.int32
    vmem, dma = pltpu.VMEM, pltpu.SemaphoreType.DMA
    block = (bx, by, nz)
    hbm = pl.BlockSpec(memory_space=pltpu.HBM)
    answer, rims = pl.pallas_call(
        functools.partial(kernel, nx, ny),
        out_shape=(
            jax.ShapeDtypeStruct((2, bx + 1, by, nz), f32),
            jax.ShapeDtypeStruct((2, bx, nz), f32),
        ),
        in_specs=[pl.BlockSpec(memory_space=pltpu.SMEM)] + [hbm] * 5,
        out_specs=[hbm] * 2,
        scratch_shapes=[
            vmem((3,) + block, i32), vmem((2, bx, by), i32), vmem(block, f32), vmem((2,) + block, f32), dma((5,)),
            vmem((bx + 1, by, nz), f32), vmem((7, bx + 2, by, nz), f32),
            vmem((2, by + 8, nz), f32), vmem((2, by + 8, nz), f32),
            vmem((2, bx + 8, nz), f32), vmem((2, bx + 8, nz), f32), dma((4,)), dma((4,)),
            vmem((ITERS // 2, 2, 2, by, nz), f32), vmem((ITERS // 2, 2, 2, by, nz), f32),
            vmem((ITERS // 2, 2, 2, bx, nz), f32), vmem((ITERS // 2, 2, 2, bx, nz), f32),
            dma((ITERS // 2, 4)), dma((ITERS // 2, 4)),
            vmem((by, nz), i32), vmem((bx, 1, nz), i32), vmem((bx, 1, nz), i32), dma((2,)), dma((2,)),
            vmem((ITERS, 2, bx + 4, by, nz), f32),
            vmem((ITERS // 2, 2, 2, bx, nz), f32), vmem((ITERS, 2, 2, bx, nz), f32),
            vmem((ITERS // 2, 4, 2, 1, nz), f32), vmem((ITERS // 2, 4, 2, 1, nz), f32),
            dma((ITERS // 2, 8)), dma((ITERS // 2, 8)),
            vmem((2,) + block, f32), vmem((1, nz), f32), vmem((nx * ny, 1, nz), f32), dma, dma,
            vmem((2, bx + 1, by, nz), f32), vmem((2, bx, nz), f32), dma((2,)),
        ],
        compiler_params=pltpu.CompilerParams(
            collective_id=0, has_side_effects=True, vmem_limit_bytes=VMEM_LIMIT
        ),
    )(levels, bond_mask, electrode, leakage, source, weight)
    return pl.pallas_call(
        functools.partial(finish, nx, ny),
        out_shape=(
            jax.ShapeDtypeStruct(block, f32),
            jax.ShapeDtypeStruct(block, f32),
            jax.ShapeDtypeStruct((3,) + block, f32),
        ),
        in_specs=[hbm] * 2,
        out_specs=[hbm] * 3,
        scratch_shapes=[
            vmem((2, bx + 1, by, nz), f32), vmem((2, bx, nz), f32), vmem((3,) + block, f32), dma((2,)), dma((3,)),
        ],
        compiler_params=pltpu.CompilerParams(vmem_limit_bytes=VMEM_LIMIT),
    )(answer, rims)


def solution(mesh):
    return jax.shard_map(
        functools.partial(body, mesh.shape["gx"], mesh.shape["gy"]),
        mesh=mesh,
        in_specs=(
            P(None, "gx", "gy", None),
            P(),
            P(None, "gx", "gy"),
            P("gx", "gy", None),
            P("gx", "gy", None),
            P("gx", "gy", None),
        ),
        out_specs=(P("gx", "gy", None), P("gx", "gy", None), P(None, "gx", "gy", None)),
        check_vma=False,
    )
```

```python
import functools

import jax
import jax.numpy as jnp
from jax import lax
from jax.experimental import pallas as pl
from jax.experimental.pallas import tpu as pltpu
from jax.sharding import PartitionSpec as P

ITERS = 4
MOMENTS = 2 * ITERS
EARLY = 5
MESH = pl.DeviceIdType.MESH
UNROLL = 4
VMEM_LIMIT = 62 * 1024 * 1024


def coefficients(mu):
    def tree(terms):
        while len(terms) > 1:
            terms = [sum(terms[i : i + 2][1:], terms[i]) for i in range(0, len(terms), 2)]
        return terms[0]

    def quadratic(c, m):
        return tree([
            tree([c[i] * c[k - i] for i in range(max(0, k - len(c) + 1), min(k + 1, len(c)))]) * m(k)
            for k in range(2 * len(c) - 1)
        ])

    def slope(k):
        return mu(k) - mu(k + 1)

    one = jnp.ones_like(mu(0))
    scaled, direction, answer = [one], [one], []
    norm_now = mu(0)
    for step in range(ITERS):
        alpha = norm_now / quadratic(direction, slope)
        answer = [a + alpha * d for a, d in zip(answer, direction)] + [alpha * direction[-1]]
        if step + 1 < ITERS:
            image = [direction[0]]
            image += [b - a for a, b in zip(direction[:-1], direction[1:])]
            image += [-direction[-1]]
            scaled = [s - alpha * q for s, q in zip(scaled, image)] + [-alpha * image[-1]]
            fresh = quadratic(scaled, mu)
            beta = fresh / norm_now
            direction = [s + beta * d for s, d in zip(scaled, direction)] + [scaled[-1]]
            norm_now = fresh
    return answer


def kernel(
    nx, ny,
    levels, mask_in, elec_in, leak_in, src_in, wgt_in,
    answer_out, rims_out,
    mask, elec, leak, rhs, in_sem,
    cx, coef, factor_x_send, factor_x, factor_y_send, factor_y, factor_send, factor_recv,
    own_x_send, own_x, own_y_send, own_y, own_send, own_recv,
    rim_x, rim_y, rim_y_send, rim_send, rim_recv,
    field, y_send, y_halo, corner_send, corner, halo_send, halo_recv,
    inner, part, gathered, part_send, part_recv,
    answer, rims, out_sem,
):
    bx, by_rows, nz = leak.shape
    ix, iy = lax.axis_index("gx"), lax.axis_index("gy")
    devices = nx * ny
    rank = ix * ny + iy
    has_x = (ix > 0, ix < nx - 1)
    has_y = (iy > 0, iy < ny - 1)
    to_x = (jnp.maximum(ix - 1, 0), jnp.minimum(ix + 1, nx - 1))
    to_y = (jnp.maximum(iy - 1, 0), jnp.minimum(iy + 1, ny - 1))
    edge_x, edge_y = (0, bx - 1), (0, by_rows - 1)

    loads = [
        pltpu.make_async_copy(mask_in, mask, in_sem.at[0]),
        pltpu.make_async_copy(elec_in, elec, in_sem.at[1]),
        pltpu.make_async_copy(leak_in, leak, in_sem.at[2]),
        pltpu.make_async_copy(src_in, rhs.at[0], in_sem.at[3]),
        pltpu.make_async_copy(wgt_in, rhs.at[1], in_sem.at[4]),
    ]
    for load in loads:
        load.start()

    def ahead(at, count, size):
        places = [at]
        for _ in range(1, count):
            later = places[-1] + 1
            places.append(jnp.where(later == size, 0, later))
        return places

    all_x, all_y = ahead(ix, nx, nx), ahead(iy, ny, ny)

    def each_other(act):
        for dx in range(nx):
            for dy in range(ny):
                if dx or dy:
                    act({"gx": all_x[dx], "gy": all_y[dy]})

    barrier = pltpu.get_barrier_semaphore()
    each_other(lambda to: pl.semaphore_signal(barrier, inc=1, device_id=to, device_id_type=MESH))
    pl.semaphore_wait(barrier, devices - 1)

    loads[0].wait()
    row = lax.broadcasted_iota(jnp.int32, (by_rows, nz), 0)
    lane = lax.broadcasted_iota(jnp.int32, (by_rows, nz), 1)
    row_x = lax.broadcasted_iota(jnp.int32, (bx, nz), 0)
    rim_y_send[...] = mask[1, :, by_rows - 1 : by_rows, :]
    rim_copy_x = pltpu.make_async_remote_copy(
        mask.at[0, bx - 1], rim_x, rim_send.at[0], rim_recv.at[0],
        device_id={"gx": to_x[1]}, device_id_type=MESH,
    )
    rim_copy_y = pltpu.make_async_remote_copy(
        rim_y_send, rim_y, rim_send.at[1], rim_recv.at[1],
        device_id={"gy": to_y[1]}, device_id_type=MESH,
    )
    pl.when(has_x[1])(rim_copy_x.start)
    pl.when(has_y[1])(rim_copy_y.start)

    @pl.when(jnp.logical_not(has_x[0]))
    def _():
        rim_x[...] = jnp.zeros_like(rim_x)

    @pl.when(jnp.logical_not(has_y[0]))
    def _():
        rim_y[...] = jnp.zeros_like(rim_y)

    for side in range(2):

        @pl.when(jnp.logical_not(has_x[side]))
        def _(side=side):
            for k in range(ITERS):
                for f in range(2):
                    field[k, f, 1 if side == 0 else bx + 2] = jnp.zeros((by_rows, nz), jnp.float32)
            factor_x[side] = jnp.zeros_like(factor_x[side])
            for e in range(ITERS // 2):
                own_x[e, side] = jnp.zeros_like(own_x[e, side])

        @pl.when(jnp.logical_not(has_y[side]))
        def _(side=side):
            factor_y[side] = jnp.zeros_like(factor_y[side])
            for e in range(ITERS // 2):
                own_y[e, side] = jnp.zeros_like(own_y[e, side])
            for k in range(ITERS):
                y_halo[k, side] = jnp.zeros_like(y_halo[k, side])

    for c in range(4):

        @pl.when(jnp.logical_not(jnp.logical_and(has_x[c // 2], has_y[c % 2])))
        def _(c=c):
            for e in range(ITERS // 2):
                corner[e, c] = jnp.zeros_like(corner[e, c])

    def conductance(bits, d):
        return jnp.where(bits == 1, levels[1, d], levels[0, d])

    x_low = has_x[0].astype(jnp.float32)
    x_high = has_x[1].astype(jnp.float32)
    y_low = has_y[0].astype(jnp.float32)
    y_high = has_y[1].astype(jnp.float32)
    not_last_row = jnp.where(row < by_rows - 1, 1.0, y_high)
    for load in loads[1:]:
        load.wait()
    square = (by_rows, by_rows)
    eye = lax.broadcasted_iota(jnp.int32, square, 0) == lax.broadcasted_iota(jnp.int32, square, 1)

    def column(which, x):
        line = elec[which, pl.ds(x, 1), :].astype(jnp.float32)
        return jnp.sum(jnp.where(eye, line, 0.0), axis=1, keepdims=True)

    def set_up(x, carry):
        here = conductance(mask[0, x], 0) * jnp.where(x < bx - 1, 1.0, x_high)
        cx[x + 1] = here
        here_y = conductance(mask[1, x], 1) * not_last_row
        coef[2, x + 1] = here_y
        here_z = jnp.where(lane < nz - 1, conductance(mask[2, x], 2), 0.0)
        coef[4, x + 1] = here_z
        back_z = pltpu.roll(here_z, 1, 1)
        coef[5, x + 1] = back_z
        first = jnp.where(lane == 0, column(0, x), 0.0)
        last = jnp.where(lane == nz - 1, column(1, x), 0.0)
        rhs[0, x] = rhs[0, x] + first
        rhs[1, x] = rhs[1, x] + last
        leak[x] = leak[x] + first + last + here + here_y + here_z + back_z
        return carry

    lax.fori_loop(0, bx, set_up, 0, unroll=UNROLL)
    pl.when(has_x[0])(rim_copy_x.wait_recv)
    pl.when(has_y[0])(rim_copy_y.wait_recv)
    cx[0] = conductance(rim_x[...], 0) * x_low

    def halos(k):
        e = k // 2
        copies = []
        for side in range(2):
            mine, theirs = ((2, bx + 2), (bx + 1, 1))[side]
            copies.append((has_x[side], has_x[1 - side], pltpu.make_async_remote_copy(
                field.at[k, :, mine], field.at[k, :, theirs],
                halo_send.at[e, side], halo_recv.at[e, side],
                device_id={"gx": to_x[side]}, device_id_type=MESH)))
            copies.append((has_y[side], has_y[1 - side], pltpu.make_async_remote_copy(
                y_send.at[e, side], y_halo.at[k, 1 - side],
                halo_send.at[e, 2 + side], halo_recv.at[e, 2 + side],
                device_id={"gy": to_y[side]}, device_id_type=MESH)))
        for c in range(4):
            a, b = c // 2, c % 2
            copies.append((
                jnp.logical_and(has_x[a], has_y[b]), jnp.logical_and(has_x[1 - a], has_y[1 - b]),
                pltpu.make_async_remote_copy(
                    corner_send.at[e, c], corner.at[e, 3 - c], halo_send.at[e, 4 + c], halo_recv.at[e, 4 + c],
                    device_id={"gx": to_x[a], "gy": to_y[b]}, device_id_type=MESH)))
        return copies

    def sided(x_from, x_to, y_from, y_to, sends, receives):
        copies = []
        for side in range(2):
            copies.append((has_x[side], has_x[1 - side], pltpu.make_async_remote_copy(
                x_from.at[side], x_to.at[1 - side], sends.at[side], receives.at[side],
                device_id={"gx": to_x[side]}, device_id_type=MESH)))
            copies.append((has_y[side], has_y[1 - side], pltpu.make_async_remote_copy(
                y_from.at[side], y_to.at[1 - side], sends.at[2 + side], receives.at[2 + side],
                device_id={"gy": to_y[side]}, device_id_type=MESH)))
        return copies

    def factor_copies():
        return sided(factor_x_send, factor_x, factor_y_send, factor_y, factor_send, factor_recv)

    def own_copies(k):
        e = k // 2
        return sided(
            own_x_send.at[e], own_x.at[e], own_y_send.at[e], own_y.at[e], own_send.at[e], own_recv.at[e]
        )

    def start(copies):
        for sends, _, copy in copies:
            pl.when(sends)(copy.start)

    def arrive(copies):
        for _, receives, copy in copies:
            pl.when(receives)(copy.wait_recv)

    def put(k, f, x, value):
        field[k, f, x + 2] = value
        if k % 2 == 0:
            for side in range(2):
                at = edge_y[side]
                y_send[k // 2, side, f, x : x + 1, :] = value[at : at + 1]

    def send(k):
        for c in range(4):
            at = edge_x[c // 2]
            for f in range(2):
                corner_send[k // 2, c, f] = y_send[k // 2, c % 2, f, at : at + 1, :]
        start(halos(k))

    def fold(value):
        total = value[0:8]
        for at in range(8, by_rows, 8):
            total = total + value[at : at + 8]
        return total

    nought = jnp.zeros((8, nz), jnp.float32)

    sums = [nought, nought]
    for x in range(bx):
        here_x, back_x, here_y = cx[x + 1], cx[x], coef[2, x + 1]
        back_y = jnp.where(row == 0, conductance(rim_y[x], 1) * y_low, pltpu.roll(here_y, 1, 0))
        scale = 1.0 / (leak[x] + back_x + back_y)
        coef[0, x + 1] = here_x
        coef[1, x + 1] = back_x
        coef[3, x + 1] = back_y
        coef[6, x + 1] = scale
        for f in range(2):
            value = rhs[f, x] * scale
            put(0, f, x, value)
            sums[f] = sums[f] + fold(rhs[f, x] * value)
    moments = [tuple(sums)]

    def factors():
        for side in range(2):
            factor_x_send[side, by_rows:, :] = jnp.zeros((8, nz), jnp.float32)
            factor_y_send[side, bx:, :] = jnp.zeros((8, nz), jnp.float32)
        for x in range(bx):
            scale = coef[6, x + 1]
            for side in range(2):
                at = edge_y[side]
                factor_y_send[side, x : x + 1, :] = (coef[(3, 2)[side], x + 1] * scale)[at : at + 1]
        for side in range(2):
            at = edge_x[side] + 1
            factor_x_send[side, 0:by_rows, :] = coef[(1, 0)[side], at] * coef[6, at]
        for side in range(2):
            for end in range(2):
                at = edge_x[side]
                factor_x_send[side, by_rows + end : by_rows + end + 1, :] = factor_y_send[end, at : at + 1, :]
                at = edge_y[side]
                factor_y_send[side, bx + end : bx + end + 1, :] = factor_x_send[end, at : at + 1, :]

    def stencil(here, dn_x, up_x, dn_y, up_y, c):
        total = c[0] * up_x + c[1] * dn_x
        total = total + (c[2] * up_y + c[3] * dn_y)
        return total + (c[4] * pltpu.roll(here, nz - 1, 1) + c[5] * pltpu.roll(here, 1, 1))

    def beside(k, f, x, low, high):
        here = field[k, f, x + 2]
        up_y = jnp.where(row == by_rows - 1, high, pltpu.roll(here, by_rows - 1, 0))
        dn_y = jnp.where(row == 0, low, pltpu.roll(here, 1, 0))
        c = [coef[i, x + 1] for i in range(6)]
        return here, stencil(here, field[k, f, x + 1], field[k, f, x + 3], dn_y, up_y, c)

    def ghosts(k):
        e = k // 2
        for side in range(2):
            fx, fy = factor_x[side], factor_y[side]
            for f in range(2):
                total = own_x[e, side, f] + fx[0:by_rows] * field[k, f, edge_x[side] + 2]
                total = total + jnp.where(row == 0, fx[by_rows : by_rows + 1] * corner[e, 2 * side, f], 0.0)
                total = total + jnp.where(
                    row == by_rows - 1, fx[by_rows + 1 : by_rows + 2] * corner[e, 2 * side + 1, f], 0.0
                )
                field[k + 1, f, (1, bx + 2)[side]] = total
                total = own_y[e, side, f] + fy[0:bx] * y_send[e, side, f]
                total = total + jnp.where(row_x == 0, fy[bx : bx + 1] * corner[e, side, f], 0.0)
                total = total + jnp.where(row_x == bx - 1, fy[bx + 1 : bx + 2] * corner[e, 2 + side, f], 0.0)
                y_halo[k + 1, side, f] = total

    def within(k):
        for x in range(bx):
            c = [coef[i, x + 1] for i in range(6)]
            for f in range(2):
                here = field[k, f, x + 2]
                up_y = jnp.where(row == by_rows - 1, 0.0, pltpu.roll(here, by_rows - 1, 0))
                dn_y = jnp.where(row == 0, 0.0, pltpu.roll(here, 1, 0))
                total = c[2] * up_y + c[3] * dn_y
                total = total + (c[4] * pltpu.roll(here, nz - 1, 1) + c[5] * pltpu.roll(here, 1, 1))
                if x > 0:
                    total = total + c[1] * field[k, f, x + 1]
                if x < bx - 1:
                    total = total + c[0] * field[k, f, x + 3]
                inner[f, x] = total
                part_here = total * coef[6, x + 1]
                for side in range(2):
                    if x == edge_x[side]:
                        own_x_send[k // 2, side, f] = part_here
                    at = edge_y[side]
                    own_y_send[k // 2, side, f, x : x + 1, :] = part_here[at : at + 1]

    def completed(k, f, x):
        total = inner[f, x]
        if x == 0:
            total = total + coef[1, 1] * field[k, f, 1]
        if x == bx - 1:
            total = total + coef[0, bx] * field[k, f, bx + 2]
        low, high = [y_halo[k, side, f, x : x + 1, :] for side in range(2)]
        total = total + jnp.where(row == 0, coef[3, x + 1] * low, 0.0)
        total = total + jnp.where(row == by_rows - 1, coef[2, x + 1] * high, 0.0)
        return field[k, f, x + 2], total

    def picked(rows):
        return lax.broadcasted_iota(jnp.int32, (rows, nz), 0) == lax.broadcasted_iota(jnp.int32, (rows, nz), 1)

    def share(which, pairs):
        lines = [jnp.sum(value, axis=0, keepdims=True) for pair in pairs for value in pair]
        each = jnp.sum(jnp.concatenate(lines, axis=0), axis=1, keepdims=True)
        message = jnp.sum(jnp.where(picked(len(lines)), each, 0.0), axis=0, keepdims=True)
        part[which] = message
        gathered[which, rank] = message
        each_other(lambda to: pltpu.make_async_remote_copy(
            part.at[which], gathered.at[which, rank], part_send.at[which], part_recv.at[which],
            device_id=to, device_id_type=MESH,
        ).start())

    def bytes_of_others(which, sem):
        others = gathered.at[which, pl.ds(0, devices - 1)]
        return pltpu.make_async_copy(others, others, sem.at[which])

    def collect(which, count):
        bytes_of_others(which, part_recv).wait()
        message = jnp.sum(gathered[which], axis=0)
        square = jnp.sum(jnp.where(picked(2 * count), message, 0.0), axis=1, keepdims=True)
        square = jnp.broadcast_to(square, (2 * count, nz))
        return [square[2 * k : 2 * k + 2] for k in range(count)]

    for k in range(ITERS):
        if k % 2 == 0:
            send(k)
            if k == 0:
                factors()
                start(factor_copies())
            within(k)
            start(own_copies(k))
            if len(moments) == EARLY:
                share(0, moments)
            arrive(halos(k))
        sums = [nought] * (4 if k + 1 < ITERS else 2)
        for x in range(bx):
            at = 0
            for f in range(2):
                if k % 2 == 0:
                    here, total = completed(k, f, x)
                else:
                    low, high = [y_halo[k, side, f, x : x + 1, :] for side in range(2)]
                    here, total = beside(k, f, x, low, high)
                sums[at] = sums[at] + fold(here * total)
                at += 1
                if k + 1 < ITERS:
                    value = total * coef[6, x + 1]
                    put(k + 1, f, x, value)
                    sums[at] = sums[at] + fold(value * total)
                    at += 1
        if k + 1 < ITERS:
            moments += [(sums[0], sums[2]), (sums[1], sums[3])]
        else:
            moments += [(sums[0], sums[1])]
        if k % 2 == 0:
            if k == 0:
                arrive(factor_copies())
            arrive(own_copies(k))
            ghosts(k)

    share(1, moments[EARLY:])
    known = list(collect(0, EARLY))

    def moment(k):
        if k >= len(known):
            known.extend(collect(1, MOMENTS - EARLY))
        return known[k]

    weights = coefficients(moment)
    weights = [[jnp.broadcast_to(w[f : f + 1], (by_rows, nz)) for w in weights] for f in range(2)]

    def combine(x, carry):
        for f in range(2):
            total = weights[f][0] * field[0, f, x + 2]
            for k in range(1, ITERS):
                total = total + weights[f][k] * field[k, f, x + 2]
            answer[f, x] = total
        return carry

    lax.fori_loop(0, bx + 1, combine, 0, unroll=bx + 1)
    for f in range(2):
        rim = weights[f][0] * y_halo[0, 1, f]
        for k in range(1, ITERS):
            rim = rim + weights[f][k] * y_halo[k, 1, f]
        rims[f] = rim
    stores = [
        pltpu.make_async_copy(answer, answer_out, out_sem.at[0]),
        pltpu.make_async_copy(rims, rims_out, out_sem.at[1]),
    ]
    for store in stores:
        store.start()
    pl.when(has_x[1])(rim_copy_x.wait_send)
    pl.when(has_y[1])(rim_copy_y.wait_send)
    for sends, _, copy in factor_copies() + own_copies(0) + own_copies(2) + halos(0) + halos(2):
        pl.when(sends)(copy.wait_send)
    for which in range(2):
        bytes_of_others(which, part_send).wait()
    for store in stores:
        store.wait()


def finish(nx, ny, answer_in, rims_in, pot_out, adj_out, sens_out, answer, rims, sens, in_sem, out_sem):
    bx, by_rows, nz = pot_out.shape
    loads = [
        pltpu.make_async_copy(answer_in, answer, in_sem.at[0]),
        pltpu.make_async_copy(rims_in, rims, in_sem.at[1]),
    ]
    for load in loads:
        load.start()
    stores = [
        pltpu.make_async_copy(answer.at[0, pl.ds(0, bx)], pot_out, out_sem.at[0]),
        pltpu.make_async_copy(answer.at[1, pl.ds(0, bx)], adj_out, out_sem.at[1]),
        pltpu.make_async_copy(sens, sens_out, out_sem.at[2]),
    ]
    loads[0].wait()
    stores[0].start()
    stores[1].start()
    loads[1].wait()
    row = lax.broadcasted_iota(jnp.int32, (by_rows, nz), 0)
    lane = lax.broadcasted_iota(jnp.int32, (by_rows, nz), 1)
    x_high = (lax.axis_index("gx") < nx - 1).astype(jnp.float32)
    y_high = (lax.axis_index("gy") < ny - 1).astype(jnp.float32)
    not_last_row = jnp.where(row < by_rows - 1, 1.0, y_high)

    def differences(x, carry):
        gaps = []
        for f in range(2):
            here = answer[f, x]
            up_y = jnp.where(row == by_rows - 1, rims[f, pl.ds(x, 1), :], pltpu.roll(here, by_rows - 1, 0))
            gaps.append((here - answer[f, x + 1], here - up_y, here - pltpu.roll(here, nz - 1, 1)))
        sens[0, x] = -gaps[1][0] * gaps[0][0] * jnp.where(x < bx - 1, 1.0, x_high)
        sens[1, x] = -gaps[1][1] * gaps[0][1] * not_last_row
        sens[2, x] = jnp.where(lane < nz - 1, -gaps[1][2] * gaps[0][2], 0.0)
        return carry

    lax.fori_loop(0, bx, differences, 0, unroll=bx)
    stores[2].start()
    for store in stores:
        store.wait()


def body(nx, ny, bond_mask, levels, electrode, leakage, source, weight):
    bx, by, nz = leakage.shape
    f32, i32 = jnp.float32, jnp.int32
    vmem, dma = pltpu.VMEM, pltpu.SemaphoreType.DMA
    block = (bx, by, nz)
    hbm = pl.BlockSpec(memory_space=pltpu.HBM)
    answer, rims = pl.pallas_call(
        functools.partial(kernel, nx, ny),
        out_shape=(
            jax.ShapeDtypeStruct((2, bx + 1, by, nz), f32),
            jax.ShapeDtypeStruct((2, bx, nz), f32),
        ),
        in_specs=[pl.BlockSpec(memory_space=pltpu.SMEM)] + [hbm] * 5,
        out_specs=[hbm] * 2,
        scratch_shapes=[
            vmem((3,) + block, i32), vmem((2, bx, by), i32), vmem(block, f32), vmem((2,) + block, f32), dma((5,)),
            vmem((bx + 1, by, nz), f32), vmem((7, bx + 2, by, nz), f32),
            vmem((2, by + 8, nz), f32), vmem((2, by + 8, nz), f32),
            vmem((2, bx + 8, nz), f32), vmem((2, bx + 8, nz), f32), dma((4,)), dma((4,)),
            vmem((ITERS // 2, 2, 2, by, nz), f32), vmem((ITERS // 2, 2, 2, by, nz), f32),
            vmem((ITERS // 2, 2, 2, bx, nz), f32), vmem((ITERS // 2, 2, 2, bx, nz), f32),
            dma((ITERS // 2, 4)), dma((ITERS // 2, 4)),
            vmem((by, nz), i32), vmem((bx, 1, nz), i32), vmem((bx, 1, nz), i32), dma((2,)), dma((2,)),
            vmem((ITERS, 2, bx + 4, by, nz), f32),
            vmem((ITERS // 2, 2, 2, bx, nz), f32), vmem((ITERS, 2, 2, bx, nz), f32),
            vmem((ITERS // 2, 4, 2, 1, nz), f32), vmem((ITERS // 2, 4, 2, 1, nz), f32),
            dma((ITERS // 2, 8)), dma((ITERS // 2, 8)),
            vmem((2,) + block, f32), vmem((2, 1, nz), f32), vmem((2, nx * ny, 1, nz), f32), dma((2,)), dma((2,)),
            vmem((2, bx + 1, by, nz), f32), vmem((2, bx, nz), f32), dma((2,)),
        ],
        compiler_params=pltpu.CompilerParams(
            collective_id=0, has_side_effects=True, vmem_limit_bytes=VMEM_LIMIT
        ),
    )(levels, bond_mask, electrode, leakage, source, weight)
    return pl.pallas_call(
        functools.partial(finish, nx, ny),
        out_shape=(
            jax.ShapeDtypeStruct(block, f32),
            jax.ShapeDtypeStruct(block, f32),
            jax.ShapeDtypeStruct((3,) + block, f32),
        ),
        in_specs=[hbm] * 2,
        out_specs=[hbm] * 3,
        scratch_shapes=[
            vmem((2, bx + 1, by, nz), f32), vmem((2, bx, nz), f32), vmem((3,) + block, f32), dma((2,)), dma((3,)),
        ],
        compiler_params=pltpu.CompilerParams(vmem_limit_bytes=VMEM_LIMIT),
    )(answer, rims)


def solution(mesh):
    return jax.shard_map(
        functools.partial(body, mesh.shape["gx"], mesh.shape["gy"]),
        mesh=mesh,
        in_specs=(
            P(None, "gx", "gy", None),
            P(),
            P(None, "gx", "gy"),
            P("gx", "gy", None),
            P("gx", "gy", None),
            P("gx", "gy", None),
        ),
        out_specs=(P("gx", "gy", None), P("gx", "gy", None), P(None, "gx", "gy", None)),
        check_vma=False,
    )
```

```python
import functools

import jax
import jax.numpy as jnp
from jax import lax
from jax.experimental import pallas as pl
from jax.experimental.pallas import tpu as pltpu
from jax.sharding import PartitionSpec as P

ITERS = 4
MOMENTS = 2 * ITERS
EARLY = 5
MESH = pl.DeviceIdType.MESH
UNROLL = 4
VMEM_LIMIT = 62 * 1024 * 1024


def coefficients(mu):
    def tree(terms):
        while len(terms) > 1:
            terms = [sum(terms[i : i + 2][1:], terms[i]) for i in range(0, len(terms), 2)]
        return terms[0]

    def quadratic(c, m):
        return tree([
            tree([c[i] * c[k - i] for i in range(max(0, k - len(c) + 1), min(k + 1, len(c)))]) * m(k)
            for k in range(2 * len(c) - 1)
        ])

    def slope(k):
        return mu(k) - mu(k + 1)

    one = jnp.ones_like(mu(0))
    scaled, direction, answer = [one], [one], []
    norm_now = mu(0)
    for step in range(ITERS):
        alpha = norm_now / quadratic(direction, slope)
        answer = [a + alpha * d for a, d in zip(answer, direction)] + [alpha * direction[-1]]
        if step + 1 < ITERS:
            image = [direction[0]]
            image += [b - a for a, b in zip(direction[:-1], direction[1:])]
            image += [-direction[-1]]
            scaled = [s - alpha * q for s, q in zip(scaled, image)] + [-alpha * image[-1]]
            fresh = quadratic(scaled, mu)
            beta = fresh / norm_now
            direction = [s + beta * d for s, d in zip(scaled, direction)] + [scaled[-1]]
            norm_now = fresh
    return answer


def kernel(
    nx, ny,
    levels, mask_in, elec_in, leak_in, src_in, wgt_in,
    answer_out, rims_out,
    mask, elec, leak, rhs, in_sem,
    cx, coef, factor_x_send, factor_x, factor_y_send, factor_y, factor_send, factor_recv,
    own_x_send, own_x, own_y_send, own_y, own_send, own_recv,
    rim_x, rim_y, rim_y_send, rim_send, rim_recv,
    field, y_send, y_halo, corner_send, corner, halo_send, halo_recv,
    inner, part, gathered, part_send, part_recv,
    answer, rims, out_sem,
):
    bx, by_rows, nz = leak.shape
    ix, iy = lax.axis_index("gx"), lax.axis_index("gy")
    devices = nx * ny
    rank = ix * ny + iy
    has_x = (ix > 0, ix < nx - 1)
    has_y = (iy > 0, iy < ny - 1)
    to_x = (jnp.maximum(ix - 1, 0), jnp.minimum(ix + 1, nx - 1))
    to_y = (jnp.maximum(iy - 1, 0), jnp.minimum(iy + 1, ny - 1))
    edge_x, edge_y = (0, bx - 1), (0, by_rows - 1)

    loads = [
        pltpu.make_async_copy(mask_in, mask, in_sem.at[0]),
        pltpu.make_async_copy(elec_in, elec, in_sem.at[1]),
        pltpu.make_async_copy(leak_in, leak, in_sem.at[2]),
        pltpu.make_async_copy(src_in, rhs.at[0], in_sem.at[3]),
        pltpu.make_async_copy(wgt_in, rhs.at[1], in_sem.at[4]),
    ]
    for load in loads:
        load.start()

    def ahead(at, count, size):
        places = [at]
        for _ in range(1, count):
            later = places[-1] + 1
            places.append(jnp.where(later == size, 0, later))
        return places

    all_x, all_y = ahead(ix, nx, nx), ahead(iy, ny, ny)

    def each_other(act):
        for dx in range(nx):
            for dy in range(ny):
                if dx or dy:
                    act({"gx": all_x[dx], "gy": all_y[dy]})

    barrier = pltpu.get_barrier_semaphore()
    each_other(lambda to: pl.semaphore_signal(barrier, inc=1, device_id=to, device_id_type=MESH))
    pl.semaphore_wait(barrier, devices - 1)

    loads[0].wait()
    row = lax.broadcasted_iota(jnp.int32, (by_rows, nz), 0)
    lane = lax.broadcasted_iota(jnp.int32, (by_rows, nz), 1)
    row_x = lax.broadcasted_iota(jnp.int32, (bx, nz), 0)
    rim_y_send[...] = mask[1, :, by_rows - 1 : by_rows, :]
    rim_copy_x = pltpu.make_async_remote_copy(
        mask.at[0, bx - 1], rim_x, rim_send.at[0], rim_recv.at[0],
        device_id={"gx": to_x[1]}, device_id_type=MESH,
    )
    rim_copy_y = pltpu.make_async_remote_copy(
        rim_y_send, rim_y, rim_send.at[1], rim_recv.at[1],
        device_id={"gy": to_y[1]}, device_id_type=MESH,
    )
    pl.when(has_x[1])(rim_copy_x.start)
    pl.when(has_y[1])(rim_copy_y.start)

    @pl.when(jnp.logical_not(has_x[0]))
    def _():
        rim_x[...] = jnp.zeros_like(rim_x)

    @pl.when(jnp.logical_not(has_y[0]))
    def _():
        rim_y[...] = jnp.zeros_like(rim_y)

    for side in range(2):

        @pl.when(jnp.logical_not(has_x[side]))
        def _(side=side):
            for k in range(ITERS):
                for f in range(2):
                    field[k, f, 1 if side == 0 else bx + 2] = jnp.zeros((by_rows, nz), jnp.float32)
            factor_x[side] = jnp.zeros_like(factor_x[side])
            for e in range(ITERS // 2):
                own_x[e, side] = jnp.zeros_like(own_x[e, side])

        @pl.when(jnp.logical_not(has_y[side]))
        def _(side=side):
            factor_y[side] = jnp.zeros_like(factor_y[side])
            for e in range(ITERS // 2):
                own_y[e, side] = jnp.zeros_like(own_y[e, side])
            for k in range(ITERS):
                y_halo[k, side] = jnp.zeros_like(y_halo[k, side])

    for c in range(4):

        @pl.when(jnp.logical_not(jnp.logical_and(has_x[c // 2], has_y[c % 2])))
        def _(c=c):
            for e in range(ITERS // 2):
                corner[e, c] = jnp.zeros_like(corner[e, c])

    def conductance(bits, d):
        return jnp.where(bits == 1, levels[1, d], levels[0, d])

    x_low = has_x[0].astype(jnp.float32)
    x_high = has_x[1].astype(jnp.float32)
    y_low = has_y[0].astype(jnp.float32)
    y_high = has_y[1].astype(jnp.float32)
    not_last_row = jnp.where(row < by_rows - 1, 1.0, y_high)
    for load in loads[1:]:
        load.wait()
    square = (by_rows, by_rows)
    eye = lax.broadcasted_iota(jnp.int32, square, 0) == lax.broadcasted_iota(jnp.int32, square, 1)

    def column(which, x):
        line = elec[which, pl.ds(x, 1), :].astype(jnp.float32)
        return jnp.sum(jnp.where(eye, line, 0.0), axis=1, keepdims=True)

    def set_up(x, carry):
        here = conductance(mask[0, x], 0) * jnp.where(x < bx - 1, 1.0, x_high)
        cx[x + 1] = here
        here_y = conductance(mask[1, x], 1) * not_last_row
        coef[2, x + 1] = here_y
        here_z = jnp.where(lane < nz - 1, conductance(mask[2, x], 2), 0.0)
        coef[4, x + 1] = here_z
        back_z = pltpu.roll(here_z, 1, 1)
        coef[5, x + 1] = back_z
        first = jnp.where(lane == 0, column(0, x), 0.0)
        last = jnp.where(lane == nz - 1, column(1, x), 0.0)
        rhs[0, x] = rhs[0, x] + first
        rhs[1, x] = rhs[1, x] + last
        leak[x] = leak[x] + first + last + here + here_y + here_z + back_z
        return carry

    lax.fori_loop(0, bx, set_up, 0, unroll=bx)
    pl.when(has_x[0])(rim_copy_x.wait_recv)
    pl.when(has_y[0])(rim_copy_y.wait_recv)
    cx[0] = conductance(rim_x[...], 0) * x_low

    def halos(k):
        e = k // 2
        copies = []
        for side in range(2):
            mine, theirs = ((2, bx + 2), (bx + 1, 1))[side]
            copies.append((has_x[side], has_x[1 - side], pltpu.make_async_remote_copy(
                field.at[k, :, mine], field.at[k, :, theirs],
                halo_send.at[e, side], halo_recv.at[e, side],
                device_id={"gx": to_x[side]}, device_id_type=MESH)))
            copies.append((has_y[side], has_y[1 - side], pltpu.make_async_remote_copy(
                y_send.at[e, side], y_halo.at[k, 1 - side],
                halo_send.at[e, 2 + side], halo_recv.at[e, 2 + side],
                device_id={"gy": to_y[side]}, device_id_type=MESH)))
        for c in range(4):
            a, b = c // 2, c % 2
            copies.append((
                jnp.logical_and(has_x[a], has_y[b]), jnp.logical_and(has_x[1 - a], has_y[1 - b]),
                pltpu.make_async_remote_copy(
                    corner_send.at[e, c], corner.at[e, 3 - c], halo_send.at[e, 4 + c], halo_recv.at[e, 4 + c],
                    device_id={"gx": to_x[a], "gy": to_y[b]}, device_id_type=MESH)))
        return copies

    def sided(x_from, x_to, y_from, y_to, sends, receives):
        copies = []
        for side in range(2):
            copies.append((has_x[side], has_x[1 - side], pltpu.make_async_remote_copy(
                x_from.at[side], x_to.at[1 - side], sends.at[side], receives.at[side],
                device_id={"gx": to_x[side]}, device_id_type=MESH)))
            copies.append((has_y[side], has_y[1 - side], pltpu.make_async_remote_copy(
                y_from.at[side], y_to.at[1 - side], sends.at[2 + side], receives.at[2 + side],
                device_id={"gy": to_y[side]}, device_id_type=MESH)))
        return copies

    def factor_copies():
        return sided(factor_x_send, factor_x, factor_y_send, factor_y, factor_send, factor_recv)

    def own_copies(k):
        e = k // 2
        return sided(
            own_x_send.at[e], own_x.at[e], own_y_send.at[e], own_y.at[e], own_send.at[e], own_recv.at[e]
        )

    def start(copies):
        for sends, _, copy in copies:
            pl.when(sends)(copy.start)

    def arrive(copies):
        for _, receives, copy in copies:
            pl.when(receives)(copy.wait_recv)

    def put(k, f, x, value):
        field[k, f, x + 2] = value
        if k % 2 == 0:
            for side in range(2):
                at = edge_y[side]
                y_send[k // 2, side, f, x : x + 1, :] = value[at : at + 1]

    def send(k):
        for c in range(4):
            at = edge_x[c // 2]
            for f in range(2):
                corner_send[k // 2, c, f] = y_send[k // 2, c % 2, f, at : at + 1, :]
        start(halos(k))

    def fold(value):
        total = value[0:8]
        for at in range(8, by_rows, 8):
            total = total + value[at : at + 8]
        return total

    nought = jnp.zeros((8, nz), jnp.float32)

    sums = [nought, nought]
    for x in range(bx):
        here_x, back_x, here_y = cx[x + 1], cx[x], coef[2, x + 1]
        back_y = jnp.where(row == 0, conductance(rim_y[x], 1) * y_low, pltpu.roll(here_y, 1, 0))
        scale = 1.0 / (leak[x] + back_x + back_y)
        coef[0, x + 1] = here_x
        coef[1, x + 1] = back_x
        coef[3, x + 1] = back_y
        coef[6, x + 1] = scale
        for f in range(2):
            value = rhs[f, x] * scale
            put(0, f, x, value)
            sums[f] = sums[f] + fold(rhs[f, x] * value)
    moments = [tuple(sums)]

    def factors():
        for side in range(2):
            factor_x_send[side, by_rows:, :] = jnp.zeros((8, nz), jnp.float32)
            factor_y_send[side, bx:, :] = jnp.zeros((8, nz), jnp.float32)
        for x in range(bx):
            scale = coef[6, x + 1]
            for side in range(2):
                at = edge_y[side]
                factor_y_send[side, x : x + 1, :] = (coef[(3, 2)[side], x + 1] * scale)[at : at + 1]
        for side in range(2):
            at = edge_x[side] + 1
            factor_x_send[side, 0:by_rows, :] = coef[(1, 0)[side], at] * coef[6, at]
        for side in range(2):
            for end in range(2):
                at = edge_x[side]
                factor_x_send[side, by_rows + end : by_rows + end + 1, :] = factor_y_send[end, at : at + 1, :]
                at = edge_y[side]
                factor_y_send[side, bx + end : bx + end + 1, :] = factor_x_send[end, at : at + 1, :]

    def stencil(here, dn_x, up_x, dn_y, up_y, c):
        total = c[0] * up_x + c[1] * dn_x
        total = total + (c[2] * up_y + c[3] * dn_y)
        return total + (c[4] * pltpu.roll(here, nz - 1, 1) + c[5] * pltpu.roll(here, 1, 1))

    def beside(k, f, x, low, high):
        here = field[k, f, x + 2]
        up_y = jnp.where(row == by_rows - 1, high, pltpu.roll(here, by_rows - 1, 0))
        dn_y = jnp.where(row == 0, low, pltpu.roll(here, 1, 0))
        c = [coef[i, x + 1] for i in range(6)]
        return here, stencil(here, field[k, f, x + 1], field[k, f, x + 3], dn_y, up_y, c)

    def ghosts(k):
        e = k // 2
        for side in range(2):
            fx, fy = factor_x[side], factor_y[side]
            for f in range(2):
                total = own_x[e, side, f] + fx[0:by_rows] * field[k, f, edge_x[side] + 2]
                total = total + jnp.where(row == 0, fx[by_rows : by_rows + 1] * corner[e, 2 * side, f], 0.0)
                total = total + jnp.where(
                    row == by_rows - 1, fx[by_rows + 1 : by_rows + 2] * corner[e, 2 * side + 1, f], 0.0
                )
                field[k + 1, f, (1, bx + 2)[side]] = total
                total = own_y[e, side, f] + fy[0:bx] * y_send[e, side, f]
                total = total + jnp.where(row_x == 0, fy[bx : bx + 1] * corner[e, side, f], 0.0)
                total = total + jnp.where(row_x == bx - 1, fy[bx + 1 : bx + 2] * corner[e, 2 + side, f], 0.0)
                y_halo[k + 1, side, f] = total

    def within(k):
        for x in range(bx):
            c = [coef[i, x + 1] for i in range(6)]
            for f in range(2):
                here = field[k, f, x + 2]
                up_y = jnp.where(row == by_rows - 1, 0.0, pltpu.roll(here, by_rows - 1, 0))
                dn_y = jnp.where(row == 0, 0.0, pltpu.roll(here, 1, 0))
                total = c[2] * up_y + c[3] * dn_y
                total = total + (c[4] * pltpu.roll(here, nz - 1, 1) + c[5] * pltpu.roll(here, 1, 1))
                if x > 0:
                    total = total + c[1] * field[k, f, x + 1]
                if x < bx - 1:
                    total = total + c[0] * field[k, f, x + 3]
                inner[f, x] = total
                part_here = total * coef[6, x + 1]
                for side in range(2):
                    if x == edge_x[side]:
                        own_x_send[k // 2, side, f] = part_here
                    at = edge_y[side]
                    own_y_send[k // 2, side, f, x : x + 1, :] = part_here[at : at + 1]

    def completed(k, f, x):
        total = inner[f, x]
        if x == 0:
            total = total + coef[1, 1] * field[k, f, 1]
        if x == bx - 1:
            total = total + coef[0, bx] * field[k, f, bx + 2]
        low, high = [y_halo[k, side, f, x : x + 1, :] for side in range(2)]
        total = total + jnp.where(row == 0, coef[3, x + 1] * low, 0.0)
        total = total + jnp.where(row == by_rows - 1, coef[2, x + 1] * high, 0.0)
        return field[k, f, x + 2], total

    def picked(rows):
        return lax.broadcasted_iota(jnp.int32, (rows, nz), 0) == lax.broadcasted_iota(jnp.int32, (rows, nz), 1)

    def share(which, pairs):
        lines = [jnp.sum(value, axis=0, keepdims=True) for pair in pairs for value in pair]
        each = jnp.sum(jnp.concatenate(lines, axis=0), axis=1, keepdims=True)
        message = jnp.sum(jnp.where(picked(len(lines)), each, 0.0), axis=0, keepdims=True)
        part[which] = message
        gathered[which, rank] = message
        each_other(lambda to: pltpu.make_async_remote_copy(
            part.at[which], gathered.at[which, rank], part_send.at[which], part_recv.at[which],
            device_id=to, device_id_type=MESH,
        ).start())

    def bytes_of_others(which, sem):
        others = gathered.at[which, pl.ds(0, devices - 1)]
        return pltpu.make_async_copy(others, others, sem.at[which])

    def collect(which, count):
        bytes_of_others(which, part_recv).wait()
        message = jnp.sum(gathered[which], axis=0)
        square = jnp.sum(jnp.where(picked(2 * count), message, 0.0), axis=1, keepdims=True)
        square = jnp.broadcast_to(square, (2 * count, nz))
        return [square[2 * k : 2 * k + 2] for k in range(count)]

    for k in range(ITERS):
        if k % 2 == 0:
            send(k)
            if k == 0:
                factors()
                start(factor_copies())
            within(k)
            start(own_copies(k))
            if len(moments) == EARLY:
                share(0, moments)
            arrive(halos(k))
        sums = [nought] * (4 if k + 1 < ITERS else 2)
        for x in range(bx):
            at = 0
            for f in range(2):
                if k % 2 == 0:
                    here, total = completed(k, f, x)
                else:
                    low, high = [y_halo[k, side, f, x : x + 1, :] for side in range(2)]
                    here, total = beside(k, f, x, low, high)
                sums[at] = sums[at] + fold(here * total)
                at += 1
                if k + 1 < ITERS:
                    value = total * coef[6, x + 1]
                    put(k + 1, f, x, value)
                    sums[at] = sums[at] + fold(value * total)
                    at += 1
        if k + 1 < ITERS:
            moments += [(sums[0], sums[2]), (sums[1], sums[3])]
        else:
            moments += [(sums[0], sums[1])]
        if k % 2 == 0:
            if k == 0:
                arrive(factor_copies())
            arrive(own_copies(k))
            ghosts(k)

    share(1, moments[EARLY:])
    known = list(collect(0, EARLY))

    def moment(k):
        if k >= len(known):
            known.extend(collect(1, MOMENTS - EARLY))
        return known[k]

    weights = coefficients(moment)
    weights = [[jnp.broadcast_to(w[f : f + 1], (by_rows, nz)) for w in weights] for f in range(2)]

    stores = [pltpu.make_async_copy(answer.at[f], answer_out.at[f], out_sem.at[f]) for f in range(2)]
    stores.append(pltpu.make_async_copy(rims, rims_out, out_sem.at[2]))
    for f in range(2):
        rim = weights[f][0] * y_halo[0, 1, f]
        for k in range(1, ITERS):
            rim = rim + weights[f][k] * y_halo[k, 1, f]
        rims[f] = rim
    stores[2].start()
    for f in range(2):
        for x in range(bx + 1):
            total = weights[f][0] * field[0, f, x + 2]
            for k in range(1, ITERS):
                total = total + weights[f][k] * field[k, f, x + 2]
            answer[f, x] = total
        stores[f].start()
    pl.when(has_x[1])(rim_copy_x.wait_send)
    pl.when(has_y[1])(rim_copy_y.wait_send)
    for sends, _, copy in factor_copies() + own_copies(0) + own_copies(2) + halos(0) + halos(2):
        pl.when(sends)(copy.wait_send)
    for which in range(2):
        bytes_of_others(which, part_send).wait()
    for store in stores:
        store.wait()


def finish(nx, ny, answer_in, rims_in, pot_out, adj_out, sens_out, answer, rims, sens, in_sem, out_sem):
    bx, by_rows, nz = pot_out.shape
    loads = [
        pltpu.make_async_copy(answer_in.at[0], answer.at[0], in_sem.at[0]),
        pltpu.make_async_copy(answer_in.at[1], answer.at[1], in_sem.at[1]),
        pltpu.make_async_copy(rims_in, rims, in_sem.at[2]),
    ]
    for load in loads:
        load.start()
    stores = [
        pltpu.make_async_copy(answer.at[0, pl.ds(0, bx)], pot_out, out_sem.at[0]),
        pltpu.make_async_copy(answer.at[1, pl.ds(0, bx)], adj_out, out_sem.at[1]),
    ]
    half = bx // 2
    for at in range(2):
        planes = pl.ds(at * half, half if at == 0 else bx - half)
        stores.append(pltpu.make_async_copy(sens.at[:, planes], sens_out.at[:, planes], out_sem.at[2 + at]))
    for f in range(2):
        loads[f].wait()
        stores[f].start()
    loads[2].wait()
    row = lax.broadcasted_iota(jnp.int32, (by_rows, nz), 0)
    lane = lax.broadcasted_iota(jnp.int32, (by_rows, nz), 1)
    x_high = (lax.axis_index("gx") < nx - 1).astype(jnp.float32)
    y_high = (lax.axis_index("gy") < ny - 1).astype(jnp.float32)
    not_last_row = jnp.where(row < by_rows - 1, 1.0, y_high)

    def differences(x, carry):
        gaps = []
        for f in range(2):
            here = answer[f, x]
            up_y = jnp.where(row == by_rows - 1, rims[f, pl.ds(x, 1), :], pltpu.roll(here, by_rows - 1, 0))
            gaps.append((here - answer[f, x + 1], here - up_y, here - pltpu.roll(here, nz - 1, 1)))
        sens[0, x] = -gaps[1][0] * gaps[0][0] * jnp.where(x < bx - 1, 1.0, x_high)
        sens[1, x] = -gaps[1][1] * gaps[0][1] * not_last_row
        sens[2, x] = jnp.where(lane < nz - 1, -gaps[1][2] * gaps[0][2], 0.0)
        return carry

    for x in range(bx):
        differences(x, 0)
        if x == half - 1:
            stores[2].start()
    stores[3].start()
    for store in stores:
        store.wait()


def body(nx, ny, bond_mask, levels, electrode, leakage, source, weight):
    bx, by, nz = leakage.shape
    f32, i32 = jnp.float32, jnp.int32
    vmem, dma = pltpu.VMEM, pltpu.SemaphoreType.DMA
    block = (bx, by, nz)
    hbm = pl.BlockSpec(memory_space=pltpu.HBM)
    answer, rims = pl.pallas_call(
        functools.partial(kernel, nx, ny),
        out_shape=(
            jax.ShapeDtypeStruct((2, bx + 1, by, nz), f32),
            jax.ShapeDtypeStruct((2, bx, nz), f32),
        ),
        in_specs=[pl.BlockSpec(memory_space=pltpu.SMEM)] + [hbm] * 5,
        out_specs=[hbm] * 2,
        scratch_shapes=[
            vmem((3,) + block, i32), vmem((2, bx, by), i32), vmem(block, f32), vmem((2,) + block, f32), dma((5,)),
            vmem((bx + 1, by, nz), f32), vmem((7, bx + 2, by, nz), f32),
            vmem((2, by + 8, nz), f32), vmem((2, by + 8, nz), f32),
            vmem((2, bx + 8, nz), f32), vmem((2, bx + 8, nz), f32), dma((4,)), dma((4,)),
            vmem((ITERS // 2, 2, 2, by, nz), f32), vmem((ITERS // 2, 2, 2, by, nz), f32),
            vmem((ITERS // 2, 2, 2, bx, nz), f32), vmem((ITERS // 2, 2, 2, bx, nz), f32),
            dma((ITERS // 2, 4)), dma((ITERS // 2, 4)),
            vmem((by, nz), i32), vmem((bx, 1, nz), i32), vmem((bx, 1, nz), i32), dma((2,)), dma((2,)),
            vmem((ITERS, 2, bx + 4, by, nz), f32),
            vmem((ITERS // 2, 2, 2, bx, nz), f32), vmem((ITERS, 2, 2, bx, nz), f32),
            vmem((ITERS // 2, 4, 2, 1, nz), f32), vmem((ITERS // 2, 4, 2, 1, nz), f32),
            dma((ITERS // 2, 8)), dma((ITERS // 2, 8)),
            vmem((2,) + block, f32), vmem((2, 1, nz), f32), vmem((2, nx * ny, 1, nz), f32), dma((2,)), dma((2,)),
            vmem((2, bx + 1, by, nz), f32), vmem((2, bx, nz), f32), dma((3,)),
        ],
        compiler_params=pltpu.CompilerParams(
            collective_id=0, has_side_effects=True, vmem_limit_bytes=VMEM_LIMIT
        ),
    )(levels, bond_mask, electrode, leakage, source, weight)
    return pl.pallas_call(
        functools.partial(finish, nx, ny),
        out_shape=(
            jax.ShapeDtypeStruct(block, f32),
            jax.ShapeDtypeStruct(block, f32),
            jax.ShapeDtypeStruct((3,) + block, f32),
        ),
        in_specs=[hbm] * 2,
        out_specs=[hbm] * 3,
        scratch_shapes=[
            vmem((2, bx + 1, by, nz), f32), vmem((2, bx, nz), f32), vmem((3,) + block, f32), dma((3,)), dma((4,)),
        ],
        compiler_params=pltpu.CompilerParams(vmem_limit_bytes=VMEM_LIMIT),
    )(answer, rims)


def solution(mesh):
    return jax.shard_map(
        functools.partial(body, mesh.shape["gx"], mesh.shape["gy"]),
        mesh=mesh,
        in_specs=(
            P(None, "gx", "gy", None),
            P(),
            P(None, "gx", "gy"),
            P("gx", "gy", None),
            P("gx", "gy", None),
            P("gx", "gy", None),
        ),
        out_specs=(P("gx", "gy", None), P("gx", "gy", None), P(None, "gx", "gy", None)),
        check_vma=False,
    )
```
